32 devices in a mesh: dp: 8 (over z, y), mp: 4 (over x, core).
Axes of the slice: x: 2, y: 2, z: 4, core: 2. Of those that a mesh axis runs over, the one named last changes fastest.
Arguments:
- block_input: bfloat16 [8, 2048, 768], P('dp', 'mp'), may hold values from -6 to 6
- out_cotangent: bfloat16 [8, 2048, 768], P('dp', 'mp'), may hold values from -6 to 6
- lengths: int32 [8], P('dp'), may hold values from 1024 to 2048, as said below
- w_qkv: float32 [768, 3, 768], P('dp', None, 'mp'), may hold values from -0.21875 to 0.21875
- w_out: float32 [768, 768], P('mp', 'dp'), may hold values from -1.75 to 1.75
- w_up: float32 [768, 3072], P('dp', 'mp'), may hold values from -0.21875 to 0.21875
- w_down: float32 [3072, 768], P('mp', 'dp'), may hold values from -0.109375 to 0.109375
- pair_bias: float32 [2048, 256], P(('dp', 'mp')), may hold values from -1.5 to 1.5
- norm_gains: float32 [2, 768], replicated, may hold values from 0.5 to 1.5
- first_qkv: float32 [768, 3, 768], P('dp', None, 'mp'), may hold values from -0.625 to 0.625
- first_out: float32 [768, 768], P('mp', 'dp'), may hold values from -0.125 to 0.125
- first_up: float32 [768, 3072], P('dp', 'mp'), may hold values from -0.625 to 0.625
- first_down: float32 [3072, 768], P('mp', 'dp'), may hold values from -0.625 to 0.625
- first_bias: float32 [2048, 256], P(('dp', 'mp')), may hold values from -0.03125 to 0.03125
- first_gains: float32 [2, 768], replicated, may hold values from -0.625 to 0.625
- second_qkv: float32 [768, 3, 768], P('dp', None, 'mp'), may hold values from 0.002 to 0.03
- second_out: float32 [768, 768], P('mp', 'dp'), may hold values from 0.0001 to 0.0015
- second_up: float32 [768, 3072], P('dp', 'mp'), may hold values from 0.002 to 0.03
- second_down: float32 [3072, 768], P('mp', 'dp'), may hold values from 0.002 to 0.03
- second_bias: float32 [2048, 256], P(('dp', 'mp')), may hold values from 5e-05 to 0.00075
- second_gains: float32 [2, 768], replicated, may hold values from 0.002 to 0.03
Outputs:
- block_output: bfloat16 [8, 2048, 768], P('dp', 'mp')
- grad_input: float32 [8, 2048, 768], P('dp', 'mp')
- grad_qkv: float32 [768, 3, 768], P('dp', None, 'mp')
- grad_out: float32 [768, 768], P('mp', 'dp')
- grad_up: float32 [768, 3072], P('dp', 'mp')
- grad_down: float32 [3072, 768], P('mp', 'dp')
- grad_bias: float32 [2048, 256], P(('dp', 'mp'))
- grad_gains: float32 [2, 768], replicated
- newfirst_qkv: float32 [768, 3, 768], P('dp', None, 'mp')
- newfirst_out: float32 [768, 768], P('mp', 'dp')
- newfirst_up: float32 [768, 3072], P('dp', 'mp')
- newfirst_down: float32 [3072, 768], P('mp', 'dp')
- newfirst_bias: float32 [2048, 256], P(('dp', 'mp'))
- newfirst_gains: float32 [2, 768], replicated
- newsecond_qkv: float32 [768, 3, 768], P('dp', None, 'mp')
- newsecond_out: float32 [768, 768], P('mp', 'dp')
- newsecond_up: float32 [768, 3072], P('dp', 'mp')
- newsecond_down: float32 [3072, 768], P('mp', 'dp')
- newsecond_bias: float32 [2048, 256], P(('dp', 'mp'))
- newsecond_gains: float32 [2, 768], replicated
- update_qkv: float32 [768, 3, 768], P('dp', None, 'mp')
- update_out: float32 [768, 768], P('mp', 'dp')
- update_up: float32 [768, 3072], P('dp', 'mp')
- update_down: float32 [3072, 768], P('mp', 'dp')
- update_bias: float32 [2048, 256], P(('dp', 'mp'))
- update_gains: float32 [2, 768], replicated
- rms_stats: float32 [3], replicated
The draws below stay inside these ranges and needn't reach their ends.
Inputs may be any that keep to these rules, and one draw needn't show every extreme that they name: `lengths`: every length is at least half of 2048, and one of them is exactly 2048.
All inputs are finite; a program needn't handle non-finite values.
Results may differ from the reference program's by a relative error of at most 0.012.
Values may be sent and summed in bfloat16 or wider, within the bound.
A program may use at most 192 MiB of HBM per device.

```python
import math
import jax
import jax.numpy as jnp
from jax import lax

D = 768
FF = 3072
WIN = 256
LEN = 2048
ADAM_STEP = 10
BATCH = 8
TOKENS = 16384


def draw_lengths(key, part):
    key_one, key_two = jax.random.split(jax.random.fold_in(key, 7))
    factor_one = jax.random.randint(key_one, (BATCH,), 0, 17)
    factor_two = jax.random.randint(key_two, (BATCH,), 0, 17)
    surplus = LEN // 2 * factor_one * factor_two // 256
    lengths = LEN // 2 + surplus
    return lengths.at[0].set(LEN).astype(jnp.int32)


def block_levels(stream_key, dims, cuts, smallest, largest):
    def one(axis_at, shards_of):
        heights = jax.random.uniform(jax.random.fold_in(jax.random.fold_in(stream_key, 6), axis_at), (shards_of,), jnp.float32, smallest / len(cuts), largest / len(cuts))
        return jnp.repeat(jnp.exp(heights), dims[axis_at] // shards_of).reshape((-1,) + (1,) * (len(dims) - axis_at - 1))

    factor_of = one(*cuts[0])
    for cut in cuts[1:]:
        factor_of = factor_of * one(*cut)
    return factor_of


def noise(rng, shape, scale, reach, pieces=(), kind=jnp.bfloat16):
    values = scale * jax.random.normal(rng, shape, jnp.float32)
    if pieces:
        values = values * block_levels(rng, shape, pieces, -0.22, 0.18)
    return jnp.clip(values, -reach, reach).astype(kind)


def setup_inputs(seed: int = 0) -> dict:
    splits = jax.random.split(jax.random.key(seed), 22)
    return {
        "block_input": noise(splits[0], (BATCH, LEN, D), 1.0, 6.0, ((0, 8), (1, 4))),
        "out_cotangent": noise(splits[1], (BATCH, LEN, D), 1.0, 6.0, ((0, 8), (1, 4))),
        "lengths": draw_lengths(jax.random.fold_in(splits[21], 71), 0),
        "w_qkv": noise(splits[3], (D, 3, D), D ** -0.5, 0.21875, ((0, 8), (2, 4)), jnp.float32),
        "w_out": noise(splits[4], (D, D), (max(D // 64, 1)) ** -0.5, 1.75, ((0, 4), (1, 8)), jnp.float32),
        "w_up": noise(splits[5], (D, FF), D ** -0.5, 0.21875, ((0, 8), (1, 4)), jnp.float32),
        "w_down": noise(splits[6], (FF, D), FF ** -0.5, 0.109375, ((0, 4), (1, 8)), jnp.float32),
        "pair_bias": noise(splits[7], (LEN, WIN), 0.3, 1.5, ((0, 32),), jnp.float32),
        "norm_gains": jnp.clip(1.0 + 0.1 * jax.random.normal(splits[8], (2, D), jnp.float32), 0.5, 1.5),
        "first_qkv": noise(splits[9], (D, 3, D), 0.1, 0.625, ((0, 8), (2, 4)), jnp.float32),
        "first_out": noise(splits[10], (D, D), 0.02, 0.125, ((0, 4), (1, 8)), jnp.float32),
        "first_up": noise(splits[11], (D, FF), 0.1, 0.625, ((0, 8), (1, 4)), jnp.float32),
        "first_down": noise(splits[12], (FF, D), 0.1, 0.625, ((0, 4), (1, 8)), jnp.float32),
        "first_bias": noise(splits[13], (LEN, WIN), 0.005, 0.03125, ((0, 32),), jnp.float32),
        "first_gains": noise(splits[14], (2, D), 0.1, 0.625, (), jnp.float32),
        "second_qkv": jnp.clip(jnp.exp(math.log(0.03) - 2.70805 * jax.random.uniform(splits[15], (D, 3, D), jnp.float32) ** block_levels(splits[15], (D, 3, D), ((0, 8), (2, 4)), -0.2, 0.2)), 0.002, 0.03),
        "second_out": jnp.clip(jnp.exp(math.log(0.0015) - 2.7080502 * jax.random.uniform(splits[16], (D, D), jnp.float32) ** block_levels(splits[16], (D, D), ((0, 4), (1, 8)), -0.2, 0.2)), 0.0001, 0.0015),
        "second_up": jnp.clip(jnp.exp(math.log(0.03) - 2.70805 * jax.random.uniform(splits[17], (D, FF), jnp.float32) ** block_levels(splits[17], (D, FF), ((0, 8), (1, 4)), -0.2, 0.2)), 0.002, 0.03),
        "second_down": jnp.clip(jnp.exp(math.log(0.03) - 2.70805 * jax.random.uniform(splits[18], (FF, D), jnp.float32) ** block_levels(splits[18], (FF, D), ((0, 4), (1, 8)), -0.2, 0.2)), 0.002, 0.03),
        "second_bias": jnp.clip(jnp.exp(math.log(0.00075) - 2.7080502 * jax.random.uniform(splits[19], (LEN, WIN), jnp.float32) ** block_levels(splits[19], (LEN, WIN), ((0, 32),), -0.2, 0.2)), 4.999999873689376e-05, 0.00075),
        "second_gains": jnp.clip(jnp.exp(jax.random.uniform(splits[20], (2, D), jnp.float32, math.log(0.002), math.log(0.03))), 0.002, 0.03),
    }


EPS = 1e-06
BETA_ONE = 0.9
BETA_TWO = 0.99
LEARN_RATE = 0.03
WEIGHT_DECAY = 0.1
ADAM_EPS = 1e-08
PRECISE = lax.Precision.HIGHEST

@jax.custom_vjp
def low(v):
    return lax.optimization_barrier(v.astype(jnp.bfloat16)).astype(jnp.float32)

@jax.custom_vjp
def low_back(v):
    return v

def low_keep(v):
    return (low(v), None)

def low_pass(kept, grad):
    return (grad,)

def back_keep(v):
    return (v, None)

def back_low(kept, grad):
    return (low(grad),)
low.defvjp(low_keep, low_pass)
low_back.defvjp(back_keep, back_low)

def skew_band(bias_rows):
    height, width = bias_rows.shape
    padded = jnp.concatenate([jnp.zeros((height, 1), bias_rows.dtype), bias_rows[:, ::-1], jnp.zeros((height, height), bias_rows.dtype)], axis=1)
    return padded.reshape(-1)[:height * (height + width)].reshape(height, height + width)

def mix_sequence(queries, key_rows, value_rows, bias_low):
    seq_len, channels = queries.shape
    window = bias_low.shape[1]
    block = min(512, seq_len)
    exp_keys = jnp.exp(key_rows)
    front = jnp.zeros((window, channels), jnp.float32)
    keys_pad = jnp.concatenate([front, low(exp_keys)], axis=0)
    product_pad = jnp.concatenate([front, low(exp_keys * value_rows)], axis=0)

    def one_block(block_index):
        offset = block_index * block
        band_rows = skew_band(lax.dynamic_slice_in_dim(bias_low, offset, block, 0))
        key_block = lax.dynamic_slice_in_dim(keys_pad, offset, block + window, 0)
        product_block = lax.dynamic_slice_in_dim(product_pad, offset, block + window, 0)
        numerator = low_back(jnp.dot(band_rows, product_block, precision=PRECISE))
        denominator = low_back(jnp.dot(band_rows, key_block, precision=PRECISE))
        return numerator / denominator
    ratios = lax.map(jax.checkpoint(one_block), jnp.arange(seq_len // block, dtype=jnp.int32))
    return jax.nn.sigmoid(queries) * ratios.reshape(seq_len, channels)

def rms_norm(inputs, gain):
    rescale = lax.rsqrt(lax.optimization_barrier(jnp.mean(inputs * inputs, axis=-1, keepdims=True)) + EPS)
    return inputs * rescale * gain

def group_layer(group_rows, w_query, w_mix, w_hidden, w_back, bias_low, gain_one, gain_two):
    normed_one = low(rms_norm(group_rows, gain_one))
    projected = low_back(jnp.einsum('std,dkc->stkc', normed_one, w_query, precision=PRECISE))
    mixed = jax.vmap(mix_sequence, in_axes=(0, 0, 0, None))(projected[:, :, 0], projected[:, :, 1], projected[:, :, 2], bias_low)
    attn_part = low_back(jnp.einsum('stc,cd->std', low(mixed), w_mix, precision=PRECISE))
    resid = group_rows + attn_part
    normed_two = low(rms_norm(resid, gain_two))
    pre_act = low_back(jnp.einsum('std,df->stf', normed_two, w_hidden, precision=PRECISE))
    act_low = low(jax.nn.gelu(pre_act, approximate=True))
    ffn_part = low_back(jnp.einsum('stf,fd->std', act_low, w_back, precision=PRECISE))
    return (resid + ffn_part, attn_part, ffn_part)

def forward(input_float, w_qkv, w_out, w_up, w_down, pair_bias, norm_gains):
    w_query = low(w_qkv)
    w_mix = low(w_out)
    w_hidden = low(w_up)
    w_back = low(w_down)
    bias_low = low(jnp.exp(pair_bias))
    groups = input_float.reshape(-1, 2, LEN, D)

    def group_step(carry, group_rows):
        return (carry, group_layer(group_rows, w_query, w_mix, w_hidden, w_back, bias_low, norm_gains[0], norm_gains[1]))
    unused, results = lax.scan(jax.checkpoint(group_step), jnp.zeros((), jnp.float32), groups)
    out_rows = results[0].reshape(BATCH, LEN, D)
    attn_rows = results[1].reshape(BATCH, LEN, D)
    ffn_rows = results[2].reshape(BATCH, LEN, D)
    return (out_rows, (attn_rows, ffn_rows))

def adam_step(param, grad, first, second, step_value, decay):
    new_first = BETA_ONE * first + (1.0 - BETA_ONE) * grad
    new_second = BETA_TWO * second + (1.0 - BETA_TWO) * grad * grad
    first_hat = new_first / (1.0 - jnp.power(jnp.float32(BETA_ONE), step_value))
    second_hat = new_second / (1.0 - jnp.power(jnp.float32(BETA_TWO), step_value))
    update = -LEARN_RATE * (first_hat / (jnp.sqrt(second_hat) + ADAM_EPS) + decay * param)
    return (new_first, new_second, update)

def reference(block_input, out_cotangent, lengths, w_qkv, w_out, w_up, w_down, pair_bias, norm_gains, first_qkv, first_out, first_up, first_down, first_bias, first_gains, second_qkv, second_out, second_up, second_down, second_bias, second_gains):
    input_float = block_input.astype(jnp.float32)
    out_rows, pullback, aux_rows = jax.vjp(forward, input_float, w_qkv, w_out, w_up, w_down, pair_bias, norm_gains, has_aux=True)
    attn_rows, ffn_rows = aux_rows
    positions = jnp.arange(LEN, dtype=jnp.int32)
    valid_mask = (positions[None, :] < lengths[:, None]).astype(jnp.float32)
    cotangent = out_cotangent.astype(jnp.float32) * valid_mask[:, :, None]
    grads = pullback(cotangent)
    grad_scale = float(TOKENS) ** (-0.5)
    params = (w_qkv, w_out, w_up, w_down, pair_bias, norm_gains)
    firsts = (first_qkv, first_out, first_up, first_down, first_bias, first_gains)
    seconds = (second_qkv, second_out, second_up, second_down, second_bias, second_gains)
    decays = (WEIGHT_DECAY, WEIGHT_DECAY, WEIGHT_DECAY, WEIGHT_DECAY, 0.0, 0.0)
    step_value = jnp.float32(ADAM_STEP)
    scaled = [grads[place + 1] * grad_scale for place in range(6)]
    states = [adam_step(params[place], scaled[place], firsts[place], seconds[place], step_value, decays[place]) for place in range(6)]
    count = jnp.sum(valid_mask)
    totals = jnp.stack([jnp.sum(valid_mask[:, :, None] * input_float * input_float), jnp.sum(valid_mask[:, :, None] * attn_rows * attn_rows), jnp.sum(valid_mask[:, :, None] * ffn_rows * ffn_rows)])
    rms_stats = jnp.sqrt(totals / (count * D))
    return (out_rows.astype(jnp.bfloat16), grads[0], scaled[0], scaled[1], scaled[2], scaled[3], scaled[4], scaled[5], states[0][0], states[1][0], states[2][0], states[3][0], states[4][0], states[5][0], states[0][1], states[1][1], states[2][1], states[3][1], states[4][1], states[5][1], states[0][2], states[1][2], states[2][2], states[3][2], states[4][2], states[5][2], rms_stats)
```

```python
import functools

import jax
import jax.numpy as jnp
from jax import lax
from jax.experimental import pallas as pl
from jax.experimental.pallas import tpu as pltpu
from jax.sharding import Mesh
from jax.sharding import PartitionSpec as P

LEN = 2048
ADAM_STEP = 10
EPS = 1e-06
BETA_ONE = 0.9
BETA_TWO = 0.99
LEARN_RATE = 0.03
WEIGHT_DECAY = 0.1
ADAM_EPS = 1e-08

F32 = jnp.float32
BF = jnp.bfloat16
ZN, YN = 4, 2
GROUPS = ZN * YN
CHUNK = 128
GELU_C = 0.7978845608028654
GELU_A = 0.044715


def dot_nn(a, b):
    return jnp.dot(a, b, preferred_element_type=F32)


def dot_nt(a, b):
    return lax.dot_general(a, b, (((1,), (1,)), ((), ())), preferred_element_type=F32)


def dot_tn(a, b):
    return lax.dot_general(a, b, (((0,), (0,)), ((), ())), preferred_element_type=F32)


def loop_rows(count, step, body, unroll=False):
    @pl.loop(0, count // step, unroll=unroll)
    def _(index):
        body(pl.multiple_of(index * step, step))


class Copies:
    def __init__(self):
        self.started = []

    def go(self, copy):
        copy.start()
        self.started.append(copy)

    def drain(self):
        for copy in self.started:
            copy.wait_send()
        self.started = []


def block_kernel(
    x_ref,
    cot_ref,
    valid_ref,
    gains_ref,
    wa_ref,
    wu_ref,
    wd_ref,
    eb_ref,
    blk_ref,
    gin_ref,
    ga_ref,
    gu_ref,
    gd_ref,
    gb_ref,
    stat_ref,
    mix_w,
    up_w,
    down_w,
    band_rows,
    x_halo,
    full_w,
    normed,
    sig,
    expk,
    val,
    ratio,
    rden,
    resid,
    exp_low,
    kv_low,
    bands,
    mixed,
    normed_two,
    cot_low,
    act,
    dpre,
    ffn,
    dn_two,
    dnum,
    dden,
    bias_part,
    bias_recv_y,
    bias_recv_z,
    stats,
    stats_recv,
    recv_core,
    recv_one,
    recv_two,
    recv_z,
    ag_send,
    ag_recv,
    rs_send,
    rs_recv,
    halo_send,
    halo_recv,
    bias_send,
    bias_recv,
    stat_send,
    stat_recv,
):
    tokens, width = x_ref.shape
    window = x_halo.shape[0]
    rows = wa_ref.shape[0]
    chan = width // 4
    group = lax.axis_index("dph")
    inner = lax.axis_index("dpl")
    mp = lax.axis_index("mp")
    z, y = group // YN, group % YN
    x, c = mp // 2, mp % 2

    def device(zs, ys, xs, cs):
        return (zs * YN + ys, inner, xs * 2 + cs)

    def z_at(k):
        return (z + k) % ZN

    core_peer = device(z, y, x, 1 - c)
    x_peer = device(z, y, 1 - x, c)
    y_peer = device(z, 1 - y, x, c)
    diag_peer = device(z, y, 1 - x, 1 - c)
    z_peers = [device(z_at(k), y, x, c) for k in range(1, ZN)]

    barrier = pltpu.get_barrier_semaphore()
    friends = [core_peer, x_peer, y_peer, diag_peer] + z_peers
    for friend in friends:
        pl.semaphore_signal(barrier, inc=1, device_id=friend, device_id_type=MESH)
    pl.semaphore_wait(barrier, len(friends))

    out = Copies()

    half = 2 * chan
    gather_pieces = [
        (mix_w, 0, half, True),
        (mix_w, half, half, False),
        (None, 0, 0, True),
        (up_w, 0, up_w.shape[2], True),
        (down_w, 0, down_w.shape[2], False),
    ]

    def place(piece, zs, ys, xs, cs):
        buf, start, size, _ = gather_pieces[piece]
        if buf is None:
            return band_rows.at[(zs * YN + ys) * 4 + xs * 2 + cs]
        at = pl.multiple_of((zs * YN + ys) * rows, 32)
        return buf.at[xs * 2 + cs, pl.ds(at, rows), pl.ds(start, size)]

    def ag(piece, loc, peer, slot):
        ref = place(piece, *loc)
        return pltpu.make_async_remote_copy(
            src_ref=ref,
            dst_ref=ref,
            send_sem=ag_send.at[piece, slot],
            recv_sem=ag_recv.at[piece, slot],
            device_id=peer,
            device_id_type=MESH,
        )

    own = (z, y, x, c)

    def behind(k):
        return (z + ZN - k) % ZN

    def spot(kind, k):
        return (behind(k), y if kind in (0, 2) else 1 - y, x if kind in (0, 1) else 1 - x, c)

    def to_core(piece, kind, k):
        out.go(ag(piece, spot(kind, k), core_peer, 15 + kind * 4 + k))

    def arrived(piece, slot):
        ag(piece, own, core_peer, slot).wait_recv()

    def gather_start(pieces):
        for p in pieces:
            for k in range(1, ZN):
                out.go(ag(p, own, device(z_at(k), y, x, c), k - 1))
        for p in pieces:
            out.go(ag(p, own, y_peer, 3))
            out.go(ag(p, own, x_peer, 7))
            to_core(p, 0, 0)

    def gather_z(pieces, k):
        for p in pieces:
            arrived(p, k - 1)
            out.go(ag(p, spot(0, k), y_peer, 3 + k))
            out.go(ag(p, spot(0, k), x_peer, 7 + k))
            to_core(p, 0, k)

    def gather_turn(pieces, k):
        for p in pieces:
            if gather_pieces[p][3]:
                arrived(p, 3 + k)
                out.go(ag(p, spot(1, k), x_peer, 11 + k))
                to_core(p, 1, k)
            else:
                arrived(p, 7 + k)
                out.go(ag(p, spot(2, k), y_peer, 11 + k))
                to_core(p, 2, k)

    def gather_side(pieces, k):
        for p in pieces:
            if gather_pieces[p][3]:
                arrived(p, 7 + k)
                to_core(p, 2, k)
            else:
                arrived(p, 3 + k)
                to_core(p, 1, k)

    def gather_last(pieces, k):
        for p in pieces:
            arrived(p, 11 + k)
            to_core(p, 3, k)

    def gather_core(pieces):
        for p in pieces:
            for slot in range(15, 31):
                arrived(p, slot)

    mix_w[mp, pl.ds(pl.multiple_of(group * rows, 32), rows), :] = wa_ref[...]
    up_w[mp, pl.ds(pl.multiple_of(group * rows, 32), rows), :] = wu_ref[...]
    down_w[mp, pl.ds(pl.multiple_of(group * rows, 32), rows), :] = wd_ref[...]
    band_rows[group * 4 + mp] = eb_ref[...]
    band_rows[4 * GROUPS : 4 * GROUPS + 4] = jnp.zeros((4,) + eb_ref.shape, BF)

    halo_copy = pltpu.make_async_remote_copy(
        src_ref=x_ref.at[pl.ds(tokens - window, window)],
        dst_ref=x_halo,
        send_sem=halo_send.at[0],
        recv_sem=halo_recv.at[0],
        device_id=(group, inner, (mp + 1) % 4),
        device_id_type=MESH,
    )

    @pl.when(mp < 3)
    def _():
        halo_copy.start()

    def gather(pieces):
        gather_start(pieces)
        for k in range(1, ZN):
            gather_z(pieces, k)
        for k in range(ZN):
            gather_turn(pieces, k)
        for k in range(ZN):
            gather_side(pieces, k)
        for k in range(ZN):
            gather_last(pieces, k)
        gather_core(pieces)

    stats[0] = jnp.zeros(stats.shape[1:], F32)

    def add_stat(row, value):
        stats[0, row : row + 1, :] += jnp.sum(value, axis=0, keepdims=True)

    def rms(value):
        return lax.rsqrt(jnp.mean(value * value, axis=-1, keepdims=True) + EPS)

    def norm_own(at):
        part = pl.ds(at, CHUNK)
        xf = x_ref[part].astype(F32)
        normed[pl.ds(at + window, CHUNK)] = (xf * rms(xf) * gains_ref[0:1]).astype(BF)
        mask = valid_ref[part]
        add_stat(2, mask * xf * xf)
        add_stat(5, mask + jnp.zeros_like(xf))
        cot_low[part] = (cot_ref[part].astype(F32) * mask).astype(BF)

    def norm_halo(at):
        part = pl.ds(at, CHUNK)
        xf = x_halo[part].astype(F32)
        normed[part] = (xf * rms(xf) * gains_ref[0:1]).astype(BF)

    def repack(at):
        part = pl.ds(at, rows)
        for kind in range(4):
            full_w[kind, part] = jnp.concatenate(
                [mix_w[m, part, kind * chan : (kind + 1) * chan] for m in range(4)], axis=1
            )

    def project_halo(at):
        part = pl.ds(at, CHUNK)
        a = normed[part]
        ek = jnp.where(mp > 0, jnp.exp(dot_nn(a, full_w[1])), 0.0)
        exp_low[part] = ek.astype(BF)
        kv_low[part] = (ek * dot_nn(a, full_w[2])).astype(BF)

    def project_own(at):
        part = pl.ds(at, CHUNK)
        shifted = pl.ds(at + window, CHUNK)
        a = normed[shifted]
        ek = jnp.exp(dot_nn(a, full_w[1]))
        v = dot_nn(a, full_w[2])
        exp_low[shifted] = ek.astype(BF)
        kv_low[shifted] = (ek * v).astype(BF)
        expk[part] = ek
        val[part] = v
        sig[part] = jax.nn.sigmoid(dot_nn(a, full_w[0]))

    def build_bands():
        for i in range(3):
            raw = band_rows[pl.ds(mp * 8 + i * 4, 4)].reshape(window, window).astype(F32)
            wide = jnp.concatenate([raw, jnp.zeros_like(raw)], axis=1)
            bands[i] = pltpu.roll(wide, 1, 1, stride=1, stride_axis=0).astype(BF)

    def mix_rows(i):
        part = slice(i * window, (i + 1) * window)
        near = slice(i * window, (i + 2) * window)
        num = dot_nn(bands[i], kv_low[near])
        den = dot_nn(bands[i], exp_low[near])
        ratio[part] = num / den
        rden[part] = 1.0 / den

    def attend(at):
        part = pl.ds(at, CHUNK)
        low = (sig[part] * ratio[part]).astype(BF)
        mixed[part] = low
        attn = dot_nt(low, full_w[3])
        add_stat(3, valid_ref[part] * attn * attn)
        total = x_ref[part].astype(F32) + attn
        resid[part] = total
        normed_two[part] = (total * rms(total) * gains_ref[1:2]).astype(BF)

    def hidden_rows(m, first):
        def body(at):
            part = pl.ds(at, CHUNK)
            p = dot_nn(normed_two[part], up_w[m])
            da = dot_nn(cot_low[part], down_w[m])
            t = jnp.tanh(GELU_C * (p + GELU_A * (p * p * p)))
            low = (0.5 * p * (1.0 + t)).astype(BF)
            slope = 0.5 * (1.0 + t) + 0.5 * p * (1.0 - t * t) * (
                GELU_C * (1.0 + 3.0 * GELU_A * (p * p))
            )
            dlow = (da * slope).astype(BF)
            act[part] = low
            dpre[part] = dlow
            f = dot_nt(low, down_w[m])
            d = dot_nt(dlow, up_w[m])
            if first:
                ffn[part] = f
                dn_two[part] = d
            else:
                ffn[part] += f
                dn_two[part] += d

        return body

    def weight_grad(result, left, right):
        for at in range(0, result.shape[1], 256):
            part = slice(at, at + 256)
            result[:, part] = dot_tn(left[...], right[:, part]).astype(BF)

    def hidden_slab(m, first):
        loop_rows(tokens, CHUNK, hidden_rows(m, first))
        weight_grad(up_w.at[m], normed_two, dpre)
        weight_grad(down_w.at[m], cot_low, act)

    def close_hidden(at):
        part = pl.ds(at, CHUNK)
        mask = valid_ref[part]
        f = ffn[part]
        res = resid[part]
        add_stat(4, mask * f * f)
        blk_ref[part] = (res + f).astype(BF)
        d = dn_two[part]
        r = rms(res)
        u = gains_ref[1:2] * d
        grad = (
            cot_ref[part].astype(F32) * mask
            + r * u
            - res * (r * r * r) * jnp.mean(u * res, axis=-1, keepdims=True)
        )
        add_stat(1, d * res * r)
        ffn[part] = grad
        act[part] = grad.astype(BF)

    def back_attend(at):
        part = pl.ds(at, CHUNK)
        dm = dot_nn(act[part], full_w[3])
        sg = sig[part]
        rt = ratio[part]
        scaled = dm * sg
        normed_two[part] = (scaled * rt * (1.0 - sg)).astype(BF)
        dn = scaled * rden[part]
        dnum[part] = dn.astype(BF)
        dden[part] = (-dn * rt).astype(BF)

    def halo_back(slot, buf):
        return pltpu.make_async_remote_copy(
            src_ref=buf.at[pl.ds(0, window)],
            dst_ref=buf.at[pl.ds(tokens, window)],
            send_sem=halo_send.at[slot],
            recv_sem=halo_recv.at[slot],
            device_id=(group, inner, (mp + 3) % 4),
            device_id_type=MESH,
        )

    def band_grad(i):
        part = slice(i * window, (i + 1) * window)
        near = slice(i * window, (i + 2) * window)
        dn_two[part, 0 : 2 * window] = dot_nt(dnum[part], kv_low[near]) + dot_nt(dden[part], exp_low[near])

    def unskew():
        wide = 2 * window
        line = lax.broadcasted_iota(jnp.int32, (8, wide), 0)

        @pl.loop(0, tokens // 8, unroll=8)
        def _(index):
            at = pl.multiple_of(index * 8, 8)
            v = pltpu.roll(dn_two[pl.ds(at, 8), 0:wide], wide - 1 - at % window, 1)
            for bit in (1, 2, 4):
                v = jnp.where((line & bit) != 0, pltpu.roll(v, wide - bit, 1), v)
            dn_two[pl.ds(at, 8), 0:window] = v[:, 0:window]

        for j in range(GROUPS):
            bias_part[j] = dn_two[j * 64 : (j + 1) * 64, 0:window].astype(BF)

    def back_keys(j):
        here = slice(j * window, (j + 1) * window)
        then = slice((j + 1) * window, (j + 2) * window)
        right = bands[j, :, window:]
        left = bands[j + 1, :, :window]
        dkv = dot_tn(right, dnum[here]) + dot_tn(left, dnum[then])
        de = dot_tn(right, dden[here]) + dot_tn(left, dden[then])
        ek = expk[here]
        cot_low[here] = (dkv * ek).astype(BF)
        dpre[here] = ((de + dkv * val[here]) * ek).astype(BF)

    def back_input(at):
        part = pl.ds(at, CHUNK)
        d = (
            dot_nt(normed_two[part], full_w[0])
            + dot_nt(dpre[part], full_w[1])
            + dot_nt(cot_low[part], full_w[2])
        )
        xf = x_ref[part].astype(F32)
        r = rms(xf)
        u = gains_ref[0:1] * d
        gin_ref[part] = (
            ffn[part] + r * u - xf * (r * r * r) * jnp.mean(u * xf, axis=-1, keepdims=True)
        )
        add_stat(0, d * xf * r)

    def unpack(at):
        part = pl.ds(at, rows)
        for m in range(4):
            mix_w[m, part] = jnp.concatenate(
                [full_w[kind, part, m * chan : (m + 1) * chan] for kind in range(4)], axis=1
            )

    scatter_pieces = [
        (mix_w, 0, half, True, ga_ref, 0),
        (mix_w, half, half, False, ga_ref, half),
        (up_w, 0, up_w.shape[2], True, gu_ref, 2 * half),
        (down_w, 0, down_w.shape[2], False, gd_ref, 2 * half + up_w.shape[2]),
    ]

    def rs(piece, src, dst, peer, slot):
        return pltpu.make_async_remote_copy(
            src_ref=src,
            dst_ref=dst,
            send_sem=rs_send.at[piece, slot],
            recv_sem=rs_recv.at[piece, slot],
            device_id=peer,
            device_id_type=MESH,
        )

    def block(piece, xs, zs, ys, count=1):
        buf, start, size = scatter_pieces[piece][:3]
        at = pl.multiple_of((zs * YN + ys) * rows, 32)
        return buf.at[xs * 2 + c, pl.ds(at, rows * count), pl.ds(start, size)]

    def lanes(piece):
        return pl.ds(scatter_pieces[piece][5], scatter_pieces[piece][2])

    def core_copies(p):
        buf, start, size = scatter_pieces[p][:3]
        return [
            rs(
                p,
                buf.at[xs * 2 + 1 - c, :, pl.ds(start, size)],
                recv_core.at[xs, :, lanes(p)],
                core_peer,
                xs,
            )
            for xs in range(2)
        ]

    def one_copies(p):
        if scatter_pieces[p][3]:
            return [
                rs(p, block(p, 1 - x, k // YN, k % YN), recv_one.at[k, :, lanes(p)], x_peer, 2 + k)
                for k in range(GROUPS)
            ]
        return [
            rs(
                p,
                block(p, k // ZN, k % ZN, 1 - y),
                recv_one.at[k, :, lanes(p)],
                y_peer,
                2 + k,
            )
            for k in range(GROUPS)
        ]

    def one_home(p, k):
        if scatter_pieces[p][3]:
            return block(p, x, k // YN, k % YN)
        return block(p, k // ZN, k % ZN, y)

    def two_copies(p):
        if scatter_pieces[p][3]:
            return [
                rs(p, block(p, x, zs, 1 - y), recv_two.at[zs, :, lanes(p)], y_peer, 10 + zs)
                for zs in range(ZN)
            ]
        return [
            rs(p, block(p, 1 - x, zs, y), recv_two.at[zs, :, lanes(p)], x_peer, 10 + zs)
            for zs in range(ZN)
        ]

    def z_copies(p):
        return [
            rs(
                p,
                block(p, x, z_at(k), y),
                recv_z.at[k - 1, :, lanes(p)],
                z_peers[k - 1],
                13 + k,
            )
            for k in range(1, ZN)
        ]

    def scatter(pieces):
        core = {p: core_copies(p) for p in pieces}
        for p in pieces:
            for copy in core[p]:
                out.go(copy)
        ones = {p: one_copies(p) for p in pieces}
        for p in pieces:
            buf, start, size = scatter_pieces[p][:3]
            for xs in range(2):
                core[p][xs].wait_recv()

                def body(at):
                    part = pl.ds(at, rows)
                    buf[xs * 2 + c, part, pl.ds(start, size)] += recv_core[xs, part, lanes(p)]

                loop_rows(GROUPS * rows, rows, body)
            for copy in ones[p]:
                out.go(copy)
        twos = {p: two_copies(p) for p in pieces}
        for p in pieces:
            for k in range(GROUPS):
                ones[p][k].wait_recv()
                home = one_home(p, k)
                home[...] += recv_one[k, :, lanes(p)]
            for copy in twos[p]:
                out.go(copy)
        zs_all = {p: z_copies(p) for p in pieces}
        for p in pieces:
            for zs in range(ZN):
                twos[p][zs].wait_recv()
                home = block(p, x, zs, y)
                home[...] += recv_two[zs, :, lanes(p)]
            for copy in zs_all[p]:
                out.go(copy)
        for p in pieces:
            total = block(p, x, z, y)[...].astype(F32)
            for k in range(1, ZN):
                zs_all[p][k - 1].wait_recv()
                total = total + recv_z[k - 1, :, lanes(p)].astype(F32)
            result, start, size = (
                scatter_pieces[p][4],
                scatter_pieces[p][1],
                scatter_pieces[p][2],
            )
            result[:, pl.ds(start, size)] = total

    def scatter_bias():
        def copy(src, dst, peer, slot):
            return pltpu.make_async_remote_copy(
                src_ref=src,
                dst_ref=dst,
                send_sem=bias_send.at[slot],
                recv_sem=bias_recv.at[slot],
                device_id=peer,
                device_id_type=MESH,
            )

        first = [
            copy(bias_part.at[zs * YN + 1 - y], bias_recv_y.at[zs], y_peer, zs)
            for zs in range(ZN)
        ]
        for item in first:
            out.go(item)
        for zs in range(ZN):
            first[zs].wait_recv()
            bias_part[zs * YN + y] += bias_recv_y[zs]
        second = [
            copy(bias_part.at[z_at(k) * YN + y], bias_recv_z.at[k - 1], z_peers[k - 1], 3 + k)
            for k in range(1, ZN)
        ]
        for item in second:
            out.go(item)
        total = bias_part[z * YN + y].astype(F32)
        for k in range(1, ZN):
            second[k - 1].wait_recv()
            total = total + bias_recv_z[k - 1].astype(F32)
        gb_ref[...] = total

    def reduce_stats():
        def copy(step, slot, peer):
            return pltpu.make_async_remote_copy(
                src_ref=stats.at[step],
                dst_ref=stats_recv.at[slot],
                send_sem=stat_send.at[slot],
                recv_sem=stat_recv.at[slot],
                device_id=peer,
                device_id_type=MESH,
            )

        for step, peer in enumerate((core_peer, x_peer, y_peer)):
            item = copy(step, step, peer)
            out.go(item)
            item.wait_recv()
            stats[step + 1] = stats[step] + stats_recv[step]
        items = [copy(3, 2 + k, z_peers[k - 1]) for k in range(1, ZN)]
        for item in items:
            out.go(item)
        total = stats[3]
        for k, item in enumerate(items):
            item.wait_recv()
            total = total + stats_recv[3 + k]
        stat_ref[...] = total

    gather([0, 1, 2])
    gather([3, 4])
    loop_rows(tokens, CHUNK, norm_own)

    @pl.when(mp > 0)
    def _():
        halo_copy.wait_recv()

    @pl.when(mp == 0)
    def _():
        x_halo[...] = jnp.zeros_like(x_halo)

    loop_rows(window, CHUNK, norm_halo)
    loop_rows(GROUPS * rows, rows, repack)
    loop_rows(window, CHUNK, project_halo)
    loop_rows(tokens, CHUNK, project_own)
    build_bands()
    for i in range(2):
        mix_rows(i)
    loop_rows(tokens, CHUNK, attend)
    out.drain()
    for r in range(4):
        slab = (x ^ (r // 2)) * 2 + (c ^ (r % 2))
        hidden_slab(slab, r == 0)
    loop_rows(tokens, CHUNK, close_hidden)
    loop_rows(tokens, CHUNK, back_attend)

    backs = [halo_back(1, dnum), halo_back(2, dden)]

    @pl.when(mp > 0)
    def _():
        for item in backs:
            item.start()

    weight_grad(full_w.at[3], act, mixed)
    for i in range(2):
        band_grad(i)
    unskew()

    @pl.when(mp < 3)
    def _():
        for item in backs:
            item.wait_recv()

    @pl.when(mp == 3)
    def _():
        dnum[pl.ds(tokens, window)] = jnp.zeros((window, width), BF)
        dden[pl.ds(tokens, window)] = jnp.zeros((window, width), BF)

    for j in range(2):
        back_keys(j)
    loop_rows(tokens, CHUNK, back_input)
    for kind, grad in enumerate((normed_two, dpre, cot_low)):
        weight_grad(full_w.at[kind], normed.at[pl.ds(window, tokens)], grad)
    loop_rows(GROUPS * rows, rows, unpack)
    scatter([2, 3, 0, 1])
    scatter_bias()
    reduce_stats()

    @pl.when(mp < 3)
    def _():
        halo_copy.wait_send()

    @pl.when(mp > 0)
    def _():
        for item in backs:
            item.wait_send()

    out.drain()


def run_block(x, cot, valid, gains, wa, wu, wd, eb):
    tokens, width = x.shape
    window = eb.shape[1]
    rows = wa.shape[0]
    full = rows * GROUPS
    vmem = pl.BlockSpec(memory_space=pltpu.VMEM)
    lanes = wa.shape[1] + wu.shape[1] + wd.shape[1]

    def shape(*dims, kind=F32):
        return jax.ShapeDtypeStruct(dims, kind)

    def buf(*dims, kind=F32):
        return pltpu.VMEM(dims, kind)

    def low(*dims):
        return pltpu.VMEM(dims, BF)

    dma = pltpu.SemaphoreType.DMA
    return pl.pallas_call(
        block_kernel,
        out_shape=(
            shape(tokens, width, kind=BF),
            shape(tokens, width),
            shape(*wa.shape),
            shape(*wu.shape),
            shape(*wd.shape),
            shape(*eb.shape),
            shape(8, width),
        ),
        in_specs=[vmem] * 8,
        out_specs=(vmem,) * 7,
        scratch_shapes=[
            low(4, full, wa.shape[1]),
            low(4, full, wu.shape[1]),
            low(4, full, wd.shape[1]),
            low(4 * GROUPS + 4, *eb.shape),
            low(window, width),
            low(4, full, width),
            low(window + tokens, width),
            buf(tokens, width),
            buf(tokens, width),
            buf(tokens, width),
            buf(tokens, width),
            buf(tokens, width),
            buf(tokens, width),
            low(window + tokens, width),
            low(window + tokens, width),
            low(3, window, 2 * window),
            low(tokens, width),
            low(tokens, width),
            low(tokens, width),
            low(tokens, wu.shape[1]),
            low(tokens, wu.shape[1]),
            buf(tokens, width),
            buf(tokens, width),
            low(tokens + window, width),
            low(tokens + window, width),
            low(GROUPS, *eb.shape),
            low(ZN, *eb.shape),
            low(ZN - 1, *eb.shape),
            buf(4, 8, width),
            buf(6, 8, width),
            low(2, full, lanes),
            low(GROUPS, rows, lanes),
            low(ZN, rows, lanes),
            low(ZN - 1, rows, lanes),
            dma((5, 31)),
            dma((5, 31)),
            dma((4, 17)),
            dma((4, 17)),
            dma((3,)),
            dma((3,)),
            dma((7,)),
            dma((7,)),
            dma((6,)),
            dma((6,)),
        ],
        compiler_params=pltpu.CompilerParams(
            collective_id=0, has_side_effects=True, vmem_limit_bytes=63 * 1024 * 1024
        ),
    )(x, cot, valid, gains, wa, wu, wd, eb)


MESH = pl.DeviceIdType.MESH


def adam_step(param, grad, first, second, step_value, decay):
    new_first = BETA_ONE * first + (1.0 - BETA_ONE) * grad
    new_second = BETA_TWO * second + (1.0 - BETA_TWO) * grad * grad
    first_hat = new_first / (1.0 - jnp.power(jnp.float32(BETA_ONE), step_value))
    second_hat = new_second / (1.0 - jnp.power(jnp.float32(BETA_TWO), step_value))
    update = -LEARN_RATE * (first_hat / (jnp.sqrt(second_hat) + ADAM_EPS) + decay * param)
    return (new_first, new_second, update)


def shards(inner, block_input, out_cotangent, lengths, *rest):
    params, firsts, seconds = rest[:6], rest[6:12], rest[12:18]
    w_qkv, w_out, w_up, w_down, pair_bias, norm_gains = params
    _, tokens, width = block_input.shape
    chan = w_qkv.shape[2]
    positions = lax.axis_index("mp") * tokens + jnp.arange(tokens, dtype=jnp.int32)
    valid = (positions < lengths[0]).astype(F32)[:, None]
    own_a = jnp.concatenate(
        [w_qkv.reshape(w_qkv.shape[0], 3 * chan).astype(BF), w_out.astype(BF).T], axis=1
    )
    own_u = w_up.astype(BF)
    own_d = w_down.astype(BF).T
    own_e = jnp.exp(pair_bias).astype(BF)[:, ::-1]
    if inner > 1:
        own_a, own_u, own_d = (
            lax.all_gather(item, "dpl", axis=0, tiled=True) for item in (own_a, own_u, own_d)
        )
        count = own_e.shape[0]
        every = lax.all_gather(own_e, ("dpl", "mp"), axis=0, tiled=True)
        own_e = lax.dynamic_slice_in_dim(
            every, lax.axis_index("mp") * inner * count, inner * count, 0
        )
    block_low, grad_input, part_a, part_u, part_d, part_b, stats = run_block(
        block_input[0], out_cotangent[0], valid, norm_gains, own_a, own_u, own_d, own_e
    )
    if inner > 1:
        part_a, part_u, part_d = (
            lax.psum_scatter(item, "dpl", scatter_dimension=0, tiled=True)
            for item in (part_a, part_u, part_d)
        )
        part_b, stats = lax.psum((part_b, stats), "dpl")
        every = lax.all_gather(part_b, ("mp", "dph"), axis=0, tiled=True)
        count = pair_bias.shape[0]
        place = lax.axis_index(("dph", "dpl", "mp"))
        owned_b = lax.dynamic_slice_in_dim(every, place * count, count, 0)
    else:
        moves = []
        for group in range(GROUPS):
            for m in range(4):
                moves.append((group * 4 + m, m * GROUPS + group))
        owned_b = lax.ppermute(part_b, ("dph", "mp"), moves)
    grad_scale = float(lax.axis_size("dph") * inner * LEN) ** (-0.5)
    grads = [
        part_a[:, : 3 * chan].reshape(w_qkv.shape) * grad_scale,
        part_a[:, 3 * chan :].T * grad_scale,
        part_u * grad_scale,
        part_d.T * grad_scale,
        owned_b[:, ::-1] * jnp.exp(pair_bias) * grad_scale,
        stats[0:2] * grad_scale,
    ]
    decays = (WEIGHT_DECAY, WEIGHT_DECAY, WEIGHT_DECAY, WEIGHT_DECAY, 0.0, 0.0)
    step_value = jnp.float32(ADAM_STEP)
    states = [
        adam_step(params[i], grads[i], firsts[i], seconds[i], step_value, decays[i])
        for i in range(6)
    ]
    sums = jnp.sum(stats, axis=1)
    rms_stats = jnp.sqrt(sums[2:5] / sums[5])
    return (
        block_low[None],
        grad_input[None],
        *grads,
        *(state[0] for state in states),
        *(state[1] for state in states),
        *(state[2] for state in states),
        rms_stats,
    )


def solution(mesh):
    inner = mesh.shape["dp"] // GROUPS
    fine = Mesh(
        mesh.devices.reshape(GROUPS, inner, mesh.shape["mp"]),
        ("dph", "dpl", "mp"),
    )
    dp = ("dph", "dpl")
    weights = (
        P(dp, None, "mp"),
        P("mp", dp),
        P(dp, "mp"),
        P("mp", dp),
        P((*dp, "mp"), None),
        P(),
    )
    acts = P(dp, "mp", None)
    return jax.shard_map(
        functools.partial(shards, inner),
        mesh=fine,
        in_specs=(acts, acts, P(dp), *weights, *weights, *weights),
        out_specs=(acts, acts, *weights, *weights, *weights, *weights, P()),
        check_vma=False,
    )
```

```python
import functools

import jax
import jax.numpy as jnp
from jax import lax
from jax.experimental import pallas as pl
from jax.experimental.pallas import tpu as pltpu
from jax.sharding import Mesh
from jax.sharding import PartitionSpec as P

LEN = 2048
ADAM_STEP = 10
EPS = 1e-06
BETA_ONE = 0.9
BETA_TWO = 0.99
LEARN_RATE = 0.03
WEIGHT_DECAY = 0.1
ADAM_EPS = 1e-08

F32 = jnp.float32
BF = jnp.bfloat16
ZN, YN = 4, 2
GROUPS = ZN * YN
CHUNK = 128
GELU_C = 0.7978845608028654
GELU_A = 0.044715


def dot_nn(a, b):
    return jnp.dot(a, b, preferred_element_type=F32)


def dot_nt(a, b):
    return lax.dot_general(a, b, (((1,), (1,)), ((), ())), preferred_element_type=F32)


def dot_tn(a, b):
    return lax.dot_general(a, b, (((0,), (0,)), ((), ())), preferred_element_type=F32)


def loop_rows(count, step, body, unroll=False):
    @pl.loop(0, count // step, unroll=unroll)
    def _(index):
        body(pl.multiple_of(index * step, step))


class Copies:
    def __init__(self):
        self.started = {}

    def go(self, copy, tag=None):
        copy.start()
        self.started.setdefault(tag, []).append(copy)

    def drain(self, *tags):
        for tag in tags or list(self.started):
            for copy in self.started.pop(tag, []):
                copy.wait_send()


def block_kernel(
    last_hop,
    len_ref,
    x_ref,
    cot_ref,
    gains_ref,
    wq_ref,
    wo_ref,
    wu_ref,
    wd_ref,
    bias_ref,
    blk_ref,
    gin_ref,
    gq_ref,
    go_ref,
    gu_ref,
    gd_ref,
    gb_ref,
    stat_ref,
    mix_w,
    up_w,
    down_w,
    band_rows,
    x_halo,
    full_w,
    normed,
    wide_rows,
    resid,
    exp_low,
    kv_low,
    bands,
    mixed,
    normed_two,
    cot_low,
    act,
    dpre,
    dn_two,
    dnum,
    dden,
    bias_part,
    bias_recv_y,
    bias_recv_z,
    bias_hop,
    stats,
    stats_recv,
    recv_core,
    recv_one,
    recv_two,
    recv_z,
    ag_send,
    ag_recv,
    rs_send,
    rs_recv,
    halo_send,
    halo_recv,
    bias_send,
    bias_recv,
    stat_send,
    stat_recv,
):
    tokens, width = x_ref.shape
    window = x_halo.shape[0]
    rows = wu_ref.shape[0]
    chan = width // 4
    ffn = gin_ref
    sig, ratio, rden, expk, val = (
        wide_rows.at[pl.ds(i * tokens, tokens)] for i in range(5)
    )
    group = lax.axis_index("dph")
    inner = lax.axis_index("dpl")
    mp = lax.axis_index("mp")
    z, y = group // YN, group % YN
    x, c = mp // 2, mp % 2

    def device(zs, ys, xs, cs):
        return (zs * YN + ys, inner, xs * 2 + cs)

    def z_at(k):
        return (z + k) % ZN

    core_peer = device(z, y, x, 1 - c)
    x_peer = device(z, y, 1 - x, c)
    y_peer = device(z, 1 - y, x, c)
    diag_peer = device(z, y, 1 - x, 1 - c)
    z_peers = [device(z_at(k), y, x, c) for k in range(1, ZN)]

    out = Copies()

    half = 2 * chan
    gather_pieces = [
        (mix_w, 0, half, True),
        (mix_w, half, half, False),
        (None, 0, 0, True),
        (up_w, 0, up_w.shape[2], True),
        (down_w, 0, down_w.shape[2], False),
    ]

    def place(piece, zs, ys, xs, cs):
        buf, start, size, _ = gather_pieces[piece]
        if buf is None:
            return band_rows.at[(zs * YN + ys) * 4 + xs * 2 + cs]
        at = pl.multiple_of((zs * YN + ys) * rows, 32)
        return buf.at[xs * 2 + cs, pl.ds(at, rows), pl.ds(start, size)]

    def ag(piece, loc, peer, slot):
        ref = place(piece, *loc)
        return pltpu.make_async_remote_copy(
            src_ref=ref,
            dst_ref=ref,
            send_sem=ag_send.at[piece, slot],
            recv_sem=ag_recv.at[piece, slot],
            device_id=peer,
            device_id_type=MESH,
        )

    own = (z, y, x, c)

    def behind(k):
        return (z + ZN - k) % ZN

    def spot(kind, k):
        return (behind(k), y if kind in (0, 2) else 1 - y, x if kind in (0, 1) else 1 - x, c)

    def forward(piece, kind, k, peer, slot):
        tag = "mix" if piece < 3 else ("near" if kind < 2 else "far")
        out.go(ag(piece, spot(kind, k), peer, slot), tag)

    def to_core(piece, kind, k):
        forward(piece, kind, k, core_peer, 15 + kind * 4 + k)

    def arrived(piece, slot):
        ag(piece, own, core_peer, slot).wait_recv()

    def turns_y(piece):
        return gather_pieces[piece][3]

    def start_z(piece):
        for k in (1, 3, 2):
            forward(piece, 0, 0, z_peers[k - 1], k - 1)

    def start_side(piece):
        forward(piece, 0, 0, y_peer, 3)
        forward(piece, 0, 0, x_peer, 7)
        to_core(piece, 0, 0)

    def gather_z(piece, k):
        arrived(piece, k - 1)
        forward(piece, 0, k, y_peer, 3 + k)
        forward(piece, 0, k, x_peer, 7 + k)
        to_core(piece, 0, k)

    def gather_turn(piece, k):
        if turns_y(piece):
            arrived(piece, 3 + k)
            forward(piece, 1, k, x_peer, 11 + k)
            to_core(piece, 1, k)
        else:
            arrived(piece, 7 + k)
            forward(piece, 2, k, y_peer, 11 + k)
            to_core(piece, 2, k)

    def gather_side(piece, k):
        if turns_y(piece):
            arrived(piece, 7 + k)
            to_core(piece, 2, k)
        else:
            arrived(piece, 3 + k)
            to_core(piece, 1, k)

    def gather_last(piece, k):
        arrived(piece, 11 + k)
        to_core(piece, 3, k)

    def gather_core(piece, kinds=(0, 1, 2, 3)):
        for kind in kinds:
            for k in range(ZN):
                arrived(piece, 15 + kind * 4 + k)

    home = pl.ds(pl.multiple_of(group * rows, 32), rows)
    mix_w[mp, home, :] = jnp.concatenate(
        [wq_ref[0], wq_ref[1], wq_ref[2], wo_ref[...].T], axis=1
    ).astype(BF)
    flip = (
        lax.broadcasted_iota(jnp.int32, (window, window), 0)
        + lax.broadcasted_iota(jnp.int32, (window, window), 1)
        == window - 1
    ).astype(F32)
    band_rows[group * 4 + mp] = dot_nn(
        jnp.exp(bias_ref[...]).astype(BF), flip.astype(BF)
    ).astype(BF)

    barrier = pltpu.get_barrier_semaphore()
    friends = [core_peer, x_peer, y_peer, diag_peer] + z_peers
    for friend in friends:
        pl.semaphore_signal(barrier, inc=1, device_id=friend, device_id_type=MESH)
    here = group * 4 + mp
    moves = here != mp * GROUPS + group
    if last_hop:

        @pl.when(moves)
        def _():
            pl.semaphore_signal(
                barrier,
                inc=1,
                device_id=(here % GROUPS, inner, here // GROUPS),
                device_id_type=MESH,
            )
            pl.semaphore_wait(barrier, len(friends) + 1)

        @pl.when(jnp.logical_not(moves))
        def _():
            pl.semaphore_wait(barrier, len(friends))

    else:
        pl.semaphore_wait(barrier, len(friends))

    halo_copy = pltpu.make_async_remote_copy(
        src_ref=x_ref.at[pl.ds(tokens - window, window)],
        dst_ref=x_halo,
        send_sem=halo_send.at[0],
        recv_sem=halo_recv.at[0],
        device_id=(group, inner, (mp + 1) % 4),
        device_id_type=MESH,
    )

    stats[0] = jnp.zeros(stats.shape[1:], F32)

    def add_stat(row, value):
        stats[0, row : row + 1, :] += jnp.sum(value, axis=0, keepdims=True)

    def rms(value):
        return lax.rsqrt(jnp.mean(value * value, axis=-1, keepdims=True) + EPS)

    def mask_at(at):
        spots = lax.broadcasted_iota(jnp.int32, (CHUNK, width), 0) + (at + mp * tokens)
        return (spots < len_ref[0]).astype(F32)

    def norm_own(at):
        part = pl.ds(at, CHUNK)
        xf = x_ref[part].astype(F32)
        normed[pl.ds(at + window, CHUNK)] = (xf * rms(xf) * gains_ref[0:1]).astype(BF)
        mask = mask_at(at)
        add_stat(2, mask * xf * xf)
        add_stat(5, mask)
        cot_low[part] = (cot_ref[part].astype(F32) * mask).astype(BF)

    def norm_halo(at):
        part = pl.ds(at, CHUNK)
        xf = x_halo[part].astype(F32)
        normed[part] = (xf * rms(xf) * gains_ref[0:1]).astype(BF)

    def repack(at):
        part = pl.ds(at, rows)
        for kind in range(4):
            full_w[kind, part] = jnp.concatenate(
                [mix_w[m, part, kind * chan : (kind + 1) * chan] for m in range(4)], axis=1
            )

    def project_halo(at):
        part = pl.ds(at, CHUNK)
        a = normed[part]
        ek = jnp.where(mp > 0, jnp.exp(dot_nn(a, full_w[1])), 0.0)
        exp_low[part] = ek.astype(BF)
        kv_low[part] = (ek * dot_nn(a, full_w[2])).astype(BF)

    def project_own(at):
        part = pl.ds(at, CHUNK)
        shifted = pl.ds(at + window, CHUNK)
        a = normed[shifted]
        ek = jnp.exp(dot_nn(a, full_w[1]))
        v = dot_nn(a, full_w[2])
        exp_low[shifted] = ek.astype(BF)
        kv_low[shifted] = (ek * v).astype(BF)
        expk[part] = ek
        val[part] = v
        sig[part] = jax.nn.sigmoid(dot_nn(a, full_w[0]))

    def build_bands():
        for i in range(3):
            raw = band_rows[pl.ds(mp * 8 + i * 4, 4)].reshape(window, window).astype(F32)
            wide = jnp.concatenate([raw, jnp.zeros_like(raw)], axis=1)
            bands[i] = pltpu.roll(wide, 1, 1, stride=1, stride_axis=0).astype(BF)

    def mix_rows(i):
        part = slice(i * window, (i + 1) * window)
        near = slice(i * window, (i + 2) * window)
        num = dot_nn(bands[i], kv_low[near])
        den = dot_nn(bands[i], exp_low[near])
        ratio[part] = num / den
        rden[part] = 1.0 / den

    def attend(at):
        part = pl.ds(at, CHUNK)
        low = (sig[part] * ratio[part]).astype(BF)
        mixed[part] = low
        attn = dot_nt(low, full_w[3])
        add_stat(3, mask_at(at) * attn * attn)
        total = x_ref[part].astype(F32) + attn
        resid[part] = total
        normed_two[part] = (total * rms(total) * gains_ref[1:2]).astype(BF)

    def hidden_rows(m, first):
        def body(at):
            part = pl.ds(at, CHUNK)
            p = dot_nn(normed_two[part], up_w[m])
            da = dot_nn(cot_low[part], down_w[m])
            t = jnp.tanh(GELU_C * (p + GELU_A * (p * p * p)))
            low = (0.5 * p * (1.0 + t)).astype(BF)
            slope = 0.5 * (1.0 + t) + 0.5 * p * (1.0 - t * t) * (
                GELU_C * (1.0 + 3.0 * GELU_A * (p * p))
            )
            dlow = (da * slope).astype(BF)
            act[part] = low
            dpre[part] = dlow
            f = dot_nt(low, down_w[m])
            d = dot_nt(dlow, up_w[m])
            if first:
                ffn[part] = f
                dn_two[part] = d
            else:
                ffn[part] += f
                dn_two[part] += d

        return body

    def weight_grad(result, left, right):
        for at in range(0, result.shape[1], 256):
            part = slice(at, at + 256)
            result[:, part] = dot_tn(left[...], right[:, part]).astype(result.dtype)

    def close_hidden(at):
        part = pl.ds(at, CHUNK)
        mask = mask_at(at)
        f = ffn[part]
        res = resid[part]
        add_stat(4, mask * f * f)
        blk_ref[part] = (res + f).astype(BF)
        d = dn_two[part]
        r = rms(res)
        u = gains_ref[1:2] * d
        grad = (
            cot_ref[part].astype(F32) * mask
            + r * u
            - res * (r * r * r) * jnp.mean(u * res, axis=-1, keepdims=True)
        )
        add_stat(1, d * res * r)
        ffn[part] = grad
        act[part] = grad.astype(BF)

    def back_attend(at):
        part = pl.ds(at, CHUNK)
        dm = dot_nn(act[part], full_w[3])
        sg = sig[part]
        rt = ratio[part]
        scaled = dm * sg
        normed_two[part] = (scaled * rt * (1.0 - sg)).astype(BF)
        dn = scaled * rden[part]
        dnum[part] = dn.astype(BF)
        dden[part] = (-dn * rt).astype(BF)

    def halo_back(slot, buf):
        return pltpu.make_async_remote_copy(
            src_ref=buf.at[pl.ds(0, window)],
            dst_ref=buf.at[pl.ds(tokens, window)],
            send_sem=halo_send.at[slot],
            recv_sem=halo_recv.at[slot],
            device_id=(group, inner, (mp + 3) % 4),
            device_id_type=MESH,
        )

    def band_grad(i):
        part = slice(i * window, (i + 1) * window)
        near = slice(i * window, (i + 2) * window)
        dn_two[part, 0 : 2 * window] = dot_nt(dnum[part], kv_low[near]) + dot_nt(dden[part], exp_low[near])

    def unskew(j):
        wide = 2 * window
        count = bias_part.shape[1]
        line = lax.broadcasted_iota(jnp.int32, (count, wide), 0)
        v = dn_two[j * count : (j + 1) * count, 0:wide]
        v = pltpu.roll(v, wide - 1 - (j * count) % window, 1)
        bit = 1
        while bit < count:
            v = jnp.where((line & bit) != 0, pltpu.roll(v, wide - bit, 1), v)
            bit *= 2
        bias_part[j] = v[:, 0:window].astype(BF)

    def back_keys(j):
        here = slice(j * window, (j + 1) * window)
        then = slice((j + 1) * window, (j + 2) * window)
        right = bands[j, :, window:]
        left = bands[j + 1, :, :window]
        dkv = dot_tn(right, dnum[here]) + dot_tn(left, dnum[then])
        de = dot_tn(right, dden[here]) + dot_tn(left, dden[then])
        ek = expk[here]
        cot_low[here] = (dkv * ek).astype(BF)
        dpre[here] = ((de + dkv * val[here]) * ek).astype(BF)

    def back_input(at):
        part = pl.ds(at, CHUNK)
        d = (
            dot_nt(normed_two[part], full_w[0])
            + dot_nt(dpre[part], full_w[1])
            + dot_nt(cot_low[part], full_w[2])
        )
        xf = x_ref[part].astype(F32)
        r = rms(xf)
        u = gains_ref[0:1] * d
        gin_ref[part] = (
            ffn[part] + r * u - xf * (r * r * r) * jnp.mean(u * xf, axis=-1, keepdims=True)
        )
        add_stat(0, d * xf * r)

    def mix_grad(kind):
        grad = (normed_two, dpre, cot_low)[kind]
        result = wide_rows.at[pl.ds(kind * GROUPS * rows, GROUPS * rows)]
        weight_grad(result, normed.at[pl.ds(window, tokens)], grad)

    def unpack(kinds):
        def body(at):
            part = pl.ds(at, rows)
            for m in range(4):
                mine = slice(m * chan, (m + 1) * chan)
                pair = [
                    full_w[3, part, mine]
                    if kind == 3
                    else wide_rows[pl.ds(at + kind * GROUPS * rows, rows), mine].astype(BF)
                    for kind in kinds
                ]
                span = slice(kinds[0] * chan, (kinds[-1] + 1) * chan)
                mix_w[m, part, span] = jnp.concatenate(pair, axis=1)

        return body

    scatter_pieces = [
        (mix_w, 0, half, True, None, 0),
        (mix_w, half, half, False, None, half),
        (up_w, 0, up_w.shape[2], False, gu_ref, 2 * half),
        (down_w, 0, down_w.shape[2], False, gd_ref, 2 * half + up_w.shape[2]),
    ]

    def rs(piece, src, dst, peer, slot):
        return pltpu.make_async_remote_copy(
            src_ref=src,
            dst_ref=dst,
            send_sem=rs_send.at[piece, slot],
            recv_sem=rs_recv.at[piece, slot],
            device_id=peer,
            device_id_type=MESH,
        )

    def x_of(far):
        return 1 - x if far else x

    def block(piece, xs, zs, ys):
        buf, start, size = scatter_pieces[piece][:3]
        at = pl.multiple_of((zs * YN + ys) * rows, 32)
        return buf.at[xs * 2 + c, pl.ds(at, rows), pl.ds(start, size)]

    def lanes(piece):
        return pl.ds(scatter_pieces[piece][5], scatter_pieces[piece][2])

    def core_copy(p, far):
        buf, start, size = scatter_pieces[p][:3]
        src = buf.at[x_of(far) * 2 + 1 - c, :, pl.ds(start, size)]
        return rs(p, src, recv_core.at[far, :, lanes(p)], core_peer, far)

    def core_send(p, far):
        out.go(core_copy(p, far))

    def core_sum(p, far):
        buf, start, size = scatter_pieces[p][:3]
        core_copy(p, far).wait_recv()

        def body(at):
            part = pl.ds(at, rows)
            buf[x_of(far) * 2 + c, part, pl.ds(start, size)] += recv_core[far, part, lanes(p)]

        loop_rows(GROUPS * rows, rows, body)

    def y_copy(p, far, k):
        src = block(p, x_of(far), behind(k), 1 - y)
        return rs(p, src, recv_one.at[far * ZN + k, :, lanes(p)], y_peer, 2 + far * ZN + k)

    def y_send(p, far):
        for k in (1, 2, 3, 0):
            out.go(y_copy(p, far, k))

    def y_take(p, far, k):
        y_copy(p, far, k).wait_recv()
        spot_ref = block(p, x_of(far), behind(k), y)
        spot_ref[...] += recv_one[far * ZN + k, :, lanes(p)]

    def x_copy(p, k):
        src = block(p, 1 - x, behind(k), y)
        return rs(p, src, recv_two.at[k, :, lanes(p)], x_peer, 10 + k)

    def x_take(p, k):
        x_copy(p, k).wait_recv()
        spot_ref = block(p, x, behind(k), y)
        spot_ref[...] += recv_two[k, :, lanes(p)]

    def z_copy(p, k):
        src = block(p, x, behind(k), y)
        return rs(p, src, recv_z.at[k - 1, :, lanes(p)], z_peers[ZN - 1 - k], 13 + k)

    def z_take(p):
        total = block(p, x, z, y)[...].astype(F32)
        for k in range(1, ZN):
            z_copy(p, k).wait_recv()
            total = total + recv_z[k - 1, :, lanes(p)].astype(F32)
        if p == 0:
            gq_ref[0] = total[:, :chan]
            gq_ref[1] = total[:, chan:]
        elif p == 1:
            gq_ref[2] = total[:, :chan]
            go_ref[...] = total[:, chan:].T
        else:
            scatter_pieces[p][4][...] = total

    def y_turn(p, k):
        y_take(p, 1, k)
        out.go(x_copy(p, k))

    def x_end(p, k):
        x_take(p, k)
        if k:
            out.go(z_copy(p, k))

    def wide_copy(p, k, ys):
        src = block(p, 1 - x, behind(k), ys)
        slot = k if ys is y else ZN + k
        return rs(p, src, recv_one.at[slot, :, lanes(p)], x_peer, 2 + slot)

    def wide_send(p):
        for k in (1, 2, 3, 0):
            out.go(wide_copy(p, k, other_y))
        for k in (1, 2, 3, 0):
            out.go(wide_copy(p, k, y))

    def wide_take(p, k, ys):
        wide_copy(p, k, ys).wait_recv()
        slot = k if ys is y else ZN + k
        spot_ref = block(p, x, behind(k), ys)
        spot_ref[...] += recv_one[slot, :, lanes(p)]

    def late_copy(p, k):
        src = block(p, x, behind(k), 1 - y)
        return rs(p, src, recv_two.at[k, :, lanes(p)], y_peer, 10 + k)

    def wide_turn(p, k):
        wide_take(p, k, other_y)
        out.go(late_copy(p, k))

    def late_end(p, k):
        wide_take(p, k, y)
        late_copy(p, k).wait_recv()
        spot_ref = block(p, x, behind(k), y)
        spot_ref[...] += recv_two[k, :, lanes(p)]
        if k:
            out.go(z_copy(p, k))

    other_y = 1 - y

    def bias_copy(src, dst, peer, slot):
        return pltpu.make_async_remote_copy(
            src_ref=src,
            dst_ref=dst,
            send_sem=bias_send.at[slot],
            recv_sem=bias_recv.at[slot],
            device_id=peer,
            device_id_type=MESH,
        )

    def bias_y(k):
        return bias_copy(
            bias_part.at[behind(k) * YN + 1 - y], bias_recv_y.at[k], y_peer, k
        )

    def bias_z(k):
        return bias_copy(
            bias_part.at[behind(k) * YN + y], bias_recv_z.at[k - 1], z_peers[ZN - 1 - k], 3 + k
        )

    def bias_turn():
        for k in (1, 2, 3, 0):
            bias_y(k).wait_recv()
            bias_part[behind(k) * YN + y] += bias_recv_y[k]
            if k:
                out.go(bias_z(k))

    def close_bias():
        total = bias_part[z * YN + y].astype(F32)
        for k in range(1, ZN):
            bias_z(k).wait_recv()
            total = total + bias_recv_z[k - 1].astype(F32)
        bias_hop[0] = jnp.dot(
            total, flip, precision=lax.Precision.HIGHEST, preferred_element_type=F32
        )

    def hop_copy():
        owner = mp * GROUPS + group
        return pltpu.make_async_remote_copy(
            src_ref=bias_hop.at[0],
            dst_ref=bias_hop.at[1],
            send_sem=bias_send.at[7],
            recv_sem=bias_recv.at[7],
            device_id=(owner // 4, inner, owner % 4),
            device_id_type=MESH,
        )

    def reduce_stats():
        def copy(step, slot, peer):
            return pltpu.make_async_remote_copy(
                src_ref=stats.at[step],
                dst_ref=stats_recv.at[slot],
                send_sem=stat_send.at[slot],
                recv_sem=stat_recv.at[slot],
                device_id=peer,
                device_id_type=MESH,
            )

        return copy

    def stats_step(step):
        copy = reduce_stats()
        peer = (core_peer, x_peer, y_peer)[step]
        copy(step, step, peer).wait_recv()
        stats[step + 1] = stats[step] + stats_recv[step]

    def stats_send(step):
        copy = reduce_stats()
        if step < 3:
            out.go(copy(step, step, (core_peer, x_peer, y_peer)[step]))
        else:
            for k in range(1, ZN):
                out.go(copy(3, 2 + k, z_peers[k - 1]))

    def stats_end():
        copy = reduce_stats()
        total = stats[3]
        for k in range(1, ZN):
            copy(3, 2 + k, z_peers[k - 1]).wait_recv()
            total = total + stats_recv[2 + k]
        stat_ref[...] = total

    steps = (0, 1, 3, 2)
    early, late = (0, 1, 2), (3, 4)

    @pl.when(mp < 3)
    def _():
        halo_copy.start()

    band_rows[4 * GROUPS : 4 * GROUPS + 4] = jnp.zeros((4, *bias_ref.shape), BF)
    for p in early:
        start_z(p)
    for p in early:
        start_side(p)
    up_w[mp, home, :] = wu_ref[...].astype(BF)
    down_w[mp, home, :] = wd_ref[...].astype(BF)
    loop_rows(tokens, CHUNK, norm_own)
    for k in steps[1:]:
        for p in early:
            gather_z(p, k)
    for p in late:
        start_z(p)
    for step in (gather_turn, gather_side):
        for k in steps:
            for p in early:
                step(p, k)
    for p in late:
        start_side(p)
    for k in steps:
        for p in early:
            gather_last(p, k)

    @pl.when(mp > 0)
    def _():
        halo_copy.wait_recv()

    @pl.when(mp == 0)
    def _():
        x_halo[...] = jnp.zeros_like(x_halo)

    loop_rows(window, CHUNK, norm_halo)
    for k in steps[1:]:
        for p in late:
            gather_z(p, k)
    for p in early:
        gather_core(p)
    tasks = [
        functools.partial(step, p, k)
        for step in (gather_turn, gather_side, gather_last)
        for k in steps
        for p in late
    ]

    def beside(count):
        for _ in range(min(count, len(tasks))):
            tasks.pop(0)()

    loop_rows(GROUPS * rows, rows, repack)
    build_bands()
    for at in range(0, window, CHUNK):
        project_halo(at)
        beside(1)
    for at in range(0, tokens, CHUNK):
        project_own(at)
        beside(1)
    for i in range(2):
        mix_rows(i)
        beside(2)
    for at in range(0, tokens, CHUNK):
        attend(at)
        beside(2)

    def slab(r):
        return x_of(r // 2) * 2 + (1 - c if r % 2 else c)

    beside(len(tasks) - 2 * ZN)
    for r in (1, 0, 3, 2):
        if r % 2:
            if r == 3:
                beside(len(tasks))
            for p in late:
                gather_core(p, (r - 1, r))
        loop_rows(tokens, CHUNK, hidden_rows(slab(r), r == 1))
        beside(2)
        if r % 2 == 0:
            out.drain("far" if r else "near")
        weight_grad(up_w.at[slab(r)], normed_two, dpre)
        if r % 2:
            core_send(2, r // 2)
        else:
            core_sum(2, r // 2)
            y_send(2, r // 2)
        beside(2)
        weight_grad(down_w.at[slab(r)], cot_low, act)
        if r % 2:
            core_send(3, r // 2)
        else:
            core_sum(3, r // 2)
            y_send(3, r // 2)
    for k in steps:
        y_take(2, 0, k)
        y_take(3, 0, k)
    loop_rows(tokens, CHUNK, close_hidden)
    loop_rows(tokens, CHUNK, back_attend)

    backs = [halo_back(1, dnum), halo_back(2, dden)]

    @pl.when(mp > 0)
    def _():
        for item in backs:
            item.start()

    weight_grad(full_w.at[3], act, mixed)
    mix_grad(0)
    for k in (1, 2, 3, 0):
        y_turn(2, k)
    for i in range(2):
        band_grad(i)
    for j in range(GROUPS):
        unskew(j)
    for k in (1, 2, 3, 0):
        out.go(bias_y(k))

    @pl.when(mp < 3)
    def _():
        for item in backs:
            item.wait_recv()

    @pl.when(mp == 3)
    def _():
        dnum[pl.ds(tokens, window)] = jnp.zeros((window, width), BF)
        dden[pl.ds(tokens, window)] = jnp.zeros((window, width), BF)

    for j in range(2):
        back_keys(j)
    mix_grad(1)
    out.drain("mix")
    loop_rows(GROUPS * rows, rows, unpack((0, 1)))
    core_send(0, 1)
    core_send(0, 0)
    mix_grad(2)
    loop_rows(GROUPS * rows, rows, unpack((2, 3)))
    core_send(1, 1)
    core_send(1, 0)
    for k in (1, 2, 3, 0):
        y_turn(3, k)
    core_sum(0, 1)
    wide_send(0)
    core_sum(1, 1)
    y_send(1, 1)
    core_sum(1, 0)
    y_send(1, 0)
    core_sum(0, 0)
    bias_turn()
    for at, k in zip(range(0, tokens, CHUNK), (1, 2, 3, 0), strict=True):
        back_input(at)
        x_end(2, k)
    stats_send(0)
    close_bias()
    if last_hop:

        @pl.when(moves)
        def _():
            hop_copy().start()

    for k in (1, 2, 3, 0):
        x_end(3, k)
    stats_step(0)
    stats_send(1)
    for k in (1, 2, 3, 0):
        wide_turn(0, k)
        y_turn(1, k)
    stats_step(1)
    stats_send(2)
    z_take(2)
    for k in (1, 2, 3, 0):
        y_take(1, 0, k)
        late_end(0, k)
        x_end(1, k)
    stats_step(2)
    stats_send(3)
    z_take(3)
    if last_hop:

        @pl.when(moves)
        def _():
            hop_copy().wait_recv()
            gb_ref[...] = bias_hop[1]

        @pl.when(jnp.logical_not(moves))
        def _():
            gb_ref[...] = bias_hop[0]

    else:
        gb_ref[...] = bias_hop[0]
    stats_end()
    z_take(0)
    z_take(1)

    @pl.when(mp < 3)
    def _():
        halo_copy.wait_send()

    @pl.when(mp > 0)
    def _():
        for item in backs:
            item.wait_send()

    if last_hop:

        @pl.when(moves)
        def _():
            hop_copy().wait_send()

    out.drain()


def run_block(lengths, x, cot, gains, wq, wo, wu, wd, bias, last_hop):
    tokens, width = x.shape
    window = bias.shape[1]
    rows = wu.shape[0]
    full = rows * GROUPS
    mix_width = 4 * wq.shape[2]
    hidden = wu.shape[1]
    lanes = mix_width + 2 * hidden
    vmem = pl.BlockSpec(memory_space=pltpu.VMEM)

    def shape(*dims, kind=F32):
        return jax.ShapeDtypeStruct(dims, kind)

    def buf(*dims):
        return pltpu.VMEM(dims, F32)

    def low(*dims):
        return pltpu.VMEM(dims, BF)

    dma = pltpu.SemaphoreType.DMA
    return pl.pallas_call(
        functools.partial(block_kernel, last_hop),
        out_shape=(
            shape(tokens, width, kind=BF),
            shape(tokens, width),
            shape(*wq.shape),
            shape(*wo.shape),
            shape(*wu.shape),
            shape(*wd.shape),
            shape(*bias.shape),
            shape(8, width),
        ),
        in_specs=[pl.BlockSpec(memory_space=pltpu.SMEM)] + [vmem] * 8,
        out_specs=(vmem,) * 8,
        scratch_shapes=[
            low(4, full, mix_width),
            low(4, full, hidden),
            low(4, full, hidden),
            low(4 * GROUPS + 4, *bias.shape),
            low(window, width),
            low(4, full, width),
            low(window + tokens, width),
            buf(5 * tokens, width),
            buf(tokens, width),
            low(window + tokens, width),
            low(window + tokens, width),
            low(3, window, 2 * window),
            low(tokens, width),
            low(tokens, width),
            low(tokens, width),
            low(tokens, hidden),
            low(tokens, hidden),
            buf(tokens, width),
            low(tokens + window, width),
            low(tokens + window, width),
            low(GROUPS, *bias.shape),
            low(ZN, *bias.shape),
            low(ZN - 1, *bias.shape),
            buf(2, *bias.shape),
            buf(4, 8, width),
            buf(6, 8, width),
            low(2, full, lanes),
            low(GROUPS, rows, lanes),
            low(ZN, rows, lanes),
            low(ZN - 1, rows, lanes),
            dma((5, 31)),
            dma((5, 31)),
            dma((4, 17)),
            dma((4, 17)),
            dma((3,)),
            dma((3,)),
            dma((8,)),
            dma((8,)),
            dma((6,)),
            dma((6,)),
        ],
        compiler_params=pltpu.CompilerParams(
            collective_id=0, has_side_effects=True, vmem_limit_bytes=63 * 1024 * 1024
        ),
    )(lengths, x, cot, gains, wq, wo, wu, wd, bias)


MESH = pl.DeviceIdType.MESH


def adam_kernel(scale, *refs):
    grads, refs = refs[:6], refs[6:]
    params, refs = refs[:6], refs[6:]
    firsts, refs = refs[:6], refs[6:]
    seconds, refs = refs[:6], refs[6:]
    out_grads, out_firsts, out_seconds, out_updates = (
        refs[6 * i : 6 * i + 6] for i in range(4)
    )
    rms_ref = refs[24]
    one = 1.0 / (1.0 - BETA_ONE**ADAM_STEP)
    two = 1.0 / (1.0 - BETA_TWO**ADAM_STEP)
    for i in range(6):
        if i == 4:
            grad = grads[4][...] * jnp.exp(params[4][...])
        elif i == 5:
            grad = grads[5][0:2]
        else:
            grad = grads[i][...]
        grad = grad * scale
        first = BETA_ONE * firsts[i][...] + (1.0 - BETA_ONE) * grad
        second = BETA_TWO * seconds[i][...] + (1.0 - BETA_TWO) * (grad * grad)
        step = (first * one) / (jnp.sqrt(second * two) + ADAM_EPS)
        if i < 4:
            step = step + WEIGHT_DECAY * params[i][...]
        out_grads[i][...] = grad
        out_firsts[i][...] = first
        out_seconds[i][...] = second
        out_updates[i][...] = -LEARN_RATE * step
    sums = jnp.sum(grads[5][...], axis=1, keepdims=True)
    rms_ref[...] = jnp.sqrt(sums[2:5] / sums[5:6])


def run_adam(scale, grads, params, firsts, seconds):
    vmem = pl.BlockSpec(memory_space=pltpu.VMEM)
    kinds = [jax.ShapeDtypeStruct(param.shape, F32) for param in params]
    return pl.pallas_call(
        functools.partial(adam_kernel, scale),
        out_shape=(*(kinds * 4), jax.ShapeDtypeStruct((3, 1), F32)),
        in_specs=[vmem] * 24,
        out_specs=(vmem,) * 25,
        compiler_params=pltpu.CompilerParams(vmem_limit_bytes=62 * 1024 * 1024),
    )(*grads, *params, *firsts, *seconds)


def stored(items):
    qkv, mix, up, down, bias, gains = items
    return [qkv.transpose(1, 0, 2), mix, up, down.T, bias, gains]


def shards(inner, block_input, out_cotangent, lengths, *rest):
    params, firsts, seconds = (stored(rest[6 * i : 6 * i + 6]) for i in range(3))
    held = params
    if inner > 1:
        axes = (1, 1, 0, 0)
        held = [
            lax.all_gather(item.astype(BF), "dpl", axis=axis, tiled=True).astype(F32)
            for item, axis in zip(params[:4], axes, strict=True)
        ]
        count = params[4].shape[0]
        every = lax.all_gather(params[4], ("dpl", "mp"), axis=0, tiled=True)
        at = lax.axis_index("mp") * inner * count
        held += [lax.dynamic_slice_in_dim(every, at, inner * count, 0), params[5]]
    block_low, grad_input, *grads = run_block(
        lengths,
        block_input[0],
        out_cotangent[0],
        held[5],
        *held[:5],
        inner == 1,
    )
    if inner > 1:
        for i, axis in enumerate(axes):
            grads[i] = lax.psum_scatter(grads[i], "dpl", scatter_dimension=axis, tiled=True)
        grads[4], grads[5] = lax.psum((grads[4], grads[5]), "dpl")
        every = lax.all_gather(grads[4], ("mp", "dph"), axis=0, tiled=True)
        place = lax.axis_index(("dph", "dpl", "mp"))
        grads[4] = lax.dynamic_slice_in_dim(every, place * count, count, 0)
    scale = float(lax.axis_size("dph") * inner * LEN) ** (-0.5)
    *results, rms_stats = run_adam(scale, grads, params, firsts, seconds)
    outs = []
    for i in range(4):
        qkv, mix, up, down, bias, gains = results[6 * i : 6 * i + 6]
        outs += [qkv.transpose(1, 0, 2), mix, up, down.T, bias, gains]
    return (block_low[None], grad_input[None], *outs, rms_stats[:, 0])


def solution(mesh):
    inner = mesh.shape["dp"] // GROUPS
    fine = Mesh(
        mesh.devices.reshape(GROUPS, inner, mesh.shape["mp"]),
        ("dph", "dpl", "mp"),
    )
    dp = ("dph", "dpl")
    weights = (
        P(dp, None, "mp"),
        P("mp", dp),
        P(dp, "mp"),
        P("mp", dp),
        P((*dp, "mp"), None),
        P(),
    )
    acts = P(dp, "mp", None)
    return jax.shard_map(
        functools.partial(shards, inner),
        mesh=fine,
        in_specs=(acts, acts, P(dp), *weights, *weights, *weights),
        out_specs=(acts, acts, *weights, *weights, *weights, *weights, P()),
        check_vma=False,
    )
```

```python
import functools

import jax
import jax.numpy as jnp
from jax import lax
from jax.experimental import pallas as pl
from jax.experimental.pallas import tpu as pltpu
from jax.sharding import Mesh
from jax.sharding import PartitionSpec as P

LEN = 2048
ADAM_STEP = 10
EPS = 1e-06
BETA_ONE = 0.9
BETA_TWO = 0.99
LEARN_RATE = 0.03
WEIGHT_DECAY = 0.1
ADAM_EPS = 1e-08

F32 = jnp.float32
BF = jnp.bfloat16
ZN, YN = 4, 2
GROUPS = ZN * YN
CHUNK = 256
GELU_C = 0.7978845608028654
GELU_A = 0.044715


ROUTES = ((True, False), (False, False), (True, True), (True, False), (False, True))
LINE_SUMS = (False, True, False, True)
SCHEDULE = (
    ("send_x", 2), ("send_x", 0), ("send_z", 2), ("send_x", 1), ("send_y", 0), ("send_y", 1),
    ("send_z", 1), ("send_z", 0), ("send_y", 2), ("y", 0, 0), ("z", 2, 1), ("z", 2, 2),
    ("z", 1, 1), ("x", 1, 0), ("send_c", 1), ("z", 0, 1), ("y", 2, 0), ("norm",), ("z", 0, 2),
    ("send_z", 3), ("send_x", 3), ("z", 0, 3), ("z", 2, 3), ("x", 2, 0), ("x", 2, 1),
    ("z", 1, 2), ("x", 2, 2), ("y", 0, 1), ("send_y", 3), ("y", 0, 2), ("y", 0, 3), ("y", 1, 0),
    ("d", 2, 0), ("send_y", 4), ("d", 2, 1), ("d", 1, 0), ("y", 2, 1), ("y", 2, 2), ("z", 1, 3),
    ("z", 3, 1), ("z", 3, 2), ("x", 3, 0), ("send_c", 2), ("x", 0, 0), ("x", 0, 1), ("y", 1, 1),
    ("x", 1, 1), ("x", 1, 2), ("d", 0, 0), ("d", 0, 1), ("y", 2, 3), ("send_x", 4), ("x", 1, 3),
    ("halo",), ("z", 3, 3), ("d", 2, 2), ("d", 2, 3), ("send_z", 4), ("d", 1, 1), ("y", 1, 2),
    ("y", 1, 3), ("x", 0, 2), ("x", 0, 3), ("send_c", 0), ("z", 4, 1), ("x", 2, 3), ("bands",),
    ("d", 1, 2), ("d", 1, 3), ("y", 3, 0), ("y", 3, 1), ("send_c", 4), ("d", 0, 2), ("d", 0, 3),
    ("x", 4, 0), ("send_c", 3), ("y", 3, 2), ("y", 3, 3), ("z", 4, 2), ("z", 4, 3), ("repack",),
    ("y", 4, 0), ("d", 4, 0), ("proj", 0), ("proj", 1), ("y", 4, 1), ("y", 4, 2), ("halow",),
    ("mix", 0), ("mix", 1), ("att", 0), ("att", 1), ("y", 4, 3), ("x", 4, 1), ("d", 3, 0),
    ("x", 3, 1), ("x", 3, 2), ("x", 3, 3), ("h", 1, 0), ("d", 4, 1), ("h", 1, 1), ("g", 1, 0),
    ("cs", 2, 0), ("d", 3, 1), ("d", 4, 2), ("g", 1, 1), ("h", 0, 0), ("d", 3, 2), ("cs", 3, 0),
    ("h", 0, 1), ("g", 0, 0), ("d", 4, 3), ("sum", 2, 0), ("x", 4, 2), ("g", 0, 1), ("x", 4, 3),
    ("d", 3, 3), ("h", 3, 0), ("h", 3, 1), ("g", 3, 0), ("g", 3, 1), ("yt", 2, 1),
    ("sum", 3, 0), ("cs", 3, 1), ("h", 2, 0), ("h", 2, 1), ("g", 2, 0), ("g", 2, 1),
    ("sum", 3, 1), ("close", 0), ("close", 1), ("cs", 2, 1), ("ba", 0), ("sum", 2, 1),
    ("yt", 2, 2), ("yt", 2, 3), ("hb",), ("ba", 1), ("bg", 0), ("bg", 1), ("yt", 3, 1),
    ("xe", 3, 1), ("yt", 3, 2), ("yt", 3, 3), ("mg", 0), ("bk", 0), ("yt", 2, 0), ("gout",),
    ("unpack", 0), ("xe", 3, 2), ("cs", 0, 1), ("unsk",), ("by",), ("cs", 0, 0), ("sum", 0, 0),
    ("bk", 1), ("yx", 2, 1), ("mg", 1), ("mg", 2), ("unpack", 1), ("cs", 1, 0), ("xe", 3, 3),
    ("xe", 3, 0), ("sum", 0, 1), ("xe", 2, 1), ("yx", 3, 1), ("yx", 3, 2), ("yx", 2, 2),
    ("yx", 2, 3), ("yx", 2, 0), ("cs", 1, 1), ("bt",), ("sum", 1, 1), ("yx", 0, 1),
    ("yx", 3, 3), ("yt", 0, 1), ("sum", 1, 0), ("xe", 2, 2), ("bi", 0), ("bi", 1), ("ss", 0),
    ("sw", 0), ("xe", 2, 3), ("yx", 3, 0), ("yx", 0, 2), ("yx", 0, 3), ("ss", 1), ("yx", 1, 1),
    ("yx", 1, 2), ("yx", 1, 3), ("yx", 0, 0), ("xe", 0, 1), ("yt", 0, 2), ("yt", 0, 3),
    ("yt", 0, 0), ("xe", 0, 2), ("yt", 3, 0), ("yt", 1, 1), ("xe", 1, 1), ("sw", 1),
    ("yt", 1, 2), ("yt", 1, 3), ("xe", 1, 2), ("xe", 2, 0), ("xe", 1, 3), ("xe", 1, 0),
    ("xe", 0, 3), ("ss", 2), ("sw", 2), ("ss", 3), ("bc",), ("yx", 1, 0), ("yt", 1, 0),
    ("zt", 1), ("xe", 0, 0), ("hopw",), ("zt", 2), ("zt", 0), ("zt", 3), ("se",),
)


def dot_nn(a, b):
    return jnp.dot(a, b, preferred_element_type=F32)


def dot_nt(a, b):
    return lax.dot_general(a, b, (((1,), (1,)), ((), ())), preferred_element_type=F32)


def dot_tn(a, b):
    return lax.dot_general(a, b, (((0,), (0,)), ((), ())), preferred_element_type=F32)


def loop_rows(count, step, body, unroll=False):
    @pl.loop(0, count // step, unroll=unroll)
    def _(index):
        body(pl.multiple_of(index * step, step))


class Copies:
    def __init__(self):
        self.started = {}

    def go(self, copy, tag=None):
        copy.start()
        self.started.setdefault(tag, []).append(copy)

    def go_if(self, when, copy, tag=None):
        pl.when(when)(copy.start)
        self.started.setdefault(tag, []).append((when, copy))

    def drain(self, *tags):
        for tag in tags or list(self.started):
            for copy in self.started.pop(tag, []):
                if isinstance(copy, tuple):
                    pl.when(copy[0])(copy[1].wait_send)
                else:
                    copy.wait_send()


def block_kernel(
    last_hop,
    len_ref,
    x_ref,
    cot_ref,
    gains_ref,
    wq_ref,
    wo_ref,
    wu_ref,
    wd_ref,
    bias_ref,
    blk_ref,
    gin_ref,
    gq_ref,
    go_ref,
    gu_ref,
    gd_ref,
    gb_ref,
    stat_ref,
    mix_w,
    up_w,
    down_w,
    band_rows,
    x_halo,
    full_w,
    normed,
    wide_rows,
    resid,
    exp_low,
    kv_low,
    bands,
    mixed,
    normed_two,
    cot_low,
    act,
    dpre,
    dn_two,
    dnum,
    dden,
    bias_part,
    bias_recv_y,
    bias_recv_z,
    bias_hop,
    stats,
    stats_recv,
    recv_core,
    recv_one,
    recv_two,
    recv_z,
    ag_send,
    ag_recv,
    rs_send,
    rs_recv,
    halo_send,
    halo_recv,
    bias_send,
    bias_recv,
    stat_send,
    stat_recv,
):
    tokens, width = x_ref.shape
    window = x_halo.shape[0]
    rows = wu_ref.shape[0]
    chan = width // 4
    ffn = gin_ref
    sig, ratio, rden, expk, val = (
        wide_rows.at[pl.ds(i * tokens, tokens)] for i in range(5)
    )
    group = lax.axis_index("dph")
    inner = lax.axis_index("dpl")
    mp = lax.axis_index("mp")
    z, y = group // YN, group % YN
    x, c = mp // 2, mp % 2

    def device(zs, ys, xs, cs):
        return (zs * YN + ys, inner, xs * 2 + cs)

    def z_at(k):
        return (z + k) % ZN

    core_peer = device(z, y, x, 1 - c)
    x_peer = device(z, y, 1 - x, c)
    y_peer = device(z, 1 - y, x, c)
    diag_peer = device(z, y, 1 - x, 1 - c)
    z_peers = [device(z_at(k), y, x, c) for k in range(1, ZN)]

    out = Copies()

    half = 2 * chan
    gather_pieces = [
        (mix_w, 0, half),
        (mix_w, half, half),
        (None, 0, 0),
        (up_w, 0, up_w.shape[2]),
        (down_w, 0, down_w.shape[2]),
    ]

    def place(piece, zs, ys, xs, cs):
        buf, start, size = gather_pieces[piece]
        if buf is None:
            return band_rows.at[(zs * YN + ys) * 4 + xs * 2 + cs]
        at = pl.multiple_of((zs * YN + ys) * rows, 32)
        return buf.at[xs * 2 + cs, pl.ds(at, rows), pl.ds(start, size)]

    def ag(piece, loc, peer, slot):
        ref = place(piece, *loc)
        return pltpu.make_async_remote_copy(
            src_ref=ref,
            dst_ref=ref,
            send_sem=ag_send.at[piece, slot],
            recv_sem=ag_recv.at[piece, slot],
            device_id=peer,
            device_id_type=MESH,
        )

    own = (z, y, x, c)

    def along(i):
        edge = jnp.where(z == 0, i, ZN - 1 - i)
        inside = jnp.where(z == 1, (1, 0, 2, 3)[i], (2, 1, 3, 0)[i])
        return jnp.where((z == 0) | (z == ZN - 1), edge, inside)

    order = [along(i) for i in range(ZN)]

    def spot(kind, zs):
        return (zs, y if kind in (0, 2) else 1 - y, x if kind in (0, 1) else 1 - x, c)

    def tag_of(piece, kind):
        return "mix" if piece < 3 else ("near" if kind < 2 else "far")

    def forward(piece, kind, zs, peer, slot):
        out.go(ag(piece, spot(kind, zs), peer, slot), tag_of(piece, kind))

    def to_core(piece, kind, i):
        forward(piece, kind, order[i], core_peer, 16 + kind * 4 + order[i])

    def arrived(piece, slot):
        ag(piece, own, core_peer, slot).wait_recv()

    def turns_y(piece):
        return ROUTES[piece][0]

    def pass_z(piece, kind, zs, step, when):
        peer = device(jnp.clip(z + step, 0, ZN - 1), y, x, c)
        copy = ag(piece, spot(kind, zs), peer, kind * 4 + zs)
        out.go_if(when, copy, tag_of(piece, kind))

    def start_line(piece, kind):
        pass_z(piece, kind, z, 1, z < ZN - 1)
        pass_z(piece, kind, z, -1, z > 0)

    def pass_line(piece, kind, zs):
        up = zs < z
        pass_z(piece, kind, zs, jnp.where(up, 1, -1), jnp.where(up, z < ZN - 1, z > 0))

    def start_z(piece):
        start_line(piece, 0)

    def start_y(piece):
        forward(piece, 0, z, y_peer, 4 + z)

    def start_x(piece):
        forward(piece, 0, z, x_peer, 8 + z)

    def start_core(piece):
        to_core(piece, 0, 0)

    def gather_z(piece, i):
        zs = order[i]
        arrived(piece, zs)
        pass_line(piece, 0, zs)
        forward(piece, 0, zs, y_peer, 4 + zs)
        forward(piece, 0, zs, x_peer, 8 + zs)
        to_core(piece, 0, i)

    def turns(piece, i):
        return not ROUTES[piece][1] or i == 0

    def gather_y(piece, i):
        zs = order[i]
        arrived(piece, 4 + zs)
        if turns_y(piece) and turns(piece, i):
            forward(piece, 1, zs, x_peer, 12 + zs)
        to_core(piece, 1, i)

    def gather_x(piece, i):
        zs = order[i]
        arrived(piece, 8 + zs)
        if not turns_y(piece) and turns(piece, i):
            forward(piece, 2, zs, y_peer, 12 + zs)
        to_core(piece, 2, i)

    def gather_last(piece, i):
        zs = order[i]
        arrived(piece, 12 + zs)
        if ROUTES[piece][1]:
            if i:
                pass_line(piece, 3, zs)
            else:
                start_line(piece, 3)
        to_core(piece, 3, i)

    def gather_core(piece, kinds=(0, 1, 2, 3)):
        for kind in kinds:
            for i in range(ZN):
                arrived(piece, 16 + kind * 4 + order[i])

    home = pl.ds(pl.multiple_of(group * rows, 32), rows)
    mix_w[mp, home, :] = jnp.concatenate(
        [wq_ref[0], wo_ref[...].T, wq_ref[1], wq_ref[2]], axis=1
    ).astype(BF)
    flip = (
        lax.broadcasted_iota(jnp.int32, (window, window), 0)
        + lax.broadcasted_iota(jnp.int32, (window, window), 1)
        == window - 1
    ).astype(F32)
    band_rows[group * 4 + mp] = dot_nn(
        jnp.exp(bias_ref[...]).astype(BF), flip.astype(BF)
    ).astype(BF)

    barrier = pltpu.get_barrier_semaphore()
    friends = [core_peer, x_peer, y_peer, diag_peer] + z_peers
    for friend in friends:
        pl.semaphore_signal(barrier, inc=1, device_id=friend, device_id_type=MESH)
    here = group * 4 + mp
    moves = here != mp * GROUPS + group
    if last_hop:

        @pl.when(moves)
        def _():
            pl.semaphore_signal(
                barrier,
                inc=1,
                device_id=(here % GROUPS, inner, here // GROUPS),
                device_id_type=MESH,
            )
            pl.semaphore_wait(barrier, len(friends) + 1)

        @pl.when(jnp.logical_not(moves))
        def _():
            pl.semaphore_wait(barrier, len(friends))

    else:
        pl.semaphore_wait(barrier, len(friends))

    halo_copy = pltpu.make_async_remote_copy(
        src_ref=x_ref.at[pl.ds(tokens - window, window)],
        dst_ref=x_halo,
        send_sem=halo_send.at[0],
        recv_sem=halo_recv.at[0],
        device_id=(group, inner, (mp + 1) % 4),
        device_id_type=MESH,
    )

    stats[0] = jnp.zeros(stats.shape[1:], F32)

    def add_stat(row, value):
        stats[0, row : row + 1, :] += jnp.sum(value, axis=0, keepdims=True)

    def rms(value):
        return lax.rsqrt(jnp.mean(value * value, axis=-1, keepdims=True) + EPS)

    def mask_at(at):
        spots = lax.broadcasted_iota(jnp.int32, (CHUNK, width), 0) + (at + mp * tokens)
        return (spots < len_ref[0]).astype(F32)

    def norm_own(at):
        part = pl.ds(at, CHUNK)
        xf = x_ref[part].astype(F32)
        normed[pl.ds(at + window, CHUNK)] = (xf * rms(xf) * gains_ref[0:1]).astype(BF)
        mask = mask_at(at)
        add_stat(2, mask * xf * xf)
        add_stat(5, mask)
        cot_low[part] = (cot_ref[part].astype(F32) * mask).astype(BF)

    def norm_halo(at):
        part = pl.ds(at, CHUNK)
        xf = x_halo[part].astype(F32)
        normed[part] = (xf * rms(xf) * gains_ref[0:1]).astype(BF)

    def repack(at):
        part = pl.ds(at, rows)
        for kind, at in ((0, 0), (3, 1), (1, 2), (2, 3)):
            full_w[kind, part] = jnp.concatenate(
                [mix_w[m, part, at * chan : (at + 1) * chan] for m in range(4)], axis=1
            )

    def project_halo(at):
        part = pl.ds(at, CHUNK)
        a = normed[part]
        ek = jnp.where(mp > 0, jnp.exp(dot_nn(a, full_w[1])), 0.0)
        exp_low[part] = ek.astype(BF)
        kv_low[part] = (ek * dot_nn(a, full_w[2])).astype(BF)

    def project_own(at):
        part = pl.ds(at, CHUNK)
        shifted = pl.ds(at + window, CHUNK)
        a = normed[shifted]
        ek = jnp.exp(dot_nn(a, full_w[1]))
        v = dot_nn(a, full_w[2])
        exp_low[shifted] = ek.astype(BF)
        kv_low[shifted] = (ek * v).astype(BF)
        expk[part] = ek
        val[part] = v
        sig[part] = jax.nn.sigmoid(dot_nn(a, full_w[0]))

    def build_bands():
        for i in range(3):
            raw = band_rows[pl.ds(mp * 8 + i * 4, 4)].reshape(window, window).astype(F32)
            wide = jnp.concatenate([raw, jnp.zeros_like(raw)], axis=1)
            bands[i] = pltpu.roll(wide, 1, 1, stride=1, stride_axis=0).astype(BF)

    def mix_rows(i):
        part = slice(i * window, (i + 1) * window)
        near = slice(i * window, (i + 2) * window)
        num = dot_nn(bands[i], kv_low[near])
        den = dot_nn(bands[i], exp_low[near])
        ratio[part] = num / den
        rden[part] = 1.0 / den

    def attend(at):
        part = pl.ds(at, CHUNK)
        low = (sig[part] * ratio[part]).astype(BF)
        mixed[part] = low
        attn = dot_nt(low, full_w[3])
        add_stat(3, mask_at(at) * attn * attn)
        total = x_ref[part].astype(F32) + attn
        resid[part] = total
        normed_two[part] = (total * rms(total) * gains_ref[1:2]).astype(BF)

    def hidden_rows(m, first):
        def body(at):
            part = pl.ds(at, CHUNK)
            p = dot_nn(normed_two[part], up_w[m])
            da = dot_nn(cot_low[part], down_w[m])
            square = p * p
            t = jnp.tanh(p * (GELU_C + GELU_C * GELU_A * square))
            gate = 0.5 + 0.5 * t
            value = p * gate
            slope = gate + value * (1.0 - gate) * (
                2.0 * GELU_C + 6.0 * GELU_C * GELU_A * square
            )
            low = value.astype(BF)
            dlow = (da * slope).astype(BF)
            act[part] = low
            dpre[part] = dlow
            f = dot_nt(low, down_w[m])
            d = dot_nt(dlow, up_w[m])
            if first:
                ffn[part] = f
                dn_two[part] = d
            else:
                ffn[part] += f
                dn_two[part] += d

        return body

    def weight_grad(result, left, right):
        for at in range(0, result.shape[1], 256):
            part = slice(at, at + 256)
            result[:, part] = dot_tn(left[...], right[:, part]).astype(result.dtype)

    def close_hidden(at):
        part = pl.ds(at, CHUNK)
        mask = mask_at(at)
        f = ffn[part]
        res = resid[part]
        add_stat(4, mask * f * f)
        blk_ref[part] = (res + f).astype(BF)
        d = dn_two[part]
        r = rms(res)
        u = gains_ref[1:2] * d
        grad = (
            cot_ref[part].astype(F32) * mask
            + r * u
            - res * (r * r * r) * jnp.mean(u * res, axis=-1, keepdims=True)
        )
        add_stat(1, d * res * r)
        ffn[part] = grad
        act[part] = grad.astype(BF)

    def back_attend(at):
        part = pl.ds(at, CHUNK)
        dm = dot_nn(act[part], full_w[3])
        sg = sig[part]
        rt = ratio[part]
        scaled = dm * sg
        normed_two[part] = (scaled * rt * (1.0 - sg)).astype(BF)
        dn = scaled * rden[part]
        dnum[part] = dn.astype(BF)
        dden[part] = (-dn * rt).astype(BF)

    def halo_back(slot, buf):
        return pltpu.make_async_remote_copy(
            src_ref=buf.at[pl.ds(0, window)],
            dst_ref=buf.at[pl.ds(tokens, window)],
            send_sem=halo_send.at[slot],
            recv_sem=halo_recv.at[slot],
            device_id=(group, inner, (mp + 3) % 4),
            device_id_type=MESH,
        )

    def band_grad(i):
        part = slice(i * window, (i + 1) * window)
        near = slice(i * window, (i + 2) * window)
        dn_two[part, 0 : 2 * window] = dot_nt(dnum[part], kv_low[near]) + dot_nt(dden[part], exp_low[near])

    def unskew(j):
        wide = 2 * window
        count = bias_part.shape[1]
        line = lax.broadcasted_iota(jnp.int32, (count, wide), 0)
        v = dn_two[j * count : (j + 1) * count, 0:wide]
        v = pltpu.roll(v, wide - 1 - (j * count) % window, 1)
        bit = 1
        while bit < count:
            v = jnp.where((line & bit) != 0, pltpu.roll(v, wide - bit, 1), v)
            bit *= 2
        bias_part[j] = v[:, 0:window].astype(BF)

    def back_keys(j):
        here = slice(j * window, (j + 1) * window)
        then = slice((j + 1) * window, (j + 2) * window)
        right = bands[j, :, window:]
        left = bands[j + 1, :, :window]
        dkv = dot_tn(right, dnum[here]) + dot_tn(left, dnum[then])
        de = dot_tn(right, dden[here]) + dot_tn(left, dden[then])
        ek = expk[here]
        cot_low[here] = (dkv * ek).astype(BF)
        dpre[here] = ((de + dkv * val[here]) * ek).astype(BF)

    def back_input(at):
        part = pl.ds(at, CHUNK)
        d = (
            dot_nt(normed_two[part], full_w[0])
            + dot_nt(dpre[part], full_w[1])
            + dot_nt(cot_low[part], full_w[2])
        )
        xf = x_ref[part].astype(F32)
        r = rms(xf)
        u = gains_ref[0:1] * d
        gin_ref[part] = (
            ffn[part] + r * u - xf * (r * r * r) * jnp.mean(u * xf, axis=-1, keepdims=True)
        )
        add_stat(0, d * xf * r)

    def mix_grad(kind):
        grad = (normed_two, dpre, cot_low)[kind]
        result = wide_rows.at[pl.ds(kind * GROUPS * rows, GROUPS * rows)]
        weight_grad(result, normed.at[pl.ds(window, tokens)], grad)

    def unpack(kinds, first):
        def body(at):
            part = pl.ds(at, rows)
            for m in range(4):
                mine = slice(m * chan, (m + 1) * chan)
                pair = [
                    full_w[3, part, mine]
                    if kind == 3
                    else wide_rows[pl.ds(at + kind * GROUPS * rows, rows), mine].astype(BF)
                    for kind in kinds
                ]
                span = slice(first * chan, (first + 2) * chan)
                mix_w[m, part, span] = jnp.concatenate(pair, axis=1)

        return body

    scatter_pieces = [
        (mix_w, 0, half, None, 0),
        (mix_w, half, half, None, half),
        (up_w, 0, up_w.shape[2], gu_ref, 2 * half),
        (down_w, 0, down_w.shape[2], gd_ref, 2 * half + up_w.shape[2]),
    ]

    def rs(piece, src, dst, peer, slot):
        return pltpu.make_async_remote_copy(
            src_ref=src,
            dst_ref=dst,
            send_sem=rs_send.at[piece, slot],
            recv_sem=rs_recv.at[piece, slot],
            device_id=peer,
            device_id_type=MESH,
        )

    def x_of(far):
        return 1 - x if far else x

    def block(piece, xs, zs, ys):
        buf, start, size = scatter_pieces[piece][:3]
        at = pl.multiple_of((zs * YN + ys) * rows, 32)
        return buf.at[xs * 2 + c, pl.ds(at, rows), pl.ds(start, size)]

    def lanes(piece):
        return pl.ds(scatter_pieces[piece][4], scatter_pieces[piece][2])

    def core_landing(p, far):
        if p < 2:
            return recv_core.at[0, :, pl.ds((far * 2 + p) * half, half)]
        return recv_core.at[far, :, pl.ds((p - 2) * up_w.shape[2], up_w.shape[2])]

    def core_copy(p, far):
        buf, start, size = scatter_pieces[p][:3]
        src = buf.at[x_of(far) * 2 + 1 - c, :, pl.ds(start, size)]
        return rs(p, src, core_landing(p, far), core_peer, far)

    def core_send(p, far):
        out.go(core_copy(p, far))

    def core_sum(p, far):
        buf, start, size = scatter_pieces[p][:3]
        core_copy(p, far).wait_recv()
        landed = core_landing(p, far)

        def body(at):
            part = pl.ds(at, rows)
            buf[x_of(far) * 2 + c, part, pl.ds(start, size)] += landed[part]

        loop_rows(GROUPS * rows, rows, body)

    def behind(k):
        return (z + ZN - k) % ZN

    def y_copy(p, far, k):
        src = block(p, x_of(far), behind(k), 1 - y)
        return rs(p, src, recv_one.at[far * ZN + k, :, lanes(p)], y_peer, 2 + far * ZN + k)

    def line_copy(p, k):
        src = block(p, 1 - x, behind(k), 1 - y)
        landing = recv_one.at[ZN + k, :, lanes(p)]
        return rs(p, src, landing, z_peers[ZN - 1 - k], 2 + ZN + k)

    def cross_copy(p):
        src = block(p, 1 - x, z, 1 - y)
        return rs(p, src, recv_one.at[ZN, :, lanes(p)], x_peer, 2 + ZN)

    def y_send(p, far):
        if not LINE_SUMS[p]:
            for k in (1, 2, 3, 0):
                out.go(y_copy(p, far, k))
        elif far:
            for k in (1, 2, 3):
                out.go(line_copy(p, k))
            for k in (1, 2, 3, 0):
                out.go(x_copy(p, k))
        else:
            for k in (1, 2, 3):
                out.go(y_copy(p, far, k))

    def line_take(p, k):
        if k:
            line_copy(p, k).wait_recv()
            spot_ref = block(p, 1 - x, z, 1 - y)
            spot_ref[...] += recv_one[ZN + k, :, lanes(p)]
            if k == 3:
                out.go(cross_copy(p))
        else:
            cross_copy(p).wait_recv()
            spot_ref = block(p, x, z, 1 - y)
            spot_ref[...] += recv_one[ZN, :, lanes(p)]
            out.go(y_copy(p, 0, 0))

    def y_take(p, far, k):
        y_copy(p, far, k).wait_recv()
        spot_ref = block(p, x_of(far), behind(k), y)
        spot_ref[...] += recv_one[far * ZN + k, :, lanes(p)]

    def x_copy(p, k):
        src = block(p, 1 - x, behind(k), y)
        return rs(p, src, recv_two.at[k, :, lanes(p)], x_peer, 10 + k)

    def x_take(p, k):
        x_copy(p, k).wait_recv()
        spot_ref = block(p, x, behind(k), y)
        spot_ref[...] += recv_two[k, :, lanes(p)]

    def z_copy(p, k):
        src = block(p, x, behind(k), y)
        return rs(p, src, recv_z.at[k - 1, :, lanes(p)], z_peers[ZN - 1 - k], 13 + k)

    def z_take(p):
        total = block(p, x, z, y)[...].astype(F32)
        for k in range(1, ZN):
            z_copy(p, k).wait_recv()
            total = total + recv_z[k - 1, :, lanes(p)].astype(F32)
        if p == 0:
            gq_ref[0] = total[:, :chan]
            go_ref[...] = total[:, chan:].T
        elif p == 1:
            gq_ref[1] = total[:, :chan]
            gq_ref[2] = total[:, chan:]
        else:
            scatter_pieces[p][3][...] = total

    def y_turn(p, k):
        if LINE_SUMS[p]:
            line_take(p, k)
        else:
            y_take(p, 1, k)
            out.go(x_copy(p, k))

    def x_end(p, k):
        x_take(p, k)
        if k:
            out.go(z_copy(p, k))

    def bias_copy(src, dst, peer, slot):
        return pltpu.make_async_remote_copy(
            src_ref=src,
            dst_ref=dst,
            send_sem=bias_send.at[slot],
            recv_sem=bias_recv.at[slot],
            device_id=peer,
            device_id_type=MESH,
        )

    def bias_y(k):
        return bias_copy(
            bias_part.at[behind(k) * YN + 1 - y], bias_recv_y.at[k], y_peer, k
        )

    def bias_z(k):
        return bias_copy(
            bias_part.at[behind(k) * YN + y], bias_recv_z.at[k - 1], z_peers[ZN - 1 - k], 3 + k
        )

    def bias_turn():
        for k in (1, 2, 3, 0):
            bias_y(k).wait_recv()
            bias_part[behind(k) * YN + y] += bias_recv_y[k]
            if k:
                out.go(bias_z(k))

    def close_bias():
        total = bias_part[z * YN + y].astype(F32)
        for k in range(1, ZN):
            bias_z(k).wait_recv()
            total = total + bias_recv_z[k - 1].astype(F32)
        bias_hop[0] = jnp.dot(
            total, flip, precision=lax.Precision.HIGHEST, preferred_element_type=F32
        )

    def hop_copy():
        owner = mp * GROUPS + group
        return pltpu.make_async_remote_copy(
            src_ref=bias_hop.at[0],
            dst_ref=bias_hop.at[1],
            send_sem=bias_send.at[7],
            recv_sem=bias_recv.at[7],
            device_id=(owner // 4, inner, owner % 4),
            device_id_type=MESH,
        )

    def reduce_stats():
        def copy(step, slot, peer):
            return pltpu.make_async_remote_copy(
                src_ref=stats.at[step],
                dst_ref=stats_recv.at[slot],
                send_sem=stat_send.at[slot],
                recv_sem=stat_recv.at[slot],
                device_id=peer,
                device_id_type=MESH,
            )

        return copy

    def stats_step(step):
        copy = reduce_stats()
        peer = (core_peer, x_peer, y_peer)[step]
        copy(step, step, peer).wait_recv()
        stats[step + 1] = stats[step] + stats_recv[step]

    def stats_send(step):
        copy = reduce_stats()
        if step < 3:
            out.go(copy(step, step, (core_peer, x_peer, y_peer)[step]))
        else:
            for k in range(1, ZN):
                out.go(copy(3, 2 + k, z_peers[k - 1]))

    def stats_end():
        copy = reduce_stats()
        total = stats[3]
        for k in range(1, ZN):
            copy(3, 2 + k, z_peers[k - 1]).wait_recv()
            total = total + stats_recv[2 + k]
        stat_ref[...] = total

    backs = [halo_back(1, dnum), halo_back(2, dden)]

    def halo_start():
        pl.when(mp < 3)(halo_copy.start)

    def repack_all():
        for p in (0, 1):
            gather_core(p)
        loop_rows(GROUPS * rows, rows, repack)

    def halo_work():
        pl.when(mp > 0)(halo_copy.wait_recv)

        @pl.when(mp == 0)
        def _():
            x_halo[...] = jnp.zeros_like(x_halo)

        norm_halo(0)
        project_halo(0)

    def bands_work():
        gather_core(2)
        build_bands()

    def slab(r):
        return x_of(r // 2) * 2 + (1 - c if r % 2 else c)

    def hidden(r, part):
        if r % 2 and part == 0:
            for p in (3, 4):
                gather_core(p, (r - 1, r))
        hidden_rows(slab(r), r == 1)(part * CHUNK)

    def hidden_grad(r, part):
        if part == 0:
            if r % 2 == 0:
                out.drain("far" if r else "near")
            weight_grad(up_w.at[slab(r)], normed_two, dpre)
        else:
            weight_grad(down_w.at[slab(r)], cot_low, act)

    def back_start():
        @pl.when(mp > 0)
        def _():
            for item in backs:
                item.start()

    def unpack_pair(part):
        out.drain("mix")
        loop_rows(GROUPS * rows, rows, unpack(((0, 3), (1, 2))[part], 2 * part))

    def keys_back(j):
        if j:

            @pl.when(mp < 3)
            def _():
                for item in backs:
                    item.wait_recv()

            @pl.when(mp == 3)
            def _():
                dnum[pl.ds(tokens, window)] = jnp.zeros((window, width), BF)
                dden[pl.ds(tokens, window)] = jnp.zeros((window, width), BF)

        back_keys(j)

    def sum_send(p, far):
        core_sum(p, far)
        y_send(p, far)

    def unskew_all():
        for j in range(GROUPS):
            unskew(j)

    def bias_start():
        for k in (1, 2, 3, 0):
            out.go(bias_y(k))

    def bias_close():
        close_bias()
        if last_hop:

            @pl.when(moves)
            def _():
                hop_copy().start()

    def bias_end():
        if last_hop:

            @pl.when(moves)
            def _():
                hop_copy().wait_recv()
                gb_ref[...] = bias_hop[1]

            @pl.when(jnp.logical_not(moves))
            def _():
                gb_ref[...] = bias_hop[0]

        else:
            gb_ref[...] = bias_hop[0]

    actions = {
        "send_z": start_z,
        "send_y": start_y,
        "send_x": start_x,
        "send_c": start_core,
        "z": gather_z,
        "y": gather_y,
        "x": gather_x,
        "d": gather_last,
        "halo": halo_start,
        "norm": lambda: loop_rows(tokens, CHUNK, norm_own),
        "repack": repack_all,
        "proj": lambda q: project_own(q * CHUNK),
        "halow": halo_work,
        "bands": bands_work,
        "mix": mix_rows,
        "att": lambda q: attend(q * CHUNK),
        "h": hidden,
        "g": hidden_grad,
        "close": lambda q: close_hidden(q * CHUNK),
        "ba": lambda q: back_attend(q * CHUNK),
        "hb": back_start,
        "gout": lambda: weight_grad(full_w.at[3], act, mixed),
        "mg": mix_grad,
        "unpack": unpack_pair,
        "bk": keys_back,
        "bg": band_grad,
        "unsk": unskew_all,
        "bi": lambda q: back_input(q * CHUNK),
        "cs": core_send,
        "sum": sum_send,
        "yt": lambda p, k: y_take(p, 0, k),
        "yx": y_turn,
        "xe": x_end,
        "zt": z_take,
        "by": bias_start,
        "bt": bias_turn,
        "bc": bias_close,
        "hopw": bias_end,
        "ss": stats_send,
        "sw": stats_step,
        "se": stats_end,
    }
    band_rows[4 * GROUPS : 4 * GROUPS + 4] = jnp.zeros((4, *bias_ref.shape), BF)
    up_w[mp, home, :] = wu_ref[...].astype(BF)
    down_w[mp, home, :] = wd_ref[...].astype(BF)
    for name, *args in SCHEDULE:
        actions[name](*args)

    @pl.when(mp < 3)
    def _():
        halo_copy.wait_send()

    @pl.when(mp > 0)
    def _():
        for item in backs:
            item.wait_send()

    if last_hop:

        @pl.when(moves)
        def _():
            hop_copy().wait_send()

    out.drain()


def run_block(lengths, x, cot, gains, wq, wo, wu, wd, bias, last_hop):
    tokens, width = x.shape
    window = bias.shape[1]
    rows = wu.shape[0]
    full = rows * GROUPS
    mix_width = 4 * wq.shape[2]
    hidden = wu.shape[1]
    lanes = mix_width + 2 * hidden
    vmem = pl.BlockSpec(memory_space=pltpu.VMEM)

    def shape(*dims, kind=F32):
        return jax.ShapeDtypeStruct(dims, kind)

    def buf(*dims):
        return pltpu.VMEM(dims, F32)

    def low(*dims):
        return pltpu.VMEM(dims, BF)

    dma = pltpu.SemaphoreType.DMA
    return pl.pallas_call(
        functools.partial(block_kernel, last_hop),
        out_shape=(
            shape(tokens, width, kind=BF),
            shape(tokens, width),
            shape(*wq.shape),
            shape(*wo.shape),
            shape(*wu.shape),
            shape(*wd.shape),
            shape(*bias.shape),
            shape(8, width),
        ),
        in_specs=[pl.BlockSpec(memory_space=pltpu.SMEM)] + [vmem] * 8,
        out_specs=(vmem,) * 8,
        scratch_shapes=[
            low(4, full, mix_width),
            low(4, full, hidden),
            low(4, full, hidden),
            low(4 * GROUPS + 4, *bias.shape),
            low(window, width),
            low(4, full, width),
            low(window + tokens, width),
            buf(5 * tokens, width),
            buf(tokens, width),
            low(window + tokens, width),
            low(window + tokens, width),
            low(3, window, 2 * window),
            low(tokens, width),
            low(tokens, width),
            low(tokens, width),
            low(tokens, hidden),
            low(tokens, hidden),
            buf(tokens, width),
            low(tokens + window, width),
            low(tokens + window, width),
            low(GROUPS, *bias.shape),
            low(ZN, *bias.shape),
            low(ZN - 1, *bias.shape),
            buf(2, *bias.shape),
            buf(4, 8, width),
            buf(6, 8, width),
            low(2, full, 2 * hidden),
            low(GROUPS, rows, lanes),
            low(ZN, rows, lanes),
            low(ZN - 1, rows, lanes),
            dma((5, 32)),
            dma((5, 32)),
            dma((4, 17)),
            dma((4, 17)),
            dma((3,)),
            dma((3,)),
            dma((8,)),
            dma((8,)),
            dma((6,)),
            dma((6,)),
        ],
        compiler_params=pltpu.CompilerParams(
            collective_id=0, has_side_effects=True, vmem_limit_bytes=63 * 1024 * 1024
        ),
    )(lengths, x, cot, gains, wq, wo, wu, wd, bias)


MESH = pl.DeviceIdType.MESH


def adam_kernel(scale, *refs):
    grads, refs = refs[:6], refs[6:]
    params, refs = refs[:6], refs[6:]
    firsts, refs = refs[:6], refs[6:]
    seconds, refs = refs[:6], refs[6:]
    out_grads, out_firsts, out_seconds, out_updates = (
        refs[6 * i : 6 * i + 6] for i in range(4)
    )
    rms_ref = refs[24]
    one = 1.0 / (1.0 - BETA_ONE**ADAM_STEP)
    two = 1.0 / (1.0 - BETA_TWO**ADAM_STEP)

    def step(i):
        if i == 4:
            grad = grads[4][...] * jnp.exp(params[4][...])
        elif i == 5:
            grad = grads[5][0:2]
        else:
            grad = grads[i][...]
        grad = grad * scale
        first = BETA_ONE * firsts[i][...] + (1.0 - BETA_ONE) * grad
        second = BETA_TWO * seconds[i][...] + (1.0 - BETA_TWO) * (grad * grad)
        change = (first * one) / (jnp.sqrt(second * two) + ADAM_EPS)
        if i < 4:
            change = change + WEIGHT_DECAY * params[i][...]
        out_grads[i][...] = grad
        out_firsts[i][...] = first
        out_seconds[i][...] = second
        out_updates[i][...] = -LEARN_RATE * change

    for i in range(4):
        step(i)

    @pl.when(pl.program_id(0) == 0)
    def _():
        for i in (4, 5):
            step(i)
        sums = jnp.sum(grads[5][...], axis=1, keepdims=True)
        rms = jnp.sqrt(sums[2:5] / sums[5:6])
        for i in range(3):
            rms_ref[i] = jnp.sum(rms[i : i + 1, :])


def run_adam(scale, grads, params, firsts, seconds):
    kinds = [jax.ShapeDtypeStruct(param.shape, F32) for param in params]
    parts = 1

    def cut(item):
        block = (item.shape[0] // parts, *item.shape[1:])
        return pl.BlockSpec(block, lambda i: (i, *[0] * (len(item.shape) - 1)))

    def whole(item):
        return pl.BlockSpec(item.shape, lambda i: (0,) * len(item.shape))

    def specs(items):
        return [cut(item) for item in items[:4]] + [whole(item) for item in items[4:]]

    return pl.pallas_call(
        functools.partial(adam_kernel, scale),
        grid=(parts,),
        out_shape=(*(kinds * 4), jax.ShapeDtypeStruct((3,), F32)),
        in_specs=specs(grads) + specs(params) * 3,
        out_specs=(*specs(kinds) * 4, pl.BlockSpec(memory_space=pltpu.SMEM)),
        compiler_params=pltpu.CompilerParams(vmem_limit_bytes=62 * 1024 * 1024),
    )(*grads, *params, *firsts, *seconds)


def stored(items):
    qkv, mix, up, down, bias, gains = items
    return [qkv.transpose(1, 0, 2), mix, up, down.T, bias, gains]


def shards(inner, block_input, out_cotangent, lengths, *rest):
    params, firsts, seconds = (stored(rest[6 * i : 6 * i + 6]) for i in range(3))
    held = params
    if inner > 1:
        axes = (1, 1, 0, 0)
        held = [
            lax.all_gather(item.astype(BF), "dpl", axis=axis, tiled=True).astype(F32)
            for item, axis in zip(params[:4], axes, strict=True)
        ]
        count = params[4].shape[0]
        every = lax.all_gather(params[4], ("dpl", "mp"), axis=0, tiled=True)
        at = lax.axis_index("mp") * inner * count
        held += [lax.dynamic_slice_in_dim(every, at, inner * count, 0), params[5]]
    block_low, grad_input, *grads = run_block(
        lengths,
        block_input[0],
        out_cotangent[0],
        held[5],
        *held[:5],
        inner == 1,
    )
    if inner > 1:
        for i, axis in enumerate(axes):
            grads[i] = lax.psum_scatter(grads[i], "dpl", scatter_dimension=axis, tiled=True)
        grads[4], grads[5] = lax.psum((grads[4], grads[5]), "dpl")
        every = lax.all_gather(grads[4], ("mp", "dph"), axis=0, tiled=True)
        place = lax.axis_index(("dph", "dpl", "mp"))
        grads[4] = lax.dynamic_slice_in_dim(every, place * count, count, 0)
    scale = float(lax.axis_size("dph") * inner * LEN) ** (-0.5)
    *results, rms_stats = run_adam(scale, grads, params, firsts, seconds)
    outs = []
    for i in range(4):
        qkv, mix, up, down, bias, gains = results[6 * i : 6 * i + 6]
        outs += [qkv.transpose(1, 0, 2), mix, up, down.T, bias, gains]
    return (block_low[None], grad_input[None], *outs, rms_stats)


def solution(mesh):
    inner = mesh.shape["dp"] // GROUPS
    fine = Mesh(
        mesh.devices.reshape(GROUPS, inner, mesh.shape["mp"]),
        ("dph", "dpl", "mp"),
    )
    dp = ("dph", "dpl")
    weights = (
        P(dp, None, "mp"),
        P("mp", dp),
        P(dp, "mp"),
        P("mp", dp),
        P((*dp, "mp"), None),
        P(),
    )
    acts = P(dp, "mp", None)
    return jax.shard_map(
        functools.partial(shards, inner),
        mesh=fine,
        in_specs=(acts, acts, P(dp), *weights, *weights, *weights),
        out_specs=(acts, acts, *weights, *weights, *weights, *weights, P()),
        check_vma=False,
    )
```

```python
import functools

import jax
import jax.numpy as jnp
from jax import lax
from jax.experimental import pallas as pl
from jax.experimental.pallas import tpu as pltpu
from jax.sharding import Mesh
from jax.sharding import PartitionSpec as P

LEN = 2048
ADAM_STEP = 10
EPS = 1e-06
BETA_ONE = 0.9
BETA_TWO = 0.99
LEARN_RATE = 0.03
WEIGHT_DECAY = 0.1
ADAM_EPS = 1e-08

F32 = jnp.float32
BF = jnp.bfloat16
ZN, YN = 4, 2
GROUPS = ZN * YN
CHUNK = 256
GELU_C = 0.7978845608028654
GELU_A = 0.044715


ROUTES = ((True, False), (False, False), (False, False), (True, False), (False, True))
LINE_SUMS = (False, False, True, False)
SCHEDULE = (
    ("send_y", 1), ("send_x", 2), ("send_c", 3), ("send_c", 0), ("send_x", 0), ("send_x", 1),
    ("send_c", 1), ("send_z", 0), ("send_y", 0), ("send_z", 1), ("norm",), ("x", 2, 0),
    ("send_c", 2), ("y", 1, 0), ("send_z", 3), ("z", 0, 1), ("x", 0, 0), ("y", 0, 0),
    ("x", 1, 0), ("z", 0, 2), ("y", 0, 1), ("x", 0, 1), ("z", 1, 1), ("send_z", 2), ("d", 1, 0),
    ("d", 0, 0), ("z", 1, 2), ("z", 3, 1), ("z", 3, 2), ("x", 1, 1), ("y", 0, 2), ("z", 2, 1),
    ("send_y", 2), ("z", 0, 3), ("z", 2, 2), ("x", 0, 2), ("z", 1, 3), ("z", 3, 3), ("y", 0, 3),
    ("z", 2, 3), ("send_y", 3), ("halo",), ("d", 1, 1), ("y", 2, 0), ("y", 1, 1), ("y", 1, 2),
    ("d", 0, 1), ("d", 0, 2), ("x", 2, 1), ("y", 1, 3), ("x", 1, 2), ("send_z", 4), ("d", 1, 2),
    ("send_x", 3), ("x", 1, 3), ("z", 4, 1), ("y", 2, 1), ("y", 2, 2), ("z", 4, 2), ("y", 2, 3),
    ("x", 2, 2), ("x", 2, 3), ("send_x", 4), ("d", 0, 3), ("d", 2, 0), ("d", 2, 1), ("x", 0, 3),
    ("send_y", 4), ("x", 3, 0), ("y", 3, 0), ("y", 3, 1), ("z", 4, 3), ("send_c", 4),
    ("d", 1, 3), ("y", 3, 2), ("y", 3, 3), ("x", 3, 1), ("repack",), ("proj", 0), ("proj", 1),
    ("d", 2, 2), ("d", 2, 3), ("bands",), ("halow",), ("y", 4, 0), ("y", 4, 1), ("y", 4, 2),
    ("x", 4, 0), ("x", 4, 1), ("mix", 0), ("mix", 1), ("y", 4, 3), ("x", 4, 2), ("att", 0),
    ("att", 1), ("d", 4, 0), ("d", 3, 0), ("h", 1, 0), ("h", 1, 1), ("g", 1, 0), ("g", 1, 1),
    ("cs", 2, 0), ("cs", 3, 0), ("d", 3, 1), ("h", 0, 0), ("h", 0, 1), ("d", 4, 1), ("g", 0, 0),
    ("sum", 2, 0), ("g", 0, 1), ("d", 3, 2), ("x", 3, 2), ("x", 4, 3), ("x", 3, 3), ("d", 4, 2),
    ("d", 4, 3), ("sum", 3, 0), ("d", 3, 3), ("h", 3, 0), ("h", 3, 1), ("g", 3, 0),
    ("cs", 2, 1), ("g", 3, 1), ("cs", 3, 1), ("yt", 2, 1), ("yt", 2, 2), ("h", 2, 0),
    ("h", 2, 1), ("g", 2, 0), ("sum", 2, 1), ("g", 2, 1), ("close", 0), ("close", 1),
    ("sum", 3, 1), ("yt", 3, 1), ("yt", 3, 2), ("xe", 2, 1), ("ba", 0), ("ba", 1), ("bh",),
    ("hb",), ("xe", 2, 2), ("bg", 0), ("bg", 1), ("unsk",), ("yt", 3, 3), ("yx", 3, 1),
    ("mg", 0), ("gout",), ("unpack", 0), ("bk", 0), ("cs", 0, 1), ("by",), ("bk", 1), ("mg", 1),
    ("bi", 0), ("yt", 3, 0), ("yt", 2, 3), ("cs", 0, 0), ("yx", 2, 1), ("yx", 2, 2),
    ("xe", 2, 3), ("yx", 2, 3), ("sum", 0, 1), ("mg", 2), ("unpack", 1), ("cs", 1, 0),
    ("bi", 1), ("ss", 0), ("sum", 0, 0), ("bt",), ("yx", 3, 2), ("yx", 3, 3), ("yx", 3, 0),
    ("sw", 0), ("xe", 3, 1), ("xe", 3, 2), ("yx", 0, 1), ("yt", 0, 1), ("sum", 1, 0),
    ("yt", 0, 2), ("cs", 1, 1), ("sum", 1, 1), ("yx", 2, 0), ("yx", 0, 2), ("xe", 3, 3),
    ("xe", 3, 0), ("yx", 0, 3), ("xe", 0, 1), ("yt", 1, 1), ("yt", 0, 3), ("yx", 0, 0),
    ("ss", 1), ("xe", 0, 2), ("xe", 0, 3), ("yt", 1, 2), ("yt", 1, 3), ("yx", 1, 1),
    ("yt", 0, 0), ("sw", 1), ("ss", 2), ("yx", 1, 2), ("yx", 1, 3), ("xe", 1, 1), ("xe", 1, 2),
    ("yx", 1, 0), ("xe", 1, 3), ("yt", 2, 0), ("xe", 0, 0), ("zt", 0), ("sw", 2), ("xe", 2, 0),
    ("zt", 2), ("yt", 1, 0), ("ss", 3), ("zt", 3), ("xe", 1, 0), ("bc",), ("hopw",), ("zt", 1),
    ("se",),
)


def dot_nn(a, b):
    return jnp.dot(a, b, preferred_element_type=F32)


def dot_nt(a, b):
    return lax.dot_general(a, b, (((1,), (1,)), ((), ())), preferred_element_type=F32)


def dot_tn(a, b):
    return lax.dot_general(a, b, (((0,), (0,)), ((), ())), preferred_element_type=F32)


def loop_rows(count, step, body, unroll=False):
    @pl.loop(0, count // step, unroll=unroll)
    def _(index):
        body(pl.multiple_of(index * step, step))


class Copies:
    def __init__(self):
        self.started = {}

    def go(self, copy, tag=None):
        copy.start()
        self.started.setdefault(tag, []).append(copy)

    def go_if(self, when, copy, tag=None):
        pl.when(when)(copy.start)
        self.started.setdefault(tag, []).append((when, copy))

    def drain(self, *tags):
        for tag in tags or list(self.started):
            for copy in self.started.pop(tag, []):
                if isinstance(copy, tuple):
                    pl.when(copy[0])(copy[1].wait_send)
                else:
                    copy.wait_send()


def block_kernel(
    last_hop,
    len_ref,
    x_ref,
    cot_ref,
    gains_ref,
    wq_ref,
    wo_ref,
    wu_ref,
    wd_ref,
    bias_ref,
    blk_ref,
    gin_ref,
    gq_ref,
    go_ref,
    gu_ref,
    gd_ref,
    gb_ref,
    stat_ref,
    mix_w,
    up_w,
    down_w,
    band_rows,
    x_halo,
    full_w,
    normed,
    wide_rows,
    resid,
    exp_low,
    kv_low,
    bands,
    mixed,
    normed_two,
    cot_low,
    act,
    dpre,
    dn_two,
    dnum,
    dden,
    dkey_halo,
    dval_halo,
    dnorm_recv,
    bias_part,
    bias_recv_y,
    bias_recv_z,
    bias_hop,
    stats,
    stats_recv,
    recv_core,
    recv_one,
    recv_two,
    recv_z,
    ag_send,
    ag_recv,
    rs_send,
    rs_recv,
    halo_send,
    halo_recv,
    bias_send,
    bias_recv,
    stat_send,
    stat_recv,
):
    tokens, width = x_ref.shape
    window = x_halo.shape[0]
    rows = wu_ref.shape[0]
    chan = width // 4
    ffn = gin_ref
    sig, ratio, rden, expk, val = (
        wide_rows.at[pl.ds(i * tokens, tokens)] for i in range(5)
    )
    group = lax.axis_index("dph")
    inner = lax.axis_index("dpl")
    mp = lax.axis_index("mp")
    z, y = group // YN, group % YN
    x, c = mp // 2, mp % 2

    def device(zs, ys, xs, cs):
        return (zs * YN + ys, inner, xs * 2 + cs)

    def z_at(k):
        return (z + k) % ZN

    core_peer = device(z, y, x, 1 - c)
    x_peer = device(z, y, 1 - x, c)
    y_peer = device(z, 1 - y, x, c)
    diag_peer = device(z, y, 1 - x, 1 - c)
    z_peers = [device(z_at(k), y, x, c) for k in range(1, ZN)]

    out = Copies()

    half = 2 * chan
    gather_pieces = [
        (mix_w, 0, half),
        (mix_w, half, half),
        (None, 0, 0),
        (up_w, 0, up_w.shape[2]),
        (down_w, 0, down_w.shape[2]),
    ]

    def place(piece, zs, ys, xs, cs):
        buf, start, size = gather_pieces[piece]
        if buf is None:
            return band_rows.at[(zs * YN + ys) * 4 + xs * 2 + cs]
        at = pl.multiple_of((zs * YN + ys) * rows, 32)
        return buf.at[xs * 2 + cs, pl.ds(at, rows), pl.ds(start, size)]

    def ag(piece, loc, peer, slot):
        ref = place(piece, *loc)
        return pltpu.make_async_remote_copy(
            src_ref=ref,
            dst_ref=ref,
            send_sem=ag_send.at[piece, slot],
            recv_sem=ag_recv.at[piece, slot],
            device_id=peer,
            device_id_type=MESH,
        )

    own = (z, y, x, c)

    def along(i):
        edge = jnp.where(z == 0, i, ZN - 1 - i)
        inside = jnp.where(z == 1, (1, 0, 2, 3)[i], (2, 1, 3, 0)[i])
        return jnp.where((z == 0) | (z == ZN - 1), edge, inside)

    order = [along(i) for i in range(ZN)]

    def spot(kind, zs):
        return (zs, y if kind in (0, 2) else 1 - y, x if kind in (0, 1) else 1 - x, c)

    def tag_of(piece, kind):
        return "mix" if piece < 3 else ("near" if kind < 2 else "far")

    def forward(piece, kind, zs, peer, slot, when=None):
        copy = ag(piece, spot(kind, zs), peer, slot)
        if piece == 2 and when is not None:
            out.go_if(when, copy, tag_of(piece, kind))
        else:
            out.go(copy, tag_of(piece, kind))

    def used_here(zs):
        return zs // 2 == x

    def to_core(piece, kind, i):
        zs = order[i]
        when = used_here(zs) & (zs % 2 != c)
        forward(piece, kind, zs, core_peer, 16 + kind * 4 + zs, when)

    def arrived(piece, slot, when=None):
        wait = ag(piece, own, core_peer, slot).wait_recv
        if piece == 2 and when is not None:
            pl.when(when)(wait)
        else:
            wait()

    def turns_y(piece):
        return ROUTES[piece][0]

    def pass_z(piece, kind, zs, step, when):
        peer = device(jnp.clip(z + step, 0, ZN - 1), y, x, c)
        copy = ag(piece, spot(kind, zs), peer, kind * 4 + zs)
        out.go_if(when, copy, tag_of(piece, kind))

    def start_line(piece, kind):
        pass_z(piece, kind, z, 1, z < ZN - 1)
        pass_z(piece, kind, z, -1, z > 0)

    def pass_line(piece, kind, zs):
        up = zs < z
        pass_z(piece, kind, zs, jnp.where(up, 1, -1), jnp.where(up, z < ZN - 1, z > 0))

    def start_z(piece):
        start_line(piece, 0)

    def start_y(piece):
        forward(piece, 0, z, y_peer, 4 + z, used_here(z))

    def start_x(piece):
        forward(piece, 0, z, x_peer, 8 + z, jnp.logical_not(used_here(z)))

    def start_core(piece):
        to_core(piece, 0, 0)

    def gather_z(piece, i):
        zs = order[i]
        arrived(piece, zs)
        pass_line(piece, 0, zs)
        forward(piece, 0, zs, y_peer, 4 + zs, used_here(zs))
        forward(piece, 0, zs, x_peer, 8 + zs, jnp.logical_not(used_here(zs)))
        to_core(piece, 0, i)

    def turns(piece, i):
        return not ROUTES[piece][1] or i == 0

    def gather_y(piece, i):
        zs = order[i]
        arrived(piece, 4 + zs, used_here(zs))
        if turns_y(piece) and turns(piece, i):
            forward(piece, 1, zs, x_peer, 12 + zs)
        to_core(piece, 1, i)

    def gather_x(piece, i):
        zs = order[i]
        arrived(piece, 8 + zs, used_here(zs))
        if not turns_y(piece) and turns(piece, i):
            forward(piece, 2, zs, y_peer, 12 + zs, used_here(zs))
        to_core(piece, 2, i)

    def gather_last(piece, i):
        zs = order[i]
        arrived(piece, 12 + zs, used_here(zs))
        if ROUTES[piece][1]:
            if i:
                pass_line(piece, 3, zs)
            else:
                start_line(piece, 3)
        to_core(piece, 3, i)

    def gather_core(piece, kinds=(0, 1, 2, 3)):
        for kind in kinds:
            for i in range(ZN):
                zs = order[i]
                arrived(piece, 16 + kind * 4 + zs, used_here(zs) & (zs % 2 == c))

    barrier = pltpu.get_barrier_semaphore()
    friends = [core_peer, x_peer, y_peer, diag_peer] + z_peers
    for friend in friends:
        pl.semaphore_signal(barrier, inc=1, device_id=friend, device_id_type=MESH)
    here = group * 4 + mp
    moves = here != mp * GROUPS + group
    if last_hop:

        @pl.when(moves)
        def _():
            pl.semaphore_signal(
                barrier,
                inc=1,
                device_id=(here % GROUPS, inner, here // GROUPS),
                device_id_type=MESH,
            )

    home = pl.ds(pl.multiple_of(group * rows, 32), rows)
    mix_w[mp, home, :] = jnp.concatenate(
        [wq_ref[0], wo_ref[...].T, wq_ref[1], wq_ref[2]], axis=1
    ).astype(BF)
    flip = (
        lax.broadcasted_iota(jnp.int32, (window, window), 0)
        + lax.broadcasted_iota(jnp.int32, (window, window), 1)
        == window - 1
    ).astype(F32)
    band_rows[group * 4 + mp] = dot_nn(
        jnp.exp(bias_ref[...]).astype(BF), flip.astype(BF)
    ).astype(BF)

    up_w[mp, home, :] = wu_ref[...].astype(BF)
    down_w[mp, home, :] = wd_ref[...].astype(BF)
    stats[0] = jnp.zeros(stats.shape[1:], F32)
    if last_hop:

        @pl.when(moves)
        def _():
            pl.semaphore_wait(barrier, len(friends) + 1)

        @pl.when(jnp.logical_not(moves))
        def _():
            pl.semaphore_wait(barrier, len(friends))

    else:
        pl.semaphore_wait(barrier, len(friends))

    halo_copy = pltpu.make_async_remote_copy(
        src_ref=x_ref.at[pl.ds(tokens - window, window)],
        dst_ref=x_halo,
        send_sem=halo_send.at[0],
        recv_sem=halo_recv.at[0],
        device_id=(group, inner, (mp + 1) % 4),
        device_id_type=MESH,
    )


    def add_stat(row, value):
        stats[0, row : row + 1, :] += jnp.sum(value, axis=0, keepdims=True)

    def rms(value):
        return lax.rsqrt(jnp.mean(value * value, axis=-1, keepdims=True) + EPS)

    def mask_at(at):
        spots = lax.broadcasted_iota(jnp.int32, (CHUNK, width), 0) + (at + mp * tokens)
        return (spots < len_ref[0]).astype(F32)

    def norm_own(at):
        part = pl.ds(at, CHUNK)
        xf = x_ref[part].astype(F32)
        normed[pl.ds(at + window, CHUNK)] = (xf * rms(xf) * gains_ref[0:1]).astype(BF)
        mask = mask_at(at)
        add_stat(2, mask * xf * xf)
        add_stat(5, mask)
        cot_low[part] = (cot_ref[part].astype(F32) * mask).astype(BF)

    def norm_halo(at):
        part = pl.ds(at, CHUNK)
        xf = x_halo[part].astype(F32)
        normed[part] = (xf * rms(xf) * gains_ref[0:1]).astype(BF)

    def repack(at):
        part = pl.ds(at, rows)
        for kind, at in ((0, 0), (3, 1), (1, 2), (2, 3)):
            full_w[kind, part] = jnp.concatenate(
                [mix_w[m, part, at * chan : (at + 1) * chan] for m in range(4)], axis=1
            )

    def project_halo(at):
        part = pl.ds(at, CHUNK)
        a = normed[part]
        ek = jnp.where(mp > 0, jnp.exp(dot_nn(a, full_w[1])), 0.0)
        exp_low[part] = ek.astype(BF)
        kv_low[part] = (ek * dot_nn(a, full_w[2])).astype(BF)

    def project_own(at):
        part = pl.ds(at, CHUNK)
        shifted = pl.ds(at + window, CHUNK)
        a = normed[shifted]
        ek = jnp.exp(dot_nn(a, full_w[1]))
        v = dot_nn(a, full_w[2])
        exp_low[shifted] = ek.astype(BF)
        kv_low[shifted] = (ek * v).astype(BF)
        expk[part] = ek
        val[part] = v
        sig[part] = jax.nn.sigmoid(dot_nn(a, full_w[0]))

    def build_bands():
        for i in range(2):
            raw = band_rows[pl.ds(mp * 8 + i * 4, 4)].reshape(window, window).astype(F32)
            wide = jnp.concatenate([raw, jnp.zeros_like(raw)], axis=1)
            bands[i] = pltpu.roll(wide, 1, 1, stride=1, stride_axis=0).astype(BF)

    def mix_rows(i):
        part = slice(i * window, (i + 1) * window)
        near = slice(i * window, (i + 2) * window)
        num = dot_nn(bands[i], kv_low[near])
        den = dot_nn(bands[i], exp_low[near])
        ratio[part] = num / den
        rden[part] = 1.0 / den

    def attend(at):
        part = pl.ds(at, CHUNK)
        low = (sig[part] * ratio[part]).astype(BF)
        mixed[part] = low
        attn = dot_nt(low, full_w[3])
        add_stat(3, mask_at(at) * attn * attn)
        total = x_ref[part].astype(F32) + attn
        resid[part] = total
        normed_two[part] = (total * rms(total) * gains_ref[1:2]).astype(BF)

    def hidden_rows(m, first):
        def body(at):
            part = pl.ds(at, CHUNK)
            p = dot_nn(normed_two[part], up_w[m])
            da = dot_nn(cot_low[part], down_w[m])
            square = p * p
            t = jnp.tanh(p * (GELU_C + GELU_C * GELU_A * square))
            gate = 0.5 + 0.5 * t
            value = p * gate
            slope = gate + value * (1.0 - gate) * (
                2.0 * GELU_C + 6.0 * GELU_C * GELU_A * square
            )
            low = value.astype(BF)
            dlow = (da * slope).astype(BF)
            act[part] = low
            dpre[part] = dlow
            f = dot_nt(low, down_w[m])
            d = dot_nt(dlow, up_w[m])
            if first:
                ffn[part] = f
                dn_two[part] = d
            else:
                ffn[part] += f
                dn_two[part] += d

        return body

    def weight_grad(result, left, right, left_more=None, right_more=None):
        for at in range(0, result.shape[1], 256):
            part = slice(at, at + 256)
            total = dot_tn(left[...], right[:, part])
            if right_more is not None:
                total = total + dot_tn(left_more[0:window], right_more[:, part])
            result[:, part] = total.astype(result.dtype)

    def close_hidden(at):
        part = pl.ds(at, CHUNK)
        mask = mask_at(at)
        f = ffn[part]
        res = resid[part]
        add_stat(4, mask * f * f)
        blk_ref[part] = (res + f).astype(BF)
        d = dn_two[part]
        r = rms(res)
        u = gains_ref[1:2] * d
        grad = (
            cot_ref[part].astype(F32) * mask
            + r * u
            - res * (r * r * r) * jnp.mean(u * res, axis=-1, keepdims=True)
        )
        add_stat(1, d * res * r)
        ffn[part] = grad
        act[part] = grad.astype(BF)

    def back_attend(at):
        part = pl.ds(at, CHUNK)
        dm = dot_nn(act[part], full_w[3])
        sg = sig[part]
        rt = ratio[part]
        scaled = dm * sg
        normed_two[part] = (scaled * rt * (1.0 - sg)).astype(BF)
        dn = scaled * rden[part]
        dnum[part] = dn.astype(BF)
        dden[part] = (-dn * rt).astype(BF)

    def halo_back():
        return pltpu.make_async_remote_copy(
            src_ref=x_halo,
            dst_ref=dnorm_recv,
            send_sem=halo_send.at[1],
            recv_sem=halo_recv.at[1],
            device_id=(group, inner, (mp + 3) % 4),
            device_id_type=MESH,
        )

    def band_grad(i):
        part = slice(i * window, (i + 1) * window)
        near = slice(i * window, (i + 2) * window)
        dn_two[part, 0 : 2 * window] = dot_nt(dnum[part], kv_low[near]) + dot_nt(dden[part], exp_low[near])

    def unskew(j):
        wide = 2 * window
        count = bias_part.shape[1]
        line = lax.broadcasted_iota(jnp.int32, (count, wide), 0)
        v = dn_two[j * count : (j + 1) * count, 0:wide]
        v = pltpu.roll(v, wide - 1 - (j * count) % window, 1)
        bit = 1
        while bit < count:
            v = jnp.where((line & bit) != 0, pltpu.roll(v, wide - bit, 1), v)
            bit *= 2
        bias_part[j] = v[:, 0:window].astype(BF)

    def back_keys(j):
        here = slice(j * window, (j + 1) * window)
        right = bands[j, :, window:]
        dkv = dot_tn(right, dnum[here])
        de = dot_tn(right, dden[here])
        if j == 0:
            then = slice(window, 2 * window)
            left = bands[1, :, :window]
            dkv = dkv + dot_tn(left, dnum[then])
            de = de + dot_tn(left, dden[then])
        ek = expk[here]
        cot_low[here] = (dkv * ek).astype(BF)
        dpre[here] = ((de + dkv * val[here]) * ek).astype(BF)

    def back_halo():
        before = slice(0, window)
        left = bands[0, :, :window]
        dkv = dot_tn(left, dnum[before])
        de = dot_tn(left, dden[before])
        ek = exp_low[before].astype(F32)
        dval_halo[...] = (dkv * ek).astype(BF)
        dkey_halo[...] = (de * ek + dkv * kv_low[before].astype(F32)).astype(BF)

    def halo_return():
        x_halo[...] = (
            dot_nt(dkey_halo[...], full_w[1]) + dot_nt(dval_halo[...], full_w[2])
        ).astype(BF)
        pl.when(mp > 0)(halo_back().start)

    def back_input(at):
        part = pl.ds(at, CHUNK)
        d = (
            dot_nt(normed_two[part], full_w[0])
            + dot_nt(dpre[part], full_w[1])
            + dot_nt(cot_low[part], full_w[2])
        )
        if at:
            pl.when(mp < 3)(halo_back().wait_recv)

            @pl.when(mp == 3)
            def _():
                dnorm_recv[...] = jnp.zeros_like(dnorm_recv)

            d = d + dnorm_recv[...].astype(F32)
        xf = x_ref[part].astype(F32)
        r = rms(xf)
        u = gains_ref[0:1] * d
        gin_ref[part] = (
            ffn[part] + r * u - xf * (r * r * r) * jnp.mean(u * xf, axis=-1, keepdims=True)
        )
        add_stat(0, d * xf * r)

    def mix_grad(kind):
        grad = (normed_two, dpre, cot_low)[kind]
        result = wide_rows.at[pl.ds(kind * GROUPS * rows, GROUPS * rows)]
        left = normed.at[pl.ds(window, tokens)]
        if kind == 0:
            weight_grad(result, left, grad)
        else:
            weight_grad(result, left, grad, normed, (dkey_halo, dval_halo)[kind - 1])

    def unpack(kinds, first):
        def body(at):
            part = pl.ds(at, rows)
            for m in range(4):
                mine = slice(m * chan, (m + 1) * chan)
                pair = [
                    full_w[3, part, mine]
                    if kind == 3
                    else wide_rows[pl.ds(at + kind * GROUPS * rows, rows), mine].astype(BF)
                    for kind in kinds
                ]
                span = slice(first * chan, (first + 2) * chan)
                mix_w[m, part, span] = jnp.concatenate(pair, axis=1)

        return body

    scatter_pieces = [
        (mix_w, 0, half, None, 0),
        (mix_w, half, half, None, half),
        (up_w, 0, up_w.shape[2], gu_ref, 2 * half),
        (down_w, 0, down_w.shape[2], gd_ref, 2 * half + up_w.shape[2]),
    ]

    def rs(piece, src, dst, peer, slot):
        return pltpu.make_async_remote_copy(
            src_ref=src,
            dst_ref=dst,
            send_sem=rs_send.at[piece, slot],
            recv_sem=rs_recv.at[piece, slot],
            device_id=peer,
            device_id_type=MESH,
        )

    def x_of(far):
        return 1 - x if far else x

    def block(piece, xs, zs, ys):
        buf, start, size = scatter_pieces[piece][:3]
        at = pl.multiple_of((zs * YN + ys) * rows, 32)
        return buf.at[xs * 2 + c, pl.ds(at, rows), pl.ds(start, size)]

    def lanes(piece):
        return pl.ds(scatter_pieces[piece][4], scatter_pieces[piece][2])

    def core_landing(p, far):
        if p < 2:
            return recv_core.at[0, :, pl.ds((far * 2 + p) * half, half)]
        return recv_core.at[far, :, pl.ds((p - 2) * up_w.shape[2], up_w.shape[2])]

    def core_copy(p, far):
        buf, start, size = scatter_pieces[p][:3]
        src = buf.at[x_of(far) * 2 + 1 - c, :, pl.ds(start, size)]
        return rs(p, src, core_landing(p, far), core_peer, far)

    def core_send(p, far):
        out.go(core_copy(p, far))

    def core_sum(p, far):
        buf, start, size = scatter_pieces[p][:3]
        core_copy(p, far).wait_recv()
        landed = core_landing(p, far)

        def body(at):
            part = pl.ds(at, rows)
            buf[x_of(far) * 2 + c, part, pl.ds(start, size)] += landed[part]

        loop_rows(GROUPS * rows, rows, body)

    def behind(k):
        return (z + ZN - k) % ZN

    def y_copy(p, far, k):
        src = block(p, x_of(far), behind(k), 1 - y)
        return rs(p, src, recv_one.at[far * ZN + k, :, lanes(p)], y_peer, 2 + far * ZN + k)

    def line_copy(p, k):
        src = block(p, 1 - x, behind(k), 1 - y)
        landing = recv_one.at[ZN + k, :, lanes(p)]
        return rs(p, src, landing, z_peers[ZN - 1 - k], 2 + ZN + k)

    def cross_copy(p):
        src = block(p, 1 - x, z, 1 - y)
        return rs(p, src, recv_one.at[ZN, :, lanes(p)], x_peer, 2 + ZN)

    def y_send(p, far):
        if not LINE_SUMS[p]:
            for k in (1, 2, 3, 0):
                out.go(y_copy(p, far, k))
        elif far:
            for k in (1, 2, 3):
                out.go(line_copy(p, k))
            for k in (1, 2, 3, 0):
                out.go(x_copy(p, k))
        else:
            for k in (1, 2, 3):
                out.go(y_copy(p, far, k))

    def line_take(p, k):
        if k:
            line_copy(p, k).wait_recv()
            spot_ref = block(p, 1 - x, z, 1 - y)
            spot_ref[...] += recv_one[ZN + k, :, lanes(p)]
            if k == 3:
                out.go(cross_copy(p))
        else:
            cross_copy(p).wait_recv()
            spot_ref = block(p, x, z, 1 - y)
            spot_ref[...] += recv_one[ZN, :, lanes(p)]
            out.go(y_copy(p, 0, 0))

    def y_take(p, far, k):
        y_copy(p, far, k).wait_recv()
        spot_ref = block(p, x_of(far), behind(k), y)
        spot_ref[...] += recv_one[far * ZN + k, :, lanes(p)]

    def x_copy(p, k):
        src = block(p, 1 - x, behind(k), y)
        return rs(p, src, recv_two.at[k, :, lanes(p)], x_peer, 10 + k)

    def x_take(p, k):
        x_copy(p, k).wait_recv()
        spot_ref = block(p, x, behind(k), y)
        spot_ref[...] += recv_two[k, :, lanes(p)]

    def z_copy(p, k):
        src = block(p, x, behind(k), y)
        return rs(p, src, recv_z.at[k - 1, :, lanes(p)], z_peers[ZN - 1 - k], 13 + k)

    def z_take(p):
        total = block(p, x, z, y)[...].astype(F32)
        for k in range(1, ZN):
            z_copy(p, k).wait_recv()
            total = total + recv_z[k - 1, :, lanes(p)].astype(F32)
        if p == 0:
            gq_ref[0] = total[:, :chan]
            go_ref[...] = total[:, chan:].T
        elif p == 1:
            gq_ref[1] = total[:, :chan]
            gq_ref[2] = total[:, chan:]
        else:
            scatter_pieces[p][3][...] = total

    def y_turn(p, k):
        if LINE_SUMS[p]:
            line_take(p, k)
        else:
            y_take(p, 1, k)
            out.go(x_copy(p, k))

    def x_end(p, k):
        x_take(p, k)
        if k:
            out.go(z_copy(p, k))

    def bias_copy(src, dst, peer, slot):
        return pltpu.make_async_remote_copy(
            src_ref=src,
            dst_ref=dst,
            send_sem=bias_send.at[slot],
            recv_sem=bias_recv.at[slot],
            device_id=peer,
            device_id_type=MESH,
        )

    def bias_y(k):
        return bias_copy(
            bias_part.at[behind(k) * YN + 1 - y], bias_recv_y.at[k], y_peer, k
        )

    def bias_z(k):
        return bias_copy(
            bias_part.at[behind(k) * YN + y], bias_recv_z.at[k - 1], z_peers[ZN - 1 - k], 3 + k
        )

    def bias_turn():
        for k in (1, 2, 3, 0):
            bias_y(k).wait_recv()
            bias_part[behind(k) * YN + y] += bias_recv_y[k]
            if k:
                out.go(bias_z(k))

    def close_bias():
        total = bias_part[z * YN + y].astype(F32)
        for k in range(1, ZN):
            bias_z(k).wait_recv()
            total = total + bias_recv_z[k - 1].astype(F32)
        bias_hop[0] = jnp.dot(
            total, flip, precision=lax.Precision.HIGHEST, preferred_element_type=F32
        )

    def hop_copy():
        owner = mp * GROUPS + group
        return pltpu.make_async_remote_copy(
            src_ref=bias_hop.at[0],
            dst_ref=bias_hop.at[1],
            send_sem=bias_send.at[7],
            recv_sem=bias_recv.at[7],
            device_id=(owner // 4, inner, owner % 4),
            device_id_type=MESH,
        )

    def reduce_stats():
        def copy(step, slot, peer):
            return pltpu.make_async_remote_copy(
                src_ref=stats.at[step],
                dst_ref=stats_recv.at[slot],
                send_sem=stat_send.at[slot],
                recv_sem=stat_recv.at[slot],
                device_id=peer,
                device_id_type=MESH,
            )

        return copy

    def stats_step(step):
        copy = reduce_stats()
        peer = (core_peer, x_peer, y_peer)[step]
        copy(step, step, peer).wait_recv()
        stats[step + 1] = stats[step] + stats_recv[step]

    def stats_send(step):
        copy = reduce_stats()
        if step < 3:
            out.go(copy(step, step, (core_peer, x_peer, y_peer)[step]))
        else:
            for k in range(1, ZN):
                out.go(copy(3, 2 + k, z_peers[k - 1]))

    def stats_end():
        copy = reduce_stats()
        total = stats[3]
        for k in range(1, ZN):
            copy(3, 2 + k, z_peers[k - 1]).wait_recv()
            total = total + stats_recv[2 + k]
        stat_ref[...] = total

    def halo_start():
        pl.when(mp < 3)(halo_copy.start)

    def repack_all():
        for p in (0, 1):
            gather_core(p)
        loop_rows(GROUPS * rows, rows, repack)

    def halo_work():
        pl.when(mp > 0)(halo_copy.wait_recv)

        @pl.when(mp == 0)
        def _():
            x_halo[...] = jnp.zeros_like(x_halo)

        norm_halo(0)
        project_halo(0)

    def bands_work():
        gather_core(2)
        build_bands()

    def slab(r):
        return x_of(r // 2) * 2 + (1 - c if r % 2 else c)

    def hidden(r, part):
        if r % 2 and part == 0:
            for p in (3, 4):
                gather_core(p, (r - 1, r))
        hidden_rows(slab(r), r == 1)(part * CHUNK)

    def hidden_grad(r, part):
        if part == 0:
            if r % 2 == 0:
                out.drain("far" if r else "near")
            weight_grad(up_w.at[slab(r)], normed_two, dpre)
        else:
            weight_grad(down_w.at[slab(r)], cot_low, act)

    def unpack_pair(part):
        out.drain("mix")
        loop_rows(GROUPS * rows, rows, unpack(((0, 3), (1, 2))[part], 2 * part))

    def sum_send(p, far):
        core_sum(p, far)
        y_send(p, far)

    def unskew_all():
        for j in range(GROUPS):
            unskew(j)

    def bias_start():
        for k in (1, 2, 3, 0):
            out.go(bias_y(k))

    def bias_close():
        close_bias()
        if last_hop:

            @pl.when(moves)
            def _():
                hop_copy().start()

    def bias_end():
        if last_hop:

            @pl.when(moves)
            def _():
                hop_copy().wait_recv()
                gb_ref[...] = bias_hop[1]

            @pl.when(jnp.logical_not(moves))
            def _():
                gb_ref[...] = bias_hop[0]

        else:
            gb_ref[...] = bias_hop[0]

    actions = {
        "send_z": start_z,
        "send_y": start_y,
        "send_x": start_x,
        "send_c": start_core,
        "z": gather_z,
        "y": gather_y,
        "x": gather_x,
        "d": gather_last,
        "halo": halo_start,
        "norm": lambda: loop_rows(tokens, CHUNK, norm_own),
        "repack": repack_all,
        "proj": lambda q: project_own(q * CHUNK),
        "halow": halo_work,
        "bands": bands_work,
        "mix": mix_rows,
        "att": lambda q: attend(q * CHUNK),
        "h": hidden,
        "g": hidden_grad,
        "close": lambda q: close_hidden(q * CHUNK),
        "ba": lambda q: back_attend(q * CHUNK),
        "hb": halo_return,
        "bh": back_halo,
        "gout": lambda: weight_grad(full_w.at[3], act, mixed),
        "mg": mix_grad,
        "unpack": unpack_pair,
        "bk": back_keys,
        "bg": band_grad,
        "unsk": unskew_all,
        "bi": lambda q: back_input(q * CHUNK),
        "cs": core_send,
        "sum": sum_send,
        "yt": lambda p, k: y_take(p, 0, k),
        "yx": y_turn,
        "xe": x_end,
        "zt": z_take,
        "by": bias_start,
        "bt": bias_turn,
        "bc": bias_close,
        "hopw": bias_end,
        "ss": stats_send,
        "sw": stats_step,
        "se": stats_end,
    }
    for name, *args in SCHEDULE:
        actions[name](*args)

    @pl.when(mp < 3)
    def _():
        halo_copy.wait_send()

    pl.when(mp > 0)(halo_back().wait_send)

    if last_hop:

        @pl.when(moves)
        def _():
            hop_copy().wait_send()

    out.drain()


def run_block(lengths, x, cot, gains, wq, wo, wu, wd, bias, last_hop):
    tokens, width = x.shape
    window = bias.shape[1]
    rows = wu.shape[0]
    full = rows * GROUPS
    mix_width = 4 * wq.shape[2]
    hidden = wu.shape[1]
    lanes = mix_width + 2 * hidden
    vmem = pl.BlockSpec(memory_space=pltpu.VMEM)

    def shape(*dims, kind=F32):
        return jax.ShapeDtypeStruct(dims, kind)

    def buf(*dims):
        return pltpu.VMEM(dims, F32)

    def low(*dims):
        return pltpu.VMEM(dims, BF)

    dma = pltpu.SemaphoreType.DMA
    return pl.pallas_call(
        functools.partial(block_kernel, last_hop),
        out_shape=(
            shape(tokens, width, kind=BF),
            shape(tokens, width),
            shape(*wq.shape),
            shape(*wo.shape),
            shape(*wu.shape),
            shape(*wd.shape),
            shape(*bias.shape),
            shape(8, width),
        ),
        in_specs=[pl.BlockSpec(memory_space=pltpu.SMEM)] + [vmem] * 8,
        out_specs=(vmem,) * 8,
        scratch_shapes=[
            low(4, full, mix_width),
            low(4, full, hidden),
            low(4, full, hidden),
            low(4 * GROUPS, *bias.shape),
            low(window, width),
            low(4, full, width),
            low(window + tokens, width),
            buf(5 * tokens, width),
            buf(tokens, width),
            low(window + tokens, width),
            low(window + tokens, width),
            low(2, window, 2 * window),
            low(tokens, width),
            low(tokens, width),
            low(tokens, width),
            low(tokens, hidden),
            low(tokens, hidden),
            buf(tokens, width),
            low(tokens, width),
            low(tokens, width),
            low(window, width),
            low(window, width),
            low(window, width),
            low(GROUPS, *bias.shape),
            low(ZN, *bias.shape),
            low(ZN - 1, *bias.shape),
            buf(2, *bias.shape),
            buf(4, 8, width),
            buf(6, 8, width),
            low(2, full, 2 * hidden),
            low(GROUPS, rows, lanes),
            low(ZN, rows, lanes),
            low(ZN - 1, rows, lanes),
            dma((5, 32)),
            dma((5, 32)),
            dma((4, 17)),
            dma((4, 17)),
            dma((2,)),
            dma((2,)),
            dma((8,)),
            dma((8,)),
            dma((6,)),
            dma((6,)),
        ],
        compiler_params=pltpu.CompilerParams(
            collective_id=0, has_side_effects=True, vmem_limit_bytes=63 * 1024 * 1024
        ),
    )(lengths, x, cot, gains, wq, wo, wu, wd, bias)


MESH = pl.DeviceIdType.MESH


def adam_kernel(scale, blk_ref, gin_ref, *refs):
    *refs, blk_out, gin_out, blk_held, gin_held, copied = refs
    taken = [
        pltpu.make_async_copy(blk_ref, blk_held, copied.at[0]),
        pltpu.make_async_copy(gin_ref, gin_held, copied.at[1]),
    ]
    given = [
        pltpu.make_async_copy(blk_held, blk_out, copied.at[2]),
        pltpu.make_async_copy(gin_held, gin_out, copied.at[3]),
    ]
    for item in taken:
        item.start()
    grads, refs = refs[:6], refs[6:]
    params, refs = refs[:6], refs[6:]
    firsts, refs = refs[:6], refs[6:]
    seconds, refs = refs[:6], refs[6:]
    out_grads, out_firsts, out_seconds, out_updates = (
        refs[6 * i : 6 * i + 6] for i in range(4)
    )
    rms_ref = refs[24]
    one = 1.0 / (1.0 - BETA_ONE**ADAM_STEP)
    two = 1.0 / (1.0 - BETA_TWO**ADAM_STEP)

    def step(i):
        if i == 4:
            grad = grads[4][...] * jnp.exp(params[4][...])
        elif i == 5:
            grad = grads[5][0:2]
        else:
            grad = grads[i][...]
        grad = grad * scale
        first = BETA_ONE * firsts[i][...] + (1.0 - BETA_ONE) * grad
        second = BETA_TWO * seconds[i][...] + (1.0 - BETA_TWO) * (grad * grad)
        change = (first * one) / (jnp.sqrt(second * two) + ADAM_EPS)
        if i < 4:
            change = change + WEIGHT_DECAY * params[i][...]
        out_grads[i][...] = grad
        out_firsts[i][...] = first
        out_seconds[i][...] = second
        out_updates[i][...] = -LEARN_RATE * change

    for i in range(6):
        if i == 2:
            for item, onward in zip(taken, given, strict=True):
                item.wait()
                onward.start()
        step(i)
    sums = jnp.sum(grads[5][...], axis=1, keepdims=True)
    rms = jnp.sqrt(sums[2:5] / sums[5:6])
    for i in range(3):
        rms_ref[i] = jnp.sum(rms[i : i + 1, :])

    for item in given:
        item.wait()


def run_adam(scale, blk, gin, grads, params, firsts, seconds):
    kinds = [jax.ShapeDtypeStruct(param.shape, F32) for param in params]
    vmem = pl.BlockSpec(memory_space=pltpu.VMEM)
    anywhere = pl.BlockSpec(memory_space=pl.ANY)
    passed = [jax.ShapeDtypeStruct(item.shape, item.dtype) for item in (blk, gin)]
    return pl.pallas_call(
        functools.partial(adam_kernel, scale),
        out_shape=(*(kinds * 4), jax.ShapeDtypeStruct((3,), F32), *passed),
        in_specs=[anywhere] * 2 + [vmem] * 24,
        out_specs=(*[vmem] * 24, pl.BlockSpec(memory_space=pltpu.SMEM), anywhere, anywhere),
        scratch_shapes=[
            pltpu.VMEM(blk.shape, blk.dtype),
            pltpu.VMEM(gin.shape, gin.dtype),
            pltpu.SemaphoreType.DMA((4,)),
        ],
        compiler_params=pltpu.CompilerParams(vmem_limit_bytes=62 * 1024 * 1024),
    )(blk, gin, *grads, *params, *firsts, *seconds)


def stored(items):
    qkv, mix, up, down, bias, gains = items
    return [qkv.transpose(1, 0, 2), mix, up, down.T, bias, gains]


def shards(inner, block_input, out_cotangent, lengths, *rest):
    params, firsts, seconds = (stored(rest[6 * i : 6 * i + 6]) for i in range(3))
    held = params
    if inner > 1:
        axes = (1, 1, 0, 0)
        held = [
            lax.all_gather(item.astype(BF), "dpl", axis=axis, tiled=True).astype(F32)
            for item, axis in zip(params[:4], axes, strict=True)
        ]
        count = params[4].shape[0]
        every = lax.all_gather(params[4], ("dpl", "mp"), axis=0, tiled=True)
        at = lax.axis_index("mp") * inner * count
        held += [lax.dynamic_slice_in_dim(every, at, inner * count, 0), params[5]]
    block_low, grad_input, *grads = run_block(
        lengths,
        block_input[0],
        out_cotangent[0],
        held[5],
        *held[:5],
        inner == 1,
    )
    if inner > 1:
        for i, axis in enumerate(axes):
            grads[i] = lax.psum_scatter(grads[i], "dpl", scatter_dimension=axis, tiled=True)
        grads[4], grads[5] = lax.psum((grads[4], grads[5]), "dpl")
        every = lax.all_gather(grads[4], ("mp", "dph"), axis=0, tiled=True)
        place = lax.axis_index(("dph", "dpl", "mp"))
        grads[4] = lax.dynamic_slice_in_dim(every, place * count, count, 0)
    scale = float(lax.axis_size("dph") * inner * LEN) ** (-0.5)
    *results, rms_stats, block_low, grad_input = run_adam(
        scale, block_low, grad_input, grads, params, firsts, seconds
    )
    outs = []
    for i in range(4):
        qkv, mix, up, down, bias, gains = results[6 * i : 6 * i + 6]
        outs += [qkv.transpose(1, 0, 2), mix, up, down.T, bias, gains]
    return (block_low[None], grad_input[None], *outs, rms_stats)


def solution(mesh):
    inner = mesh.shape["dp"] // GROUPS
    fine = Mesh(
        mesh.devices.reshape(GROUPS, inner, mesh.shape["mp"]),
        ("dph", "dpl", "mp"),
    )
    dp = ("dph", "dpl")
    weights = (
        P(dp, None, "mp"),
        P("mp", dp),
        P(dp, "mp"),
        P("mp", dp),
        P((*dp, "mp"), None),
        P(),
    )
    acts = P(dp, "mp", None)
    return jax.shard_map(
        functools.partial(shards, inner),
        mesh=fine,
        in_specs=(acts, acts, P(dp), *weights, *weights, *weights),
        out_specs=(acts, acts, *weights, *weights, *weights, *weights, P()),
        check_vma=False,
    )
```

```python
import functools

import jax
import jax.numpy as jnp
from jax import lax
from jax.experimental import pallas as pl
from jax.experimental.pallas import tpu as pltpu
from jax.sharding import Mesh
from jax.sharding import PartitionSpec as P

LEN = 2048
ADAM_STEP = 10
EPS = 1e-06
BETA_ONE = 0.9
BETA_TWO = 0.99
LEARN_RATE = 0.03
WEIGHT_DECAY = 0.1
ADAM_EPS = 1e-08

F32 = jnp.float32
BF = jnp.bfloat16
ZN, YN = 4, 2
GROUPS = ZN * YN
CHUNK = 256
GELU_C = 0.7978845608028654
GELU_A = 0.044715


ROUTES = ((True, False), (False, False), (False, False), (True, False), (False, True))
LINE_SUMS = (False, False, False, True)
SCHEDULE = (
    ("send_z", 0), ("send_c", 1), ("send_x", 0), ("send_x", 1), ("send_y", 2), ("send_z", 1),
    ("send_x", 3), ("send_y", 0), ("send_x", 2), ("send_y", 3), ("x", 0, 0), ("y", 0, 0),
    ("z", 1, 1), ("send_y", 1), ("x", 1, 0), ("send_z", 2), ("z", 0, 1), ("z", 0, 2),
    ("z", 0, 3), ("z", 1, 2), ("z", 1, 3), ("send_z", 4), ("y", 3, 0), ("x", 1, 1), ("norm",),
    ("y", 2, 0), ("z", 2, 1), ("send_c", 0), ("send_y", 4), ("x", 3, 0), ("z", 2, 2),
    ("y", 1, 0), ("y", 1, 1), ("x", 1, 2), ("send_c", 3), ("d", 0, 0), ("send_z", 3),
    ("x", 0, 1), ("y", 0, 1), ("y", 0, 2), ("y", 1, 2), ("x", 0, 2), ("z", 2, 3), ("send_x", 4),
    ("z", 3, 1), ("d", 3, 0), ("z", 4, 1), ("x", 0, 3), ("d", 1, 0), ("d", 1, 1), ("send_c", 4),
    ("y", 2, 1), ("y", 2, 2), ("y", 0, 3), ("halo",), ("y", 4, 0), ("x", 2, 0), ("x", 2, 1),
    ("x", 1, 3), ("z", 3, 2), ("x", 2, 2), ("x", 2, 3), ("y", 2, 3), ("y", 1, 3), ("d", 1, 2),
    ("d", 0, 1), ("d", 0, 2), ("z", 4, 2), ("z", 4, 3), ("y", 3, 1), ("z", 3, 3), ("y", 3, 2),
    ("send_c", 2), ("d", 2, 0), ("d", 2, 1), ("d", 1, 3), ("d", 2, 2), ("d", 2, 3), ("d", 0, 3),
    ("x", 3, 1), ("bands",), ("repack",), ("proj", 0), ("proj", 1), ("x", 4, 0), ("y", 4, 1),
    ("y", 4, 2), ("halow",), ("y", 4, 3), ("x", 4, 1), ("mix", 0), ("mix", 1), ("att", 0),
    ("x", 3, 2), ("y", 3, 3), ("att", 1), ("h", 1, 0), ("h", 1, 1), ("d", 4, 0), ("g", 1, 0),
    ("g", 1, 1), ("cs", 2, 0), ("cs", 3, 0), ("h", 0, 0), ("h", 0, 1), ("g", 0, 0), ("d", 4, 1),
    ("sum", 2, 0), ("d", 4, 2), ("g", 0, 1), ("x", 4, 2), ("x", 4, 3), ("d", 3, 1), ("d", 3, 2),
    ("d", 3, 3), ("sum", 3, 0), ("x", 3, 3), ("d", 4, 3), ("h", 3, 0), ("h", 3, 1),
    ("yt", 2, 1), ("g", 3, 0), ("cs", 2, 1), ("g", 3, 1), ("cs", 3, 1), ("h", 2, 0),
    ("h", 2, 1), ("g", 2, 0), ("g", 2, 1), ("sum", 3, 1), ("close", 0), ("close", 1), ("ba", 0),
    ("sum", 2, 1), ("ba", 1), ("yt", 2, 2), ("yt", 2, 3), ("bh",), ("bg", 0), ("bg", 1),
    ("yt", 3, 1), ("xe", 3, 1), ("yt", 3, 2), ("xe", 3, 2), ("unsk",), ("hb",), ("by",),
    ("mg", 0), ("gout",), ("unpack", 0), ("cs", 0, 1), ("bk", 0), ("sum", 0, 1), ("yx", 2, 1),
    ("bk", 1), ("mg", 1), ("cs", 0, 0), ("yt", 3, 3), ("xe", 3, 3), ("yx", 2, 2), ("mg", 2),
    ("yx", 2, 3), ("unpack", 1), ("cs", 1, 1), ("sum", 1, 1), ("yx", 2, 0), ("bt",),
    ("sum", 0, 0), ("cs", 1, 0), ("yx", 3, 1), ("bi", 0), ("bi", 1), ("ss", 0), ("yx", 3, 2),
    ("yt", 2, 0), ("xe", 2, 1), ("xe", 2, 2), ("xe", 2, 3), ("sum", 1, 0), ("sw", 0), ("ss", 1),
    ("yx", 3, 3), ("yx", 3, 0), ("yx", 0, 1), ("yx", 0, 2), ("yx", 0, 3), ("yx", 0, 0),
    ("yt", 0, 1), ("xe", 0, 1), ("xe", 2, 0), ("yt", 0, 2), ("yt", 0, 3), ("sw", 1),
    ("yx", 1, 1), ("ss", 2), ("yx", 1, 2), ("yx", 1, 3), ("yt", 0, 0), ("xe", 0, 2),
    ("xe", 0, 3), ("xe", 0, 0), ("yx", 1, 0), ("bc",), ("yt", 1, 1), ("yt", 1, 2), ("xe", 1, 1),
    ("xe", 1, 2), ("sw", 2), ("hopw",), ("yt", 1, 3), ("yt", 1, 0), ("xe", 1, 3), ("ss", 3),
    ("zt", 2), ("yt", 3, 0), ("xe", 3, 0), ("zt", 3), ("zt", 0), ("xe", 1, 0), ("zt", 1),
    ("se",),
)


def dot_nn(a, b):
    return jnp.dot(a, b, preferred_element_type=F32)


def dot_nt(a, b):
    return lax.dot_general(a, b, (((1,), (1,)), ((), ())), preferred_element_type=F32)


def dot_tn(a, b):
    return lax.dot_general(a, b, (((0,), (0,)), ((), ())), preferred_element_type=F32)


def loop_rows(count, step, body, unroll=False):
    @pl.loop(0, count // step, unroll=unroll)
    def _(index):
        body(pl.multiple_of(index * step, step))


class Copies:
    def __init__(self):
        self.started = {}

    def go(self, copy, tag=None):
        copy.start()
        self.started.setdefault(tag, []).append(copy)

    def go_if(self, when, copy, tag=None):
        pl.when(when)(copy.start)
        self.started.setdefault(tag, []).append((when, copy))

    def drain(self, *tags):
        for tag in tags or list(self.started):
            for copy in self.started.pop(tag, []):
                if isinstance(copy, tuple):
                    pl.when(copy[0])(copy[1].wait_send)
                else:
                    copy.wait_send()


def block_kernel(
    last_hop,
    len_ref,
    x_ref,
    cot_ref,
    gains_ref,
    wq_ref,
    wo_ref,
    wu_ref,
    wd_ref,
    bias_ref,
    blk_ref,
    gin_ref,
    gq_ref,
    go_ref,
    gu_ref,
    gd_ref,
    gb_ref,
    stat_ref,
    mix_w,
    up_w,
    down_w,
    band_rows,
    x_halo,
    full_w,
    normed,
    wide_rows,
    resid,
    exp_low,
    kv_low,
    bands,
    mixed,
    normed_two,
    cot_low,
    act,
    dpre,
    dn_two,
    dnum,
    dden,
    dkey_halo,
    dval_halo,
    dnorm_recv,
    bias_part,
    bias_recv_y,
    bias_recv_z,
    bias_hop,
    stats,
    stats_recv,
    recv_core,
    recv_one,
    recv_two,
    recv_z,
    ag_send,
    ag_recv,
    rs_send,
    rs_recv,
    halo_send,
    halo_recv,
    bias_send,
    bias_recv,
    stat_send,
    stat_recv,
):
    tokens, width = x_ref.shape
    window = x_halo.shape[0]
    rows = wu_ref.shape[0]
    chan = width // 4
    ffn = gin_ref
    sig, ratio, rden, expk, val = (
        wide_rows.at[pl.ds(i * tokens, tokens)] for i in range(5)
    )
    group = lax.axis_index("dph")
    inner = lax.axis_index("dpl")
    mp = lax.axis_index("mp")
    z, y = group // YN, group % YN
    x, c = mp // 2, mp % 2

    def device(zs, ys, xs, cs):
        return (zs * YN + ys, inner, xs * 2 + cs)

    def z_at(k):
        return (z + k) % ZN

    core_peer = device(z, y, x, 1 - c)
    x_peer = device(z, y, 1 - x, c)
    y_peer = device(z, 1 - y, x, c)
    diag_peer = device(z, y, 1 - x, 1 - c)
    z_peers = [device(z_at(k), y, x, c) for k in range(1, ZN)]

    out = Copies()

    half = 2 * chan
    gather_pieces = [
        (mix_w, 0, half),
        (mix_w, half, half),
        (None, 0, 0),
        (up_w, 0, up_w.shape[2]),
        (down_w, 0, down_w.shape[2]),
    ]

    def place(piece, zs, ys, xs, cs):
        buf, start, size = gather_pieces[piece]
        if buf is None:
            return band_rows.at[(zs * YN + ys) * 4 + xs * 2 + cs]
        at = pl.multiple_of((zs * YN + ys) * rows, 32)
        return buf.at[xs * 2 + cs, pl.ds(at, rows), pl.ds(start, size)]

    def ag(piece, loc, peer, slot):
        ref = place(piece, *loc)
        return pltpu.make_async_remote_copy(
            src_ref=ref,
            dst_ref=ref,
            send_sem=ag_send.at[piece, slot],
            recv_sem=ag_recv.at[piece, slot],
            device_id=peer,
            device_id_type=MESH,
        )

    own = (z, y, x, c)

    def along(i):
        edge = jnp.where(z == 0, i, ZN - 1 - i)
        inside = jnp.where(z == 1, (1, 0, 2, 3)[i], (2, 1, 3, 0)[i])
        return jnp.where((z == 0) | (z == ZN - 1), edge, inside)

    order = [along(i) for i in range(ZN)]

    def spot(kind, zs):
        return (zs, y if kind in (0, 2) else 1 - y, x if kind in (0, 1) else 1 - x, c)

    def tag_of(piece, kind):
        return "mix" if piece < 3 else ("near" if kind < 2 else "far")

    def forward(piece, kind, zs, peer, slot, when=None):
        copy = ag(piece, spot(kind, zs), peer, slot)
        if piece == 2 and when is not None:
            out.go_if(when, copy, tag_of(piece, kind))
        else:
            out.go(copy, tag_of(piece, kind))

    def used_here(zs):
        return zs // 2 == x

    def to_core(piece, kind, i):
        zs = order[i]
        when = used_here(zs) & (zs % 2 != c)
        forward(piece, kind, zs, core_peer, 16 + kind * 4 + zs, when)

    def arrived(piece, slot, when=None):
        wait = ag(piece, own, core_peer, slot).wait_recv
        if piece == 2 and when is not None:
            pl.when(when)(wait)
        else:
            wait()

    def turns_y(piece):
        return ROUTES[piece][0]

    def pass_z(piece, kind, zs, step, when):
        peer = device(jnp.clip(z + step, 0, ZN - 1), y, x, c)
        copy = ag(piece, spot(kind, zs), peer, kind * 4 + zs)
        out.go_if(when, copy, tag_of(piece, kind))

    def start_line(piece, kind):
        pass_z(piece, kind, z, 1, z < ZN - 1)
        pass_z(piece, kind, z, -1, z > 0)

    def pass_line(piece, kind, zs):
        up = zs < z
        pass_z(piece, kind, zs, jnp.where(up, 1, -1), jnp.where(up, z < ZN - 1, z > 0))

    def start_z(piece):
        start_line(piece, 0)

    def start_y(piece):
        forward(piece, 0, z, y_peer, 4 + z, used_here(z))

    def start_x(piece):
        forward(piece, 0, z, x_peer, 8 + z, jnp.logical_not(used_here(z)))

    def start_core(piece):
        to_core(piece, 0, 0)

    def gather_z(piece, i):
        zs = order[i]
        arrived(piece, zs)
        pass_line(piece, 0, zs)
        forward(piece, 0, zs, y_peer, 4 + zs, used_here(zs))
        forward(piece, 0, zs, x_peer, 8 + zs, jnp.logical_not(used_here(zs)))
        to_core(piece, 0, i)

    def turns(piece, i):
        return not ROUTES[piece][1] or i == 0

    def gather_y(piece, i):
        zs = order[i]
        arrived(piece, 4 + zs, used_here(zs))
        if turns_y(piece) and turns(piece, i):
            forward(piece, 1, zs, x_peer, 12 + zs)
        to_core(piece, 1, i)

    def gather_x(piece, i):
        zs = order[i]
        arrived(piece, 8 + zs, used_here(zs))
        if not turns_y(piece) and turns(piece, i):
            forward(piece, 2, zs, y_peer, 12 + zs, used_here(zs))
        to_core(piece, 2, i)

    def gather_last(piece, i):
        zs = order[i]
        arrived(piece, 12 + zs, used_here(zs))
        if ROUTES[piece][1]:
            if i:
                pass_line(piece, 3, zs)
            else:
                start_line(piece, 3)
        to_core(piece, 3, i)

    def gather_core(piece, kinds=(0, 1, 2, 3)):
        for kind in kinds:
            for i in range(ZN):
                zs = order[i]
                arrived(piece, 16 + kind * 4 + zs, used_here(zs) & (zs % 2 == c))

    barrier = pltpu.get_barrier_semaphore()
    friends = [core_peer, x_peer, y_peer, diag_peer] + z_peers
    for friend in friends:
        pl.semaphore_signal(barrier, inc=1, device_id=friend, device_id_type=MESH)
    here = group * 4 + mp
    moves = here != mp * GROUPS + group
    if last_hop:

        @pl.when(moves)
        def _():
            pl.semaphore_signal(
                barrier,
                inc=1,
                device_id=(here % GROUPS, inner, here // GROUPS),
                device_id_type=MESH,
            )

    home = pl.ds(pl.multiple_of(group * rows, 32), rows)
    mix_w[mp, home, :] = jnp.concatenate(
        [wq_ref[0], wo_ref[...].T, wq_ref[1], wq_ref[2]], axis=1
    ).astype(BF)
    flip = (
        lax.broadcasted_iota(jnp.int32, (window, window), 0)
        + lax.broadcasted_iota(jnp.int32, (window, window), 1)
        == window - 1
    ).astype(F32)
    band_rows[group * 4 + mp] = dot_nn(
        jnp.exp(bias_ref[...]).astype(BF), flip.astype(BF)
    ).astype(BF)

    up_w[mp, home, :] = wu_ref[...].astype(BF)
    down_w[mp, home, :] = wd_ref[...].astype(BF)
    stats[0] = jnp.zeros(stats.shape[1:], F32)
    if last_hop:

        @pl.when(moves)
        def _():
            pl.semaphore_wait(barrier, len(friends) + 1)

        @pl.when(jnp.logical_not(moves))
        def _():
            pl.semaphore_wait(barrier, len(friends))

    else:
        pl.semaphore_wait(barrier, len(friends))

    halo_copy = pltpu.make_async_remote_copy(
        src_ref=x_ref.at[pl.ds(tokens - window, window)],
        dst_ref=x_halo,
        send_sem=halo_send.at[0],
        recv_sem=halo_recv.at[0],
        device_id=(group, inner, (mp + 1) % 4),
        device_id_type=MESH,
    )


    def add_stat(row, value):
        stats[0, row : row + 1, :] += jnp.sum(value, axis=0, keepdims=True)

    def rms(value):
        return lax.rsqrt(jnp.mean(value * value, axis=-1, keepdims=True) + EPS)

    def mask_at(at):
        spots = lax.broadcasted_iota(jnp.int32, (CHUNK, width), 0) + (at + mp * tokens)
        return (spots < len_ref[0]).astype(F32)

    def norm_own(at):
        part = pl.ds(at, CHUNK)
        xf = x_ref[part].astype(F32)
        normed[pl.ds(at + window, CHUNK)] = (xf * rms(xf) * gains_ref[0:1]).astype(BF)
        mask = mask_at(at)
        add_stat(2, mask * xf * xf)
        add_stat(5, mask)
        cot_low[part] = (cot_ref[part].astype(F32) * mask).astype(BF)

    def norm_halo(at):
        part = pl.ds(at, CHUNK)
        xf = x_halo[part].astype(F32)
        normed[part] = (xf * rms(xf) * gains_ref[0:1]).astype(BF)

    def repack(at):
        part = pl.ds(at, rows)
        for kind, at in ((0, 0), (3, 1), (1, 2), (2, 3)):
            full_w[kind, part] = jnp.concatenate(
                [mix_w[m, part, at * chan : (at + 1) * chan] for m in range(4)], axis=1
            )

    def project_halo(at):
        part = pl.ds(at, CHUNK)
        a = normed[part]
        ek = jnp.where(mp > 0, jnp.exp(dot_nn(a, full_w[1])), 0.0)
        exp_low[part] = ek.astype(BF)
        kv_low[part] = (ek * dot_nn(a, full_w[2])).astype(BF)

    def project_own(at):
        part = pl.ds(at, CHUNK)
        shifted = pl.ds(at + window, CHUNK)
        a = normed[shifted]
        ek = jnp.exp(dot_nn(a, full_w[1]))
        v = dot_nn(a, full_w[2])
        exp_low[shifted] = ek.astype(BF)
        kv_low[shifted] = (ek * v).astype(BF)
        expk[part] = ek
        val[part] = v
        sig[part] = jax.nn.sigmoid(dot_nn(a, full_w[0]))

    def build_bands():
        for i in range(2):
            raw = band_rows[pl.ds(mp * 8 + i * 4, 4)].reshape(window, window).astype(F32)
            wide = jnp.concatenate([raw, jnp.zeros_like(raw)], axis=1)
            bands[i] = pltpu.roll(wide, 1, 1, stride=1, stride_axis=0).astype(BF)

    def mix_rows(i):
        part = slice(i * window, (i + 1) * window)
        near = slice(i * window, (i + 2) * window)
        num = dot_nn(bands[i], kv_low[near])
        den = dot_nn(bands[i], exp_low[near])
        ratio[part] = num / den
        rden[part] = 1.0 / den

    def attend(at):
        part = pl.ds(at, CHUNK)
        low = (sig[part] * ratio[part]).astype(BF)
        mixed[part] = low
        attn = dot_nt(low, full_w[3])
        add_stat(3, mask_at(at) * attn * attn)
        total = x_ref[part].astype(F32) + attn
        resid[part] = total
        normed_two[part] = (total * rms(total) * gains_ref[1:2]).astype(BF)

    def hidden_rows(m, first):
        def body(at):
            part = pl.ds(at, CHUNK)
            p = dot_nn(normed_two[part], up_w[m])
            da = dot_nn(cot_low[part], down_w[m])
            square = p * p
            t = jnp.tanh(p * (GELU_C + GELU_C * GELU_A * square))
            gate = 0.5 + 0.5 * t
            value = p * gate
            slope = gate + value * (1.0 - gate) * (
                2.0 * GELU_C + 6.0 * GELU_C * GELU_A * square
            )
            low = value.astype(BF)
            dlow = (da * slope).astype(BF)
            act[part] = low
            dpre[part] = dlow
            f = dot_nt(low, down_w[m])
            d = dot_nt(dlow, up_w[m])
            if first:
                ffn[part] = f
                dn_two[part] = d
            else:
                ffn[part] += f
                dn_two[part] += d

        return body

    def weight_grad(result, left, right, left_more=None, right_more=None):
        for at in range(0, result.shape[1], 256):
            part = slice(at, at + 256)
            total = dot_tn(left[...], right[:, part])
            if right_more is not None:
                total = total + dot_tn(left_more[0:window], right_more[:, part])
            result[:, part] = total.astype(result.dtype)

    def close_hidden(at):
        part = pl.ds(at, CHUNK)
        mask = mask_at(at)
        f = ffn[part]
        res = resid[part]
        add_stat(4, mask * f * f)
        blk_ref[part] = (res + f).astype(BF)
        d = dn_two[part]
        r = rms(res)
        u = gains_ref[1:2] * d
        grad = (
            cot_ref[part].astype(F32) * mask
            + r * u
            - res * (r * r * r) * jnp.mean(u * res, axis=-1, keepdims=True)
        )
        add_stat(1, d * res * r)
        ffn[part] = grad
        act[part] = grad.astype(BF)

    def back_attend(at):
        part = pl.ds(at, CHUNK)
        dm = dot_nn(act[part], full_w[3])
        sg = sig[part]
        rt = ratio[part]
        scaled = dm * sg
        normed_two[part] = (scaled * rt * (1.0 - sg)).astype(BF)
        dn = scaled * rden[part]
        dnum[part] = dn.astype(BF)
        dden[part] = (-dn * rt).astype(BF)

    def halo_back():
        return pltpu.make_async_remote_copy(
            src_ref=x_halo,
            dst_ref=dnorm_recv,
            send_sem=halo_send.at[1],
            recv_sem=halo_recv.at[1],
            device_id=(group, inner, (mp + 3) % 4),
            device_id_type=MESH,
        )

    def band_grad(i):
        part = slice(i * window, (i + 1) * window)
        near = slice(i * window, (i + 2) * window)
        dn_two[part, 0 : 2 * window] = dot_nt(dnum[part], kv_low[near]) + dot_nt(dden[part], exp_low[near])

    def unskew(j):
        wide = 2 * window
        count = bias_part.shape[1]
        line = lax.broadcasted_iota(jnp.int32, (count, wide), 0)
        v = dn_two[j * count : (j + 1) * count, 0:wide]
        v = pltpu.roll(v, wide - 1 - (j * count) % window, 1)
        bit = 1
        while bit < count:
            v = jnp.where((line & bit) != 0, pltpu.roll(v, wide - bit, 1), v)
            bit *= 2
        bias_part[j] = v[:, 0:window].astype(BF)

    def back_keys(j):
        here = slice(j * window, (j + 1) * window)
        right = bands[j, :, window:]
        dkv = dot_tn(right, dnum[here])
        de = dot_tn(right, dden[here])
        if j == 0:
            then = slice(window, 2 * window)
            left = bands[1, :, :window]
            dkv = dkv + dot_tn(left, dnum[then])
            de = de + dot_tn(left, dden[then])
        ek = expk[here]
        cot_low[here] = (dkv * ek).astype(BF)
        dpre[here] = ((de + dkv * val[here]) * ek).astype(BF)

    def back_halo():
        before = slice(0, window)
        left = bands[0, :, :window]
        dkv = dot_tn(left, dnum[before])
        de = dot_tn(left, dden[before])
        ek = exp_low[before].astype(F32)
        dval_halo[...] = (dkv * ek).astype(BF)
        dkey_halo[...] = (de * ek + dkv * kv_low[before].astype(F32)).astype(BF)

    def halo_return():
        x_halo[...] = (
            dot_nt(dkey_halo[...], full_w[1]) + dot_nt(dval_halo[...], full_w[2])
        ).astype(BF)
        pl.when(mp > 0)(halo_back().start)

    def back_input(at):
        part = pl.ds(at, CHUNK)
        d = (
            dot_nt(normed_two[part], full_w[0])
            + dot_nt(dpre[part], full_w[1])
            + dot_nt(cot_low[part], full_w[2])
        )
        if at:
            pl.when(mp < 3)(halo_back().wait_recv)

            @pl.when(mp == 3)
            def _():
                dnorm_recv[...] = jnp.zeros_like(dnorm_recv)

            d = d + dnorm_recv[...].astype(F32)
        xf = x_ref[part].astype(F32)
        r = rms(xf)
        u = gains_ref[0:1] * d
        gin_ref[part] = (
            ffn[part] + r * u - xf * (r * r * r) * jnp.mean(u * xf, axis=-1, keepdims=True)
        )
        add_stat(0, d * xf * r)

    def mix_grad(kind):
        grad = (normed_two, dpre, cot_low)[kind]
        result = wide_rows.at[pl.ds(kind * GROUPS * rows, GROUPS * rows)]
        left = normed.at[pl.ds(window, tokens)]
        if kind == 0:
            weight_grad(result, left, grad)
        else:
            weight_grad(result, left, grad, normed, (dkey_halo, dval_halo)[kind - 1])

    def unpack(kinds, first):
        def body(at):
            part = pl.ds(at, rows)
            for m in range(4):
                mine = slice(m * chan, (m + 1) * chan)
                pair = [
                    full_w[3, part, mine]
                    if kind == 3
                    else wide_rows[pl.ds(at + kind * GROUPS * rows, rows), mine].astype(BF)
                    for kind in kinds
                ]
                span = slice(first * chan, (first + 2) * chan)
                mix_w[m, part, span] = jnp.concatenate(pair, axis=1)

        return body

    scatter_pieces = [
        (mix_w, 0, half, None, 0),
        (mix_w, half, half, None, half),
        (up_w, 0, up_w.shape[2], gu_ref, 2 * half),
        (down_w, 0, down_w.shape[2], gd_ref, 2 * half + up_w.shape[2]),
    ]

    def rs(piece, src, dst, peer, slot):
        return pltpu.make_async_remote_copy(
            src_ref=src,
            dst_ref=dst,
            send_sem=rs_send.at[piece, slot],
            recv_sem=rs_recv.at[piece, slot],
            device_id=peer,
            device_id_type=MESH,
        )

    def x_of(far):
        return 1 - x if far else x

    def block(piece, xs, zs, ys):
        buf, start, size = scatter_pieces[piece][:3]
        at = pl.multiple_of((zs * YN + ys) * rows, 32)
        return buf.at[xs * 2 + c, pl.ds(at, rows), pl.ds(start, size)]

    def lanes(piece):
        return pl.ds(scatter_pieces[piece][4], scatter_pieces[piece][2])

    def core_landing(p, far):
        if p < 2:
            return recv_core.at[0, :, pl.ds((far * 2 + p) * half, half)]
        return recv_core.at[far, :, pl.ds((p - 2) * up_w.shape[2], up_w.shape[2])]

    def core_copy(p, far):
        buf, start, size = scatter_pieces[p][:3]
        src = buf.at[x_of(far) * 2 + 1 - c, :, pl.ds(start, size)]
        return rs(p, src, core_landing(p, far), core_peer, far)

    def core_send(p, far):
        out.go(core_copy(p, far))

    def core_sum(p, far):
        buf, start, size = scatter_pieces[p][:3]
        core_copy(p, far).wait_recv()
        landed = core_landing(p, far)

        def body(at):
            part = pl.ds(at, rows)
            buf[x_of(far) * 2 + c, part, pl.ds(start, size)] += landed[part]

        loop_rows(GROUPS * rows, rows, body)

    def behind(k):
        return (z + ZN - k) % ZN

    def y_copy(p, far, k):
        src = block(p, x_of(far), behind(k), 1 - y)
        return rs(p, src, recv_one.at[far * ZN + k, :, lanes(p)], y_peer, 2 + far * ZN + k)

    def line_copy(p, k):
        src = block(p, 1 - x, behind(k), 1 - y)
        landing = recv_one.at[ZN + k, :, lanes(p)]
        return rs(p, src, landing, z_peers[ZN - 1 - k], 2 + ZN + k)

    def cross_copy(p):
        src = block(p, 1 - x, z, 1 - y)
        return rs(p, src, recv_one.at[ZN, :, lanes(p)], x_peer, 2 + ZN)

    def y_send(p, far):
        if not LINE_SUMS[p]:
            for k in (1, 2, 3, 0):
                out.go(y_copy(p, far, k))
        elif far:
            for k in (1, 2, 3):
                out.go(line_copy(p, k))
            for k in (1, 2, 3, 0):
                out.go(x_copy(p, k))
        else:
            for k in (1, 2, 3):
                out.go(y_copy(p, far, k))

    def line_take(p, k):
        if k:
            line_copy(p, k).wait_recv()
            spot_ref = block(p, 1 - x, z, 1 - y)
            spot_ref[...] += recv_one[ZN + k, :, lanes(p)]
            if k == 3:
                out.go(cross_copy(p))
        else:
            cross_copy(p).wait_recv()
            spot_ref = block(p, x, z, 1 - y)
            spot_ref[...] += recv_one[ZN, :, lanes(p)]
            out.go(y_copy(p, 0, 0))

    def y_take(p, far, k):
        y_copy(p, far, k).wait_recv()
        spot_ref = block(p, x_of(far), behind(k), y)
        spot_ref[...] += recv_one[far * ZN + k, :, lanes(p)]

    def x_copy(p, k):
        src = block(p, 1 - x, behind(k), y)
        return rs(p, src, recv_two.at[k, :, lanes(p)], x_peer, 10 + k)

    def x_take(p, k):
        x_copy(p, k).wait_recv()
        spot_ref = block(p, x, behind(k), y)
        spot_ref[...] += recv_two[k, :, lanes(p)]

    def z_copy(p, k):
        src = block(p, x, behind(k), y)
        return rs(p, src, recv_z.at[k - 1, :, lanes(p)], z_peers[ZN - 1 - k], 13 + k)

    def z_take(p):
        total = block(p, x, z, y)[...].astype(F32)
        for k in range(1, ZN):
            z_copy(p, k).wait_recv()
            total = total + recv_z[k - 1, :, lanes(p)].astype(F32)
        if p == 0:
            gq_ref[0] = total[:, :chan]
            go_ref[...] = total[:, chan:].T
        elif p == 1:
            gq_ref[1] = total[:, :chan]
            gq_ref[2] = total[:, chan:]
        else:
            scatter_pieces[p][3][...] = total

    def y_turn(p, k):
        if LINE_SUMS[p]:
            line_take(p, k)
        else:
            y_take(p, 1, k)
            out.go(x_copy(p, k))

    def x_end(p, k):
        x_take(p, k)
        if k:
            out.go(z_copy(p, k))

    def bias_copy(src, dst, peer, slot):
        return pltpu.make_async_remote_copy(
            src_ref=src,
            dst_ref=dst,
            send_sem=bias_send.at[slot],
            recv_sem=bias_recv.at[slot],
            device_id=peer,
            device_id_type=MESH,
        )

    def bias_y(k):
        return bias_copy(
            bias_part.at[behind(k) * YN + 1 - y], bias_recv_y.at[k], y_peer, k
        )

    def bias_z(k):
        return bias_copy(
            bias_part.at[behind(k) * YN + y], bias_recv_z.at[k - 1], z_peers[ZN - 1 - k], 3 + k
        )

    def bias_turn():
        for k in (1, 2, 3, 0):
            bias_y(k).wait_recv()
            bias_part[behind(k) * YN + y] += bias_recv_y[k]
            if k:
                out.go(bias_z(k))

    def close_bias():
        total = bias_part[z * YN + y].astype(F32)
        for k in range(1, ZN):
            bias_z(k).wait_recv()
            total = total + bias_recv_z[k - 1].astype(F32)
        bias_hop[0] = jnp.dot(
            total, flip, precision=lax.Precision.HIGHEST, preferred_element_type=F32
        )

    def hop_copy():
        owner = mp * GROUPS + group
        return pltpu.make_async_remote_copy(
            src_ref=bias_hop.at[0],
            dst_ref=bias_hop.at[1],
            send_sem=bias_send.at[7],
            recv_sem=bias_recv.at[7],
            device_id=(owner // 4, inner, owner % 4),
            device_id_type=MESH,
        )

    def reduce_stats():
        def copy(step, slot, peer):
            return pltpu.make_async_remote_copy(
                src_ref=stats.at[step],
                dst_ref=stats_recv.at[slot],
                send_sem=stat_send.at[slot],
                recv_sem=stat_recv.at[slot],
                device_id=peer,
                device_id_type=MESH,
            )

        return copy

    def stats_step(step):
        copy = reduce_stats()
        peer = (core_peer, x_peer, y_peer)[step]
        copy(step, step, peer).wait_recv()
        stats[step + 1] = stats[step] + stats_recv[step]

    def stats_send(step):
        copy = reduce_stats()
        if step < 3:
            out.go(copy(step, step, (core_peer, x_peer, y_peer)[step]))
        else:
            for k in range(1, ZN):
                out.go(copy(3, 2 + k, z_peers[k - 1]))

    def stats_end():
        copy = reduce_stats()
        total = stats[3]
        for k in range(1, ZN):
            copy(3, 2 + k, z_peers[k - 1]).wait_recv()
            total = total + stats_recv[2 + k]
        stat_ref[...] = total

    def halo_start():
        pl.when(mp < 3)(halo_copy.start)

    def repack_all():
        for p in (0, 1):
            gather_core(p)
        loop_rows(GROUPS * rows, rows, repack)

    def halo_work():
        pl.when(mp > 0)(halo_copy.wait_recv)

        @pl.when(mp == 0)
        def _():
            x_halo[...] = jnp.zeros_like(x_halo)

        norm_halo(0)
        project_halo(0)

    def bands_work():
        gather_core(2)
        build_bands()

    def slab(r):
        return x_of(r // 2) * 2 + (1 - c if r % 2 else c)

    def hidden(r, part):
        if r % 2 and part == 0:
            for p in (3, 4):
                gather_core(p, (r - 1, r))
        hidden_rows(slab(r), r == 1)(part * CHUNK)

    def hidden_grad(r, part):
        if part == 0:
            if r % 2 == 0:
                out.drain("far" if r else "near")
            weight_grad(up_w.at[slab(r)], normed_two, dpre)
        else:
            weight_grad(down_w.at[slab(r)], cot_low, act)

    def unpack_pair(part):
        out.drain("mix")
        loop_rows(GROUPS * rows, rows, unpack(((0, 3), (1, 2))[part], 2 * part))

    def sum_send(p, far):
        core_sum(p, far)
        y_send(p, far)

    def unskew_all():
        for j in range(GROUPS):
            unskew(j)

    def bias_start():
        for k in (1, 2, 3, 0):
            out.go(bias_y(k))

    def bias_close():
        close_bias()
        if last_hop:

            @pl.when(moves)
            def _():
                hop_copy().start()

    def bias_end():
        if last_hop:

            @pl.when(moves)
            def _():
                hop_copy().wait_recv()
                gb_ref[...] = bias_hop[1]

            @pl.when(jnp.logical_not(moves))
            def _():
                gb_ref[...] = bias_hop[0]

        else:
            gb_ref[...] = bias_hop[0]

    actions = {
        "send_z": start_z,
        "send_y": start_y,
        "send_x": start_x,
        "send_c": start_core,
        "z": gather_z,
        "y": gather_y,
        "x": gather_x,
        "d": gather_last,
        "halo": halo_start,
        "norm": lambda: loop_rows(tokens, CHUNK, norm_own),
        "repack": repack_all,
        "proj": lambda q: project_own(q * CHUNK),
        "halow": halo_work,
        "bands": bands_work,
        "mix": mix_rows,
        "att": lambda q: attend(q * CHUNK),
        "h": hidden,
        "g": hidden_grad,
        "close": lambda q: close_hidden(q * CHUNK),
        "ba": lambda q: back_attend(q * CHUNK),
        "hb": halo_return,
        "bh": back_halo,
        "gout": lambda: weight_grad(full_w.at[3], act, mixed),
        "mg": mix_grad,
        "unpack": unpack_pair,
        "bk": back_keys,
        "bg": band_grad,
        "unsk": unskew_all,
        "bi": lambda q: back_input(q * CHUNK),
        "cs": core_send,
        "sum": sum_send,
        "yt": lambda p, k: y_take(p, 0, k),
        "yx": y_turn,
        "xe": x_end,
        "zt": z_take,
        "by": bias_start,
        "bt": bias_turn,
        "bc": bias_close,
        "hopw": bias_end,
        "ss": stats_send,
        "sw": stats_step,
        "se": stats_end,
    }
    for name, *args in SCHEDULE:
        actions[name](*args)

    @pl.when(mp < 3)
    def _():
        halo_copy.wait_send()

    pl.when(mp > 0)(halo_back().wait_send)

    if last_hop:

        @pl.when(moves)
        def _():
            hop_copy().wait_send()

    out.drain()


def run_block(lengths, x, cot, gains, wq, wo, wu, wd, bias, last_hop):
    tokens, width = x.shape
    window = bias.shape[1]
    rows = wu.shape[0]
    full = rows * GROUPS
    mix_width = 4 * wq.shape[2]
    hidden = wu.shape[1]
    lanes = mix_width + 2 * hidden
    vmem = pl.BlockSpec(memory_space=pltpu.VMEM)

    def shape(*dims, kind=F32):
        return jax.ShapeDtypeStruct(dims, kind)

    def buf(*dims):
        return pltpu.VMEM(dims, F32)

    def low(*dims):
        return pltpu.VMEM(dims, BF)

    dma = pltpu.SemaphoreType.DMA
    return pl.pallas_call(
        functools.partial(block_kernel, last_hop),
        out_shape=(
            shape(tokens, width, kind=BF),
            shape(tokens, width),
            shape(*wq.shape),
            shape(*wo.shape),
            shape(*wu.shape),
            shape(*wd.shape),
            shape(*bias.shape),
            shape(8, width),
        ),
        in_specs=[pl.BlockSpec(memory_space=pltpu.SMEM)] + [vmem] * 8,
        out_specs=(vmem,) * 8,
        scratch_shapes=[
            low(4, full, mix_width),
            low(4, full, hidden),
            low(4, full, hidden),
            low(4 * GROUPS, *bias.shape),
            low(window, width),
            low(4, full, width),
            low(window + tokens, width),
            buf(5 * tokens, width),
            buf(tokens, width),
            low(window + tokens, width),
            low(window + tokens, width),
            low(2, window, 2 * window),
            low(tokens, width),
            low(tokens, width),
            low(tokens, width),
            low(tokens, hidden),
            low(tokens, hidden),
            buf(tokens, width),
            low(tokens, width),
            low(tokens, width),
            low(window, width),
            low(window, width),
            low(window, width),
            low(GROUPS, *bias.shape),
            low(ZN, *bias.shape),
            low(ZN - 1, *bias.shape),
            buf(2, *bias.shape),
            buf(4, 8, width),
            buf(6, 8, width),
            low(2, full, 2 * hidden),
            low(GROUPS, rows, lanes),
            low(ZN, rows, lanes),
            low(ZN - 1, rows, lanes),
            dma((5, 32)),
            dma((5, 32)),
            dma((4, 17)),
            dma((4, 17)),
            dma((2,)),
            dma((2,)),
            dma((8,)),
            dma((8,)),
            dma((6,)),
            dma((6,)),
        ],
        compiler_params=pltpu.CompilerParams(
            collective_id=0, has_side_effects=True, vmem_limit_bytes=63 * 1024 * 1024
        ),
    )(lengths, x, cot, gains, wq, wo, wu, wd, bias)


MESH = pl.DeviceIdType.MESH


def adam_kernel(scale, blk_ref, gin_ref, *refs):
    *refs, blk_out, gin_out, blk_held, gin_held, copied = refs
    taken = [
        pltpu.make_async_copy(blk_ref, blk_held, copied.at[0]),
        pltpu.make_async_copy(gin_ref, gin_held, copied.at[1]),
    ]
    given = [
        pltpu.make_async_copy(blk_held, blk_out, copied.at[2]),
        pltpu.make_async_copy(gin_held, gin_out, copied.at[3]),
    ]
    for item in taken:
        item.start()
    grads, refs = refs[:6], refs[6:]
    params, refs = refs[:6], refs[6:]
    firsts, refs = refs[:6], refs[6:]
    seconds, refs = refs[:6], refs[6:]
    out_grads, out_firsts, out_seconds, out_updates = (
        refs[6 * i : 6 * i + 6] for i in range(4)
    )
    rms_ref = refs[24]
    one = 1.0 / (1.0 - BETA_ONE**ADAM_STEP)
    two = 1.0 / (1.0 - BETA_TWO**ADAM_STEP)

    def step(i):
        if i == 4:
            grad = grads[4][...] * jnp.exp(params[4][...])
        elif i == 5:
            grad = grads[5][0:2]
        else:
            grad = grads[i][...]
        grad = grad * scale
        first = BETA_ONE * firsts[i][...] + (1.0 - BETA_ONE) * grad
        second = BETA_TWO * seconds[i][...] + (1.0 - BETA_TWO) * (grad * grad)
        change = (first * one) / (jnp.sqrt(second * two) + ADAM_EPS)
        if i < 4:
            change = change + WEIGHT_DECAY * params[i][...]
        out_grads[i][...] = grad
        out_firsts[i][...] = first
        out_seconds[i][...] = second
        out_updates[i][...] = -LEARN_RATE * change

    for i in range(6):
        if i == 2:
            for item, onward in zip(taken, given, strict=True):
                item.wait()
                onward.start()
        step(i)
    sums = jnp.sum(grads[5][...], axis=1, keepdims=True)
    rms = jnp.sqrt(sums[2:5] / sums[5:6])
    for i in range(3):
        rms_ref[i] = jnp.sum(rms[i : i + 1, :])

    for item in given:
        item.wait()


def run_adam(scale, blk, gin, grads, params, firsts, seconds):
    kinds = [jax.ShapeDtypeStruct(param.shape, F32) for param in params]
    vmem = pl.BlockSpec(memory_space=pltpu.VMEM)
    anywhere = pl.BlockSpec(memory_space=pl.ANY)
    passed = [jax.ShapeDtypeStruct(item.shape, item.dtype) for item in (blk, gin)]
    return pl.pallas_call(
        functools.partial(adam_kernel, scale),
        out_shape=(*(kinds * 4), jax.ShapeDtypeStruct((3,), F32), *passed),
        in_specs=[anywhere] * 2 + [vmem] * 24,
        out_specs=(*[vmem] * 24, pl.BlockSpec(memory_space=pltpu.SMEM), anywhere, anywhere),
        scratch_shapes=[
            pltpu.VMEM(blk.shape, blk.dtype),
            pltpu.VMEM(gin.shape, gin.dtype),
            pltpu.SemaphoreType.DMA((4,)),
        ],
        compiler_params=pltpu.CompilerParams(vmem_limit_bytes=62 * 1024 * 1024),
    )(blk, gin, *grads, *params, *firsts, *seconds)


def stored(items):
    qkv, mix, up, down, bias, gains = items
    return [qkv.transpose(1, 0, 2), mix, up, down.T, bias, gains]


def shards(inner, block_input, out_cotangent, lengths, *rest):
    params, firsts, seconds = (stored(rest[6 * i : 6 * i + 6]) for i in range(3))
    held = params
    if inner > 1:
        axes = (1, 1, 0, 0)
        held = [
            lax.all_gather(item.astype(BF), "dpl", axis=axis, tiled=True).astype(F32)
            for item, axis in zip(params[:4], axes, strict=True)
        ]
        count = params[4].shape[0]
        every = lax.all_gather(params[4], ("dpl", "mp"), axis=0, tiled=True)
        at = lax.axis_index("mp") * inner * count
        held += [lax.dynamic_slice_in_dim(every, at, inner * count, 0), params[5]]
    block_low, grad_input, *grads = run_block(
        lengths,
        block_input[0],
        out_cotangent[0],
        held[5],
        *held[:5],
        inner == 1,
    )
    if inner > 1:
        for i, axis in enumerate(axes):
            grads[i] = lax.psum_scatter(grads[i], "dpl", scatter_dimension=axis, tiled=True)
        grads[4], grads[5] = lax.psum((grads[4], grads[5]), "dpl")
        every = lax.all_gather(grads[4], ("mp", "dph"), axis=0, tiled=True)
        place = lax.axis_index(("dph", "dpl", "mp"))
        grads[4] = lax.dynamic_slice_in_dim(every, place * count, count, 0)
    scale = float(lax.axis_size("dph") * inner * LEN) ** (-0.5)
    *results, rms_stats, block_low, grad_input = run_adam(
        scale, block_low, grad_input, grads, params, firsts, seconds
    )
    outs = []
    for i in range(4):
        qkv, mix, up, down, bias, gains = results[6 * i : 6 * i + 6]
        outs += [qkv.transpose(1, 0, 2), mix, up, down.T, bias, gains]
    return (block_low[None], grad_input[None], *outs, rms_stats)


def solution(mesh):
    inner = mesh.shape["dp"] // GROUPS
    fine = Mesh(
        mesh.devices.reshape(GROUPS, inner, mesh.shape["mp"]),
        ("dph", "dpl", "mp"),
    )
    dp = ("dph", "dpl")
    weights = (
        P(dp, None, "mp"),
        P("mp", dp),
        P(dp, "mp"),
        P("mp", dp),
        P((*dp, "mp"), None),
        P(),
    )
    acts = P(dp, "mp", None)
    return jax.shard_map(
        functools.partial(shards, inner),
        mesh=fine,
        in_specs=(acts, acts, P(dp), *weights, *weights, *weights),
        out_specs=(acts, acts, *weights, *weights, *weights, *weights, P()),
        check_vma=False,
    )
```
